32 devices in a mesh: row: 2 (over x), col: 4 (over z), layer: 4 (over y, core).
Axes of the slice: x: 2, y: 2, z: 4, core: 2. Of those that a mesh axis runs over, the one named last changes fastest.
Arguments:
- blocks: float32 [16, 4, 3, 96, 96], P(('row', 'layer'), 'col'), may hold values from -2.4 to 2.4
- block_cols: int32 [16, 4, 3], replicated, may hold values from 0 to 3, as said below
- occupancy: int32 [16, 4, 3], replicated, may hold values from 0 to 1, as said below
Outputs:
- product: float32 [16, 4, 3, 96, 96], P(('row', 'layer'), 'col')
- trace: float32 [], replicated
The draws below stay inside these ranges and needn't reach their ends.
Inputs may be any that keep to these rules, and one draw needn't show every extreme that they name: `block_cols`: within one block row and column group the 3 block columns are distinct; for block row I the column group I // 4 holds I % 4 in slot 0. `occupancy`: slot 0 of block row I in column group I // 4 is always 1.
All inputs are finite; a program needn't handle non-finite values.
Results may differ from the reference program's by a relative error of at most 0.0003.
Values sent between devices are 32-bit elements; how exact they have to be, the bound alone decides.
No kernel may reach another device: no remote copies, remote signals or barrier semaphores. Data moves between devices by JAX's collectives and lax.ppermute only.
A program may use at most 64 MiB of HBM per device.

```python
import jax
import jax.numpy as jnp
from jax import lax

B = 96
RMAX = 3
NB = 16
GCOLS = 4
N_COL = 4


def draw_block_cols(key, part):
    key = jax.random.fold_in(key, 11)
    noise = jax.random.randint(key, (NB, N_COL, GCOLS), 0, 2 ** 20)
    column = jnp.arange(GCOLS, dtype=jnp.int32)[None, None, :]
    rows = jnp.arange(NB, dtype=jnp.int32)[:, None, None]
    group = jnp.arange(N_COL, dtype=jnp.int32)[None, :, None]
    diagonal = ((group == rows // GCOLS) & (column == rows % GCOLS)).astype(jnp.int32)
    score = noise * GCOLS + column + diagonal * 2 ** 28
    values, picked = lax.top_k(score, RMAX)
    return picked.astype(jnp.int32)


def draw_occupancy(key, part):
    key = jax.random.fold_in(key, 23)
    base = jax.random.randint(key, (NB, N_COL, RMAX), 0, 2)
    rows = jnp.arange(NB, dtype=jnp.int32)[:, None, None]
    group = jnp.arange(N_COL, dtype=jnp.int32)[None, :, None]
    slot = jnp.arange(RMAX, dtype=jnp.int32)[None, None, :]
    forced = ((group == rows // GCOLS) & (slot == 0)).astype(jnp.int32)
    return jnp.maximum(base, forced).astype(jnp.int32)


def shard_levels(own_key, shape, cuts, least, top_value):
    loudness, own = 1.0, jax.random.fold_in(own_key, 6)
    for axis_at, parts in cuts:
        steps = jnp.exp(jax.random.uniform(jax.random.fold_in(own, axis_at), (parts,), jnp.float32, least / len(cuts), top_value / len(cuts)))
        loudness = loudness * jnp.repeat(steps, shape[axis_at] // parts).reshape([-1 if axis == axis_at else 1 for axis in range(len(shape))])
    return loudness


def bell_draw(stream_key, extent, deviation, reach, split=(), held_as=jnp.bfloat16):
    level = shard_levels(stream_key, extent, split, -0.22, 0.18) if split else 1.0
    drawn = jax.random.normal(stream_key, extent, jnp.float32) * deviation * level
    return jnp.minimum(jnp.maximum(drawn, -reach), reach).astype(held_as)


def setup_inputs(seed: int = 0) -> dict:
    seeds = jax.random.split(jax.random.key(seed), 4)
    return {
        "blocks": bell_draw(seeds[0], (NB, N_COL, RMAX, B, B), 0.3, 2.4, ((0, 8), (1, 4)), jnp.float32),
        "block_cols": draw_block_cols(jax.random.fold_in(seeds[3], 71), 0),
        "occupancy": draw_occupancy(jax.random.fold_in(seeds[3], 71), 0),
    }


def reference(blocks, block_cols, occupancy):
    count = blocks.shape[0]
    groups = blocks.shape[1]
    width = count // groups
    occ_float = occupancy.astype(jnp.float32)
    group_ids = jnp.arange(groups, dtype=jnp.int32)

    def one_row(index):
        row_blocks = blocks[index]
        row_cols = block_cols[index]
        row_occ = occ_float[index]
        inner = (group_ids[:, None] * width + row_cols).astype(jnp.int32)
        gathered = blocks[inner]
        inner_cols = block_cols[inner]
        inner_occ = occ_float[inner]
        match = (inner_cols[:, :, :, :, None] == row_cols[None, None, :, None, :]).astype(jnp.float32)
        match = match * inner_occ[:, :, :, :, None] * row_occ[:, :, None, None, None]
        combined = jnp.einsum('gtcus,gtcubd->gtcsbd', match, gathered, precision=lax.Precision.HIGHEST)
        result = jnp.einsum('gtab,gtcsbd->csad', row_blocks, combined, precision=lax.Precision.HIGHEST)
        return result * row_occ[:, :, None, None]

    product = lax.map(one_row, jnp.arange(count, dtype=jnp.int32))
    rows = jnp.arange(count, dtype=jnp.int32)[:, None, None]
    global_cols = group_ids[None, :, None] * width + block_cols
    diagonal = (global_cols == rows).astype(jnp.float32) * occ_float
    traces = jnp.trace(product, axis1=3, axis2=4)
    return product, jnp.sum(diagonal * traces)
```

```python
import functools

import jax
import jax.numpy as jnp
from jax import lax
from jax.experimental import pallas as pl
from jax.experimental.pallas import tpu as pltpu
from jax.sharding import PartitionSpec as P

LANES = 128
AXES = ("row", "col", "layer")
LIMIT = pltpu.CompilerParams(vmem_limit_bytes=48 * 2 ** 20)
VMEM = pl.BlockSpec(memory_space=pltpu.VMEM)
SMEM = pl.BlockSpec(memory_space=pltpu.SMEM)


def tall_of(size):
    return size * size // LANES


def unpack(block, size):
    tall = block.shape[0]
    spare = LANES - size
    rest = size - tall
    pieces = [block[q * rest:(q + 1) * rest, size:] for q in range(size // spare)]
    pieces.append(jnp.zeros((rest, spare), block.dtype))
    return jnp.concatenate([block, jnp.concatenate(pieces, axis=1)], axis=0)


def parts_of(value):
    parts = []
    for _ in range(3):
        part = value.astype(jnp.bfloat16)
        parts.append(part)
        value = value - part.astype(jnp.float32)
    return parts


def found(cols_ref, occ_ref, row, group, target):
    index = jnp.int32(0)
    valid = jnp.int32(0)
    for u in range(cols_ref.shape[0]):
        hit = jnp.where((cols_ref[u, group, row] == target) & (occ_ref[u, group, row] == 1), 1, 0)
        index = index + hit * u
        valid = valid + hit
    return index, valid > 0


def place(sizes):
    n_row, n_col, n_layer = sizes
    per_group = n_row * n_layer // n_col
    pair = lax.axis_index("row") * n_layer + lax.axis_index("layer")
    return pair, lax.axis_index("col"), lax.div(pair, per_group), lax.rem(pair, per_group), per_group


def pack_kernel(sizes, cols_ref, occ_ref, x_ref, out_ref, *crossed_refs):
    rows, _, slots, size, _ = x_ref.shape
    tall = tall_of(size)
    spare = LANES - size
    rest = size - tall
    for i in range(rows):
        for t in range(slots):
            n = i * slots + t
            out_ref[n, :, :size] = x_ref[i, 0, t, :tall, :]
            for q in range(size // spare):
                out_ref[n, q * rest:(q + 1) * rest, size:] = x_ref[i, 0, t, tall:, q * spare:(q + 1) * spare]
    pair, here, group, number, per_group = place(sizes)
    for d, crossed_ref in enumerate(crossed_refs):
        shift = jnp.where(here < group, d, d + 1)
        column = lax.rem(number - shift + per_group, per_group) * rows
        for i in range(rows):
            for j in range(rows):
                index, valid = found(cols_ref, occ_ref, pair * rows + i, here, column + j)
                crossed_ref[i * rows + j] = jnp.where(valid, out_ref[i * slots + index], 0.0)


def trace_kernel(sizes, rows, size, cols_ref, occ_ref, packed_ref, *refs):
    crossed_refs, total_ref, sum_ref = refs[:-2], refs[-2], refs[-1]
    slots = packed_ref.shape[0] // rows
    pair, here, group, number, per_group = place(sizes)
    total = jnp.zeros((size, size), jnp.float32)

    def own(i, column):
        index, valid = found(cols_ref, occ_ref, pair * rows + i, here, column)
        return jnp.where(valid, unpack(packed_ref[i * slots + index], size)[:, :size], 0.0)

    def turned(block):
        return unpack(block, size)[:, :size].T

    for d, crossed_ref in enumerate(crossed_refs):
        shift = jnp.where(group < here, d, d + 1)
        column = lax.rem(number + shift, per_group) * rows
        once = (group == here) & (d + 1 == per_group // 2)
        weight = jnp.where(once, 1.0, 2.0)
        for i in range(rows):
            for j in range(rows):
                total = total + weight * own(i, column + j) * turned(crossed_ref[j * rows + i])
    sum_ref[...] = total

    @pl.when(group == here)
    def _():
        more = jnp.zeros((size, size), jnp.float32)
        for i in range(rows):
            for j in range(rows):
                more = more + own(i, number * rows + j) * own(j, number * rows + i).T
        sum_ref[...] += more

    total_ref[...] = jnp.sum(sum_ref[...], keepdims=True)


def stack_kernel(_, *refs):
    out_ref = refs[-1]
    for n, ref in enumerate(refs[:-1]):
        out_ref[n * ref.shape[0]:(n + 1) * ref.shape[0]] = ref[...]


def product_kernel(sizes, cols_ref, occ_ref, *refs):
    n_row, n_col, n_layer = sizes
    strip_refs, (mine_ref, other_ref), out_ref = refs[:n_col], refs[n_col:n_col + 2], refs[n_col + 2]
    a_refs, w_refs = refs[n_col + 3:n_col + 6], refs[n_col + 6:]
    rows, _, slots, size, _ = out_ref.shape
    pair, here, _, _, per_group = place(sizes)
    width = per_group * rows
    inner = n_col * slots
    chips = n_layer // 2
    my_row, my_layer = lax.axis_index("row"), lax.axis_index("layer")
    my_chip, my_core = lax.div(my_layer, 2), lax.rem(my_layer, 2)

    for w_ref in w_refs:
        for j in range(inner):
            w_ref[j * LANES + size:(j + 1) * LANES, :] = jnp.zeros((LANES - size, slots * LANES), jnp.bfloat16)
    for i in range(rows):
        row = pair * rows + i
        targets = [cols_ref[s, here, row] for s in range(slots)]
        for k in range(n_col):
            group = lax.rem(here + k, n_col)
            for t in range(slots):
                j = k * slots + t
                for a_ref, part in zip(a_refs, parts_of(unpack(strip_refs[k][i * slots + t], size))):
                    a_ref[:, j * LANES:(j + 1) * LANES] = part
                stored = occ_ref[t, group, row] == 1
                contracted = group * width + cols_ref[t, group, row]
                source = lax.div(contracted, rows)
                source_row, source_layer = lax.div(source, n_layer), lax.rem(source, n_layer)
                chip = lax.rem(lax.div(source_layer, 2) - my_chip + chips, chips)
                base = (lax.rem(source_row - my_row + n_row, n_row) * chips + chip) * (rows * slots)
                base = base + lax.rem(contracted, rows) * slots
                same_core = lax.rem(source_layer, 2) == my_core
                for s in range(slots):
                    index, valid = found(cols_ref, occ_ref, contracted, here, targets[s])
                    valid = valid & stored & (occ_ref[s, here, row] == 1)
                    block = jnp.where(same_core, mine_ref[base + index], other_ref[base + index])
                    block = jnp.where(valid, unpack(block, size), 0.0)
                    for w_ref, part in zip(w_refs, parts_of(block)):
                        w_ref[j * LANES:j * LANES + size, s * LANES:(s + 1) * LANES] = part

        def dot(a, w):
            return jnp.dot(a_refs[a][...], w_refs[w][...], preferred_element_type=jnp.float32)

        result = dot(0, 0) + ((dot(0, 1) + dot(1, 0)) + (dot(1, 1) + (dot(0, 2) + dot(2, 0))))
        for s in range(slots):
            out_ref[i, 0, s] = result[:, s * LANES:s * LANES + size]


def summed_over(value, axis):
    size = lax.axis_size(axis)
    step = 1
    while step < size:
        value = value + lax.ppermute(value, axis, [(i, i ^ step) for i in range(size)])
        step *= 2
    return value


def crossing(sizes, d):
    n_row, n_col, n_layer = sizes
    per_group = n_row * n_layer // n_col

    def device(group, number, column):
        pair = group * per_group + number
        return (pair // n_layer * n_col + column) * n_layer + pair % n_layer

    pairs = []
    for group in range(n_col):
        for number in range(per_group):
            for column in range(n_col):
                shift = d if group < column else d + 1
                pairs.append((device(column, (number + shift) % per_group, group), device(group, number, column)))
    return pairs


def body(blocks, block_cols, occupancy):
    rows, _, slots, size, _ = blocks.shape
    sizes = tuple(lax.axis_size(axis) for axis in AXES)
    n_row, n_col, n_layer = sizes
    per_group = n_row * n_layer // n_col
    tall = tall_of(size)
    inner = n_col * slots
    cols = jnp.transpose(block_cols, (2, 1, 0))
    occ = jnp.transpose(occupancy, (2, 1, 0))

    packed, *crossed = pl.pallas_call(
        functools.partial(pack_kernel, sizes),
        out_shape=[jax.ShapeDtypeStruct((rows * slots, tall, LANES), jnp.float32)]
        + [jax.ShapeDtypeStruct((rows * rows, tall, LANES), jnp.float32)] * (per_group // 2),
        in_specs=[SMEM, SMEM, VMEM],
        out_specs=[VMEM] * (1 + per_group // 2),
        compiler_params=LIMIT,
        name="pack",
    )(cols, occ, blocks)

    crossed = [lax.ppermute(value, AXES, crossing(sizes, d)) for d, value in enumerate(crossed)]
    strip = [packed]
    for k in range(1, n_col):
        strip.append(lax.ppermute(packed, "col", [((c + k) % n_col, c) for c in range(n_col)]))
    mine = [packed]
    for r in range(n_row):
        for y in range(0, n_layer, 2):
            if r or y:
                route = [
                    ((a + r) % n_row * n_layer + (b + y) % n_layer, a * n_layer + b)
                    for a in range(n_row) for b in range(n_layer)
                ]
                mine.append(lax.ppermute(packed, ("row", "layer"), route))

    trace = pl.pallas_call(
        functools.partial(trace_kernel, sizes, rows, size),
        out_shape=jax.ShapeDtypeStruct((1, 1), jnp.float32),
        in_specs=[SMEM, SMEM] + [VMEM] * (1 + len(crossed)),
        out_specs=VMEM,
        scratch_shapes=[pltpu.VMEM((size, size), jnp.float32)],
        compiler_params=LIMIT,
        name="trace_terms",
    )(cols, occ, packed, *crossed)
    trace = summed_over(trace, "layer")
    stacked = pl.pallas_call(
        stack_kernel,
        out_shape=jax.ShapeDtypeStruct((len(mine) * rows * slots, tall, LANES), jnp.float32),
        in_specs=[VMEM] * (1 + len(mine)),
        out_specs=VMEM,
        compiler_params=LIMIT,
        name="stack",
    )(trace, *mine)
    other = lax.ppermute(stacked, "layer", [(i, i ^ 1) for i in range(n_layer)])
    trace = summed_over(summed_over(trace, "row"), "col")

    product = pl.pallas_call(
        functools.partial(product_kernel, sizes),
        out_shape=jax.ShapeDtypeStruct(blocks.shape, jnp.float32),
        in_specs=[SMEM, SMEM] + [VMEM] * (n_col + 2),
        out_specs=VMEM,
        scratch_shapes=[pltpu.VMEM((size, inner * LANES), jnp.bfloat16)] * 3
        + [pltpu.VMEM((inner * LANES, slots * LANES), jnp.bfloat16)] * 3,
        compiler_params=LIMIT,
        name="multiply",
    )(cols, occ, *strip, stacked, other)
    return product, trace.reshape(())


def solution(mesh):
    in_specs = (P(("row", "layer"), "col", None, None, None), P(), P())
    out_specs = (P(("row", "layer"), "col", None, None, None), P())
    return jax.shard_map(body, mesh=mesh, in_specs=in_specs, out_specs=out_specs, check_vma=False)
```

```python
import functools

import jax
import jax.numpy as jnp
from jax import lax
from jax.experimental import pallas as pl
from jax.experimental.pallas import tpu as pltpu
from jax.sharding import PartitionSpec as P

LANES = 128
AXES = ("row", "col", "layer")
LIMIT = pltpu.CompilerParams(vmem_limit_bytes=48 * 2 ** 20)
VMEM = pl.BlockSpec(memory_space=pltpu.VMEM)
SMEM = pl.BlockSpec(memory_space=pltpu.SMEM)


def tall_of(size):
    return size * size // LANES


def unpack(block, size):
    tall = block.shape[0]
    spare = LANES - size
    rest = size - tall
    pieces = [block[q * rest:(q + 1) * rest, size:] for q in range(size // spare)]
    pieces.append(jnp.zeros((rest, spare), block.dtype))
    return jnp.concatenate([block, jnp.concatenate(pieces, axis=1)], axis=0)


def parts_of(value):
    parts = []
    for _ in range(3):
        part = value.astype(jnp.bfloat16)
        parts.append(part)
        value = value - part.astype(jnp.float32)
    return parts


def found(cols_ref, occ_ref, row, group, target):
    index = jnp.int32(0)
    valid = jnp.int32(0)
    for u in range(cols_ref.shape[0]):
        hit = jnp.where((cols_ref[u, group, row] == target) & (occ_ref[u, group, row] == 1), 1, 0)
        index = index + hit * u
        valid = valid + hit
    return index, valid > 0


def place(sizes):
    n_row, n_col, n_layer = sizes
    per_group = n_row * n_layer // n_col
    pair = lax.axis_index("row") * n_layer + lax.axis_index("layer")
    return pair, lax.axis_index("col"), lax.div(pair, per_group), lax.rem(pair, per_group), per_group


def pack_kernel(x_ref, out_ref):
    rows, _, slots, size, _ = x_ref.shape
    tall = tall_of(size)
    spare = LANES - size
    rest = size - tall
    for i in range(rows):
        for t in range(slots):
            n = i * slots + t
            out_ref[n, :, :size] = x_ref[i, 0, t, :tall, :]
            for q in range(size // spare):
                out_ref[n, q * rest:(q + 1) * rest, size:] = x_ref[i, 0, t, tall:, q * spare:(q + 1) * spare]


def cross_kernel(sizes, rows, cols_ref, occ_ref, packed_ref, *crossed_refs):
    slots = packed_ref.shape[0] // rows
    pair, here, group, number, per_group = place(sizes)
    for d, crossed_ref in enumerate(crossed_refs):
        shift = jnp.where(here < group, d, d + 1)
        column = lax.rem(number - shift + per_group, per_group) * rows
        for i in range(rows):
            for j in range(rows):
                index, valid = found(cols_ref, occ_ref, pair * rows + i, here, column + j)
                crossed_ref[i * rows + j] = jnp.where(valid, packed_ref[i * slots + index], 0.0)


def strip_block(sizes, rows, slots, mine_ref, other_ref, contracted):
    n_row, _, n_layer = sizes
    chips = n_layer // 2
    my_row, my_layer = lax.axis_index("row"), lax.axis_index("layer")
    source = lax.div(contracted, rows)
    source_row, source_layer = lax.div(source, n_layer), lax.rem(source, n_layer)
    chip = lax.rem(lax.div(source_layer, 2) - lax.div(my_layer, 2) + chips, chips)
    base = (lax.rem(source_row - my_row + n_row, n_row) * chips + chip) * (rows * slots)
    base = base + lax.rem(contracted, rows) * slots
    same_core = lax.rem(source_layer, 2) == lax.rem(my_layer, 2)
    return lambda index: jnp.where(same_core, mine_ref[base + index], other_ref[base + index])


def trace_kernel(sizes, rows, size, early, late, cols_ref, occ_ref, *refs):
    n_col = sizes[1]
    strip_refs, (mine_ref, other_ref) = refs[:len(early)], refs[len(early):len(early) + 2]
    crossed_refs, total_ref, sum_ref = refs[len(early) + 2:-2], refs[-2], refs[-1]
    packed_ref = strip_refs[0]
    slots = packed_ref.shape[0] // rows
    pair, here, group, number, per_group = place(sizes)
    width = per_group * rows
    sum_ref[...] = jnp.zeros((size, size), jnp.float32)

    def straight(block):
        return unpack(block, size)[:, :size]

    apart = lax.rem(here - group + n_col, n_col)
    is_late = functools.reduce(jnp.logical_or, [apart == k for k in late], jnp.bool_(False))

    @pl.when(is_late)
    def _():
        total = jnp.zeros((size, size), jnp.float32)
        for d, crossed_ref in enumerate(crossed_refs):
            shift = jnp.where(group < here, d, d + 1)
            column = lax.rem(number + shift, per_group) * rows
            for i in range(rows):
                for j in range(rows):
                    index, valid = found(cols_ref, occ_ref, pair * rows + i, here, column + j)
                    term = straight(packed_ref[i * slots + index]) * straight(crossed_ref[j * rows + i]).T
                    total = total + jnp.where(valid, 2.0 * term, 0.0)
        sum_ref[...] = total

    @pl.when(group == here)
    def _():
        total = jnp.zeros((size, size), jnp.float32)
        for i in range(rows):
            row = pair * rows + i
            for k, strip_ref in zip(early, strip_refs):
                contracted_group = lax.rem(here + k, n_col)
                for t in range(slots):
                    contracted = contracted_group * width + cols_ref[t, contracted_group, row]
                    index, valid = found(cols_ref, occ_ref, contracted, here, number * rows + i)
                    valid = valid & (occ_ref[t, contracted_group, row] == 1)
                    block = strip_block(sizes, rows, slots, mine_ref, other_ref, contracted)(index)
                    term = straight(strip_ref[i * slots + t]) * straight(block).T
                    total = total + jnp.where(valid, term, 0.0)
        sum_ref[...] = total

    total_ref[...] = jnp.sum(sum_ref[...], keepdims=True)


def stack_kernel(ahead, *refs):
    out_ref = refs[-1]
    for n, ref in enumerate(refs[ahead:-1]):
        out_ref[n * ref.shape[0]:(n + 1) * ref.shape[0]] = ref[...]


def product_kernel(sizes, shifts, added, cols_ref, occ_ref, *refs):
    n_row, n_col, n_layer = sizes
    count = len(shifts)
    strip_refs, (mine_ref, other_ref), refs = refs[:count], refs[count:count + 2], refs[count + 2:]
    before_ref, refs = (refs[0], refs[1:]) if added else (None, refs)
    out_ref, a_refs, w_refs = refs[0], refs[1:4], refs[4:]
    rows, _, slots, size, _ = out_ref.shape
    pair, here, _, _, per_group = place(sizes)
    width = per_group * rows

    for w_ref in w_refs:
        for j in range(count * slots):
            w_ref[j * LANES + size:(j + 1) * LANES, :] = jnp.zeros((LANES - size, slots * LANES), jnp.bfloat16)
    for i in range(rows):
        row = pair * rows + i
        targets = [cols_ref[s, here, row] for s in range(slots)]
        for k, shift in enumerate(shifts):
            group = lax.rem(here + shift, n_col)
            for t in range(slots):
                j = k * slots + t
                for a_ref, part in zip(a_refs, parts_of(unpack(strip_refs[k][i * slots + t], size))):
                    a_ref[:, j * LANES:(j + 1) * LANES] = part
                stored = occ_ref[t, group, row] == 1
                contracted = group * width + cols_ref[t, group, row]
                read = strip_block(sizes, rows, slots, mine_ref, other_ref, contracted)
                for s in range(slots):
                    index, valid = found(cols_ref, occ_ref, contracted, here, targets[s])
                    valid = valid & stored & (occ_ref[s, here, row] == 1)
                    block = jnp.where(valid, unpack(read(index), size), 0.0)
                    for w_ref, part in zip(w_refs, parts_of(block)):
                        w_ref[j * LANES:j * LANES + size, s * LANES:(s + 1) * LANES] = part

        def dot(a, w):
            return jnp.dot(a_refs[a][...], w_refs[w][...], preferred_element_type=jnp.float32)

        result = dot(0, 0) + ((dot(0, 1) + dot(1, 0)) + (dot(1, 1) + (dot(0, 2) + dot(2, 0))))
        for s in range(slots):
            block = result[:, s * LANES:s * LANES + size]
            out_ref[i, 0, s] = before_ref[i, 0, s] + block if added else block


def summed_over_all(value, sizes):
    n_row, n_col, n_layer = sizes
    total = n_row * n_col * n_layer
    bits = [1 << b for b in range((total - 1).bit_length())]
    in_layer = [b for b in bits if b < n_layer]
    in_col = [b for b in bits if n_layer <= b < n_layer * n_col]
    in_row = [b for b in bits if b >= n_layer * n_col]
    in_plane = in_layer[1:] + in_row
    stages = [in_layer[:1]]
    for some in (in_plane, in_col):
        stages += [some[n:n + 2] for n in range(0, len(some), 2)]

    def moved(mask):
        return lax.ppermute(value, AXES, [(n, n ^ mask) for n in range(total)])

    for stage in stages:
        if len(stage) == 1:
            value = value + moved(stage[0])
        elif stage:
            one, two = stage
            value = (value + moved(one)) + (moved(two) + moved(one ^ two))
    return value


def crossing(sizes, late, d):
    n_row, n_col, n_layer = sizes
    per_group = n_row * n_layer // n_col

    def device(group, number, column):
        pair = group * per_group + number
        return (pair // n_layer * n_col + column) * n_layer + pair % n_layer

    pairs = []
    for group in range(n_col):
        for number in range(per_group):
            for column in range(n_col):
                if (column - group) % n_col in late:
                    shift = d if group < column else d + 1
                    pairs.append((device(column, (number + shift) % per_group, group), device(group, number, column)))
    return pairs


def body(blocks, block_cols, occupancy):
    rows, _, slots, size, _ = blocks.shape
    sizes = tuple(lax.axis_size(axis) for axis in AXES)
    n_row, n_col, n_layer = sizes
    per_group = n_row * n_layer // n_col
    tall = tall_of(size)
    cols = jnp.transpose(block_cols, (2, 1, 0))
    occ = jnp.transpose(occupancy, (2, 1, 0))
    late = [k for k in range(n_col) if n_col < 4 * k < 3 * n_col]
    early = [k for k in range(n_col) if k not in late]

    def shape(count):
        return jax.ShapeDtypeStruct((count, tall, LANES), jnp.float32)

    packed = pl.pallas_call(
        pack_kernel,
        out_shape=shape(rows * slots),
        in_specs=[VMEM],
        out_specs=VMEM,
        compiler_params=LIMIT,
        name="pack",
    )(blocks)

    def shifted(k):
        return lax.ppermute(packed, "col", [((c + k) % n_col, c) for c in range(n_col)]) if k else packed

    strip = {k: shifted(k) for k in early}
    mine = [packed]
    for r in range(n_row):
        for y in range(0, n_layer, 2):
            if r or y:
                route = [
                    ((a + r) % n_row * n_layer + (b + y) % n_layer, a * n_layer + b)
                    for a in range(n_row) for b in range(n_layer)
                ]
                mine.append(lax.ppermute(packed, ("row", "layer"), route))
    crossed = pl.pallas_call(
        functools.partial(cross_kernel, sizes, rows),
        out_shape=[shape(rows * rows)] * (per_group // 2),
        in_specs=[SMEM, SMEM, VMEM],
        out_specs=[VMEM] * (per_group // 2),
        compiler_params=LIMIT,
        name="cross",
    )(cols, occ, packed)
    crossed = [lax.ppermute(value, AXES, crossing(sizes, late, d)) for d, value in enumerate(crossed)]

    ahead = [strip[k] for k in early if k]
    stacked = pl.pallas_call(
        functools.partial(stack_kernel, len(ahead)),
        out_shape=shape(len(mine) * rows * slots),
        in_specs=[pl.BlockSpec(memory_space=pl.ANY)] * len(ahead) + [VMEM] * len(mine),
        out_specs=VMEM,
        compiler_params=LIMIT,
        name="stack",
    )(*ahead, *mine)
    other = lax.ppermute(stacked, "layer", [(i, i ^ 1) for i in range(n_layer)])
    for k in late:
        strip[k] = shifted(k)

    trace = pl.pallas_call(
        functools.partial(trace_kernel, sizes, rows, size, early, late),
        out_shape=jax.ShapeDtypeStruct((1, 1), jnp.float32),
        in_specs=[SMEM, SMEM] + [VMEM] * (len(early) + 2 + len(crossed)),
        out_specs=VMEM,
        scratch_shapes=[pltpu.VMEM((size, size), jnp.float32)],
        compiler_params=LIMIT,
        name="trace_terms",
    )(cols, occ, *[strip[k] for k in early], stacked, other, *crossed)
    trace = summed_over_all(trace, sizes)

    product = None
    for shifts in (early, late):
        inner = len(shifts) * slots * LANES
        product = pl.pallas_call(
            functools.partial(product_kernel, sizes, shifts, product is not None),
            out_shape=jax.ShapeDtypeStruct(blocks.shape, jnp.float32),
            in_specs=[SMEM, SMEM] + [VMEM] * (len(shifts) + 2 + (product is not None)),
            out_specs=VMEM,
            scratch_shapes=[pltpu.VMEM((size, inner), jnp.bfloat16)] * 3
            + [pltpu.VMEM((inner, slots * LANES), jnp.bfloat16)] * 3,
            compiler_params=LIMIT,
            name="multiply",
        )(cols, occ, *[strip[k] for k in shifts], stacked, other, *([] if product is None else [product]))
    return product, trace.reshape(())


def solution(mesh):
    in_specs = (P(("row", "layer"), "col", None, None, None), P(), P())
    out_specs = (P(("row", "layer"), "col", None, None, None), P())
    return jax.shard_map(body, mesh=mesh, in_specs=in_specs, out_specs=out_specs, check_vma=False)
```

```python
import functools

import jax
import jax.numpy as jnp
from jax import lax
from jax.experimental import pallas as pl
from jax.experimental.pallas import tpu as pltpu
from jax.sharding import PartitionSpec as P

LANES = 128
AXES = ("row", "col", "layer")
LIMIT = pltpu.CompilerParams(vmem_limit_bytes=48 * 2 ** 20)
VMEM = pl.BlockSpec(memory_space=pltpu.VMEM)
SMEM = pl.BlockSpec(memory_space=pltpu.SMEM)


def tall_of(size):
    return size * size // LANES


def unpack(block, size):
    tall = block.shape[0]
    spare = LANES - size
    rest = size - tall
    pieces = [block[q * rest:(q + 1) * rest, size:] for q in range(size // spare)]
    pieces.append(jnp.zeros((rest, spare), block.dtype))
    return jnp.concatenate([block, jnp.concatenate(pieces, axis=1)], axis=0)


def parts_of(value):
    parts = []
    for _ in range(3):
        part = value.astype(jnp.bfloat16)
        parts.append(part)
        value = value - part.astype(jnp.float32)
    return parts


def found(cols_ref, occ_ref, row, group, target):
    index = jnp.int32(0)
    valid = jnp.int32(0)
    for u in range(cols_ref.shape[0]):
        hit = jnp.where((cols_ref[u, group, row] == target) & (occ_ref[u, group, row] == 1), 1, 0)
        index = index + hit * u
        valid = valid + hit
    return index, valid > 0


def place(sizes):
    n_row, n_col, n_layer = sizes
    per_group = n_row * n_layer // n_col
    pair = lax.axis_index("row") * n_layer + lax.axis_index("layer")
    return pair, lax.axis_index("col"), lax.div(pair, per_group), lax.rem(pair, per_group), per_group


def pack_kernel(x_ref, out_ref, *more_refs):
    rows, _, slots, size, _ = x_ref.shape
    tall = tall_of(size)
    spare = LANES - size
    rest = size - tall
    for i in range(rows):
        for t in range(slots):
            n = i * slots + t
            out_ref[n, :, :size] = x_ref[i, 0, t, :tall, :]
            for q in range(size // spare):
                out_ref[n, q * rest:(q + 1) * rest, size:] = x_ref[i, 0, t, tall:, q * spare:(q + 1) * spare]
    for more_ref in more_refs:
        for n in range(more_ref.shape[0]):
            more_ref[n] = out_ref[...]


def strip_block(n_col, rows, slots, strip_ref, contracted):
    return lambda index: strip_ref[lax.div(contracted, rows), lax.rem(contracted, rows) * slots + index]


def trace_kernel(sizes, rows, size, cols_ref, occ_ref, row_ref, column_ref, total_ref, sum_ref):
    n_col = sizes[1]
    slots = row_ref.shape[1] // rows
    pair, here, group, number, per_group = place(sizes)
    width = per_group * rows
    total_ref[...] = jnp.zeros(total_ref.shape, jnp.float32)

    def straight(block):
        return unpack(block, size)[:, :size]

    @pl.when(group == here)
    def _():
        total = jnp.zeros((size, size), jnp.float32)
        for i in range(rows):
            row = pair * rows + i
            for k in range(n_col):
                for t in range(slots):
                    contracted = k * width + cols_ref[t, k, row]
                    index, valid = found(cols_ref, occ_ref, contracted, here, number * rows + i)
                    valid = valid & (occ_ref[t, k, row] == 1)
                    block = strip_block(n_col, rows, slots, column_ref, contracted)(index)
                    term = straight(row_ref[k, i * slots + t]) * straight(block).T
                    total = total + jnp.where(valid, term, 0.0)
        total_ref[...] = jnp.full(total_ref.shape, jnp.sum(total), jnp.float32)


def product_kernel(sizes, cols_ref, occ_ref, row_ref, column_ref, out_ref, *refs):
    n_row, n_col, n_layer = sizes
    a_refs, w_refs = refs[:3], refs[3:]
    rows, _, slots, size, _ = out_ref.shape
    pair, here, _, _, per_group = place(sizes)
    width = per_group * rows

    for w_ref in w_refs:
        for j in range(n_col * slots):
            w_ref[j * LANES + size:(j + 1) * LANES, :] = jnp.zeros((LANES - size, slots * LANES), jnp.bfloat16)
    for i in range(rows):
        row = pair * rows + i
        targets = [cols_ref[s, here, row] for s in range(slots)]
        for k in range(n_col):
            for t in range(slots):
                j = k * slots + t
                for a_ref, part in zip(a_refs, parts_of(unpack(row_ref[k, i * slots + t], size))):
                    a_ref[:, j * LANES:(j + 1) * LANES] = part
                stored = occ_ref[t, k, row] == 1
                contracted = k * width + cols_ref[t, k, row]
                read = strip_block(n_col, rows, slots, column_ref, contracted)
                for s in range(slots):
                    index, valid = found(cols_ref, occ_ref, contracted, here, targets[s])
                    valid = valid & stored & (occ_ref[s, here, row] == 1)
                    block = jnp.where(valid, unpack(read(index), size), 0.0)
                    for w_ref, part in zip(w_refs, parts_of(block)):
                        w_ref[j * LANES:j * LANES + size, s * LANES:(s + 1) * LANES] = part

        def dot(a, w):
            return jnp.dot(a_refs[a][...], w_refs[w][...], preferred_element_type=jnp.float32)

        result = dot(0, 0) + ((dot(0, 1) + dot(1, 0)) + (dot(1, 1) + (dot(0, 2) + dot(2, 0))))
        for s in range(slots):
            out_ref[i, 0, s] = result[:, s * LANES:s * LANES + size]


def body(blocks, block_cols, occupancy):
    rows, _, slots, size, _ = blocks.shape
    sizes = tuple(lax.axis_size(axis) for axis in AXES)
    n_row, n_col, n_layer = sizes
    n_pair = n_row * n_layer
    tall = tall_of(size)
    cols = jnp.transpose(block_cols, (2, 1, 0))
    occ = jnp.transpose(occupancy, (2, 1, 0))
    share = (rows * slots, tall, LANES)

    _, for_col, for_plane = pl.pallas_call(
        pack_kernel,
        out_shape=[jax.ShapeDtypeStruct(s, jnp.float32) for s in (share, (n_col,) + share, (n_pair,) + share)],
        in_specs=[VMEM],
        out_specs=[VMEM] * 3,
        compiler_params=LIMIT,
        name="pack",
    )(blocks)
    row_strip = lax.all_to_all(for_col, "col", 0, 0, tiled=True)
    column_strip = lax.all_to_all(for_plane, ("row", "layer"), 0, 0, tiled=True)

    trace = pl.pallas_call(
        functools.partial(trace_kernel, sizes, rows, size),
        out_shape=jax.ShapeDtypeStruct((n_col * n_pair, 1, LANES), jnp.float32),
        in_specs=[SMEM, SMEM, VMEM, VMEM],
        out_specs=VMEM,
        scratch_shapes=[pltpu.VMEM((size, size), jnp.float32)],
        compiler_params=LIMIT,
        name="trace_terms",
    )(cols, occ, row_strip, column_strip)
    trace = lax.all_to_all(trace, AXES, 0, 0, tiled=True)
    inner = n_col * slots * LANES
    product = pl.pallas_call(
        functools.partial(product_kernel, sizes),
        out_shape=jax.ShapeDtypeStruct(blocks.shape, jnp.float32),
        in_specs=[SMEM, SMEM, VMEM, VMEM],
        out_specs=VMEM,
        scratch_shapes=[pltpu.VMEM((size, inner), jnp.bfloat16)] * 3
        + [pltpu.VMEM((inner, slots * LANES), jnp.bfloat16)] * 3,
        compiler_params=LIMIT,
        name="multiply",
    )(cols, occ, row_strip, column_strip)
    return product, jnp.sum(trace[:, 0, 0])


def solution(mesh):
    in_specs = (P(("row", "layer"), "col", None, None, None), P(), P())
    out_specs = (P(("row", "layer"), "col", None, None, None), P())
    return jax.shard_map(body, mesh=mesh, in_specs=in_specs, out_specs=out_specs, check_vma=False)
```

```python
import functools

import jax
import jax.numpy as jnp
from jax import lax
from jax.experimental import pallas as pl
from jax.experimental.pallas import tpu as pltpu
from jax.sharding import PartitionSpec as P

LANES = 128
AXES = ("row", "col", "layer")
LIMIT = pltpu.CompilerParams(vmem_limit_bytes=48 * 2 ** 20)
VMEM = pl.BlockSpec(memory_space=pltpu.VMEM)
SMEM = pl.BlockSpec(memory_space=pltpu.SMEM)


def tall_of(size):
    return size * size // LANES


def unpack(block, size):
    tall = block.shape[0]
    spare = LANES - size
    rest = size - tall
    pieces = [block[q * rest:(q + 1) * rest, size:] for q in range(size // spare)]
    pieces.append(jnp.zeros((rest, spare), block.dtype))
    return jnp.concatenate([block, jnp.concatenate(pieces, axis=1)], axis=0)


def parts_of(value):
    parts = []
    for _ in range(3):
        part = value.astype(jnp.bfloat16)
        parts.append(part)
        value = value - part.astype(jnp.float32)
    return parts


def found(cols_ref, occ_ref, row, group, target):
    index = jnp.int32(0)
    valid = jnp.int32(0)
    for u in range(cols_ref.shape[0]):
        hit = jnp.where((cols_ref[u, group, row] == target) & (occ_ref[u, group, row] == 1), 1, 0)
        index = index + hit * u
        valid = valid + hit
    return index, valid > 0


def place(sizes):
    n_row, n_col, n_layer = sizes
    per_group = n_row * n_layer // n_col
    pair = lax.axis_index("row") * n_layer + lax.axis_index("layer")
    return pair, lax.axis_index("col"), lax.div(pair, per_group), lax.rem(pair, per_group), per_group


def pack_kernel(x_ref, out_ref):
    rows, _, slots, size, _ = x_ref.shape
    tall = tall_of(size)
    spare = LANES - size
    rest = size - tall
    for i in range(rows):
        for t in range(slots):
            n = i * slots + t
            out_ref[n, :, :size] = x_ref[i, 0, t, :tall, :]
            for q in range(size // spare):
                out_ref[n, q * rest:(q + 1) * rest, size:] = x_ref[i, 0, t, tall:, q * spare:(q + 1) * spare]


def cross_kernel(sizes, rows, cols_ref, occ_ref, packed_ref, *crossed_refs):
    slots = packed_ref.shape[0] // rows
    pair, here, group, number, per_group = place(sizes)
    for d, crossed_ref in enumerate(crossed_refs):
        shift = jnp.where(here < group, d, d + 1)
        column = lax.rem(number - shift + per_group, per_group) * rows
        for i in range(rows):
            for j in range(rows):
                index, valid = found(cols_ref, occ_ref, pair * rows + i, here, column + j)
                crossed_ref[i * rows + j] = jnp.where(valid, packed_ref[i * slots + index], 0.0)


def strip_block(sizes, rows, slots, mine_ref, other_ref, contracted):
    n_row, _, n_layer = sizes
    chips = n_layer // 2
    my_row, my_layer = lax.axis_index("row"), lax.axis_index("layer")
    source = lax.div(contracted, rows)
    source_row, source_layer = lax.div(source, n_layer), lax.rem(source, n_layer)
    chip = lax.rem(lax.div(source_layer, 2) - lax.div(my_layer, 2) + chips, chips)
    base = (lax.rem(source_row - my_row + n_row, n_row) * chips + chip) * (rows * slots)
    base = base + lax.rem(contracted, rows) * slots
    same_core = lax.rem(source_layer, 2) == lax.rem(my_layer, 2)
    return lambda index: jnp.where(same_core, mine_ref[base + index], other_ref[base + index])


def trace_kernel(sizes, rows, size, early, late, cols_ref, occ_ref, *refs):
    n_col = sizes[1]
    strip_refs, (mine_ref, other_ref) = refs[:len(early)], refs[len(early):len(early) + 2]
    crossed_refs, total_ref, sum_ref = refs[len(early) + 2:-2], refs[-2], refs[-1]
    packed_ref = strip_refs[0]
    slots = packed_ref.shape[0] // rows
    pair, here, group, number, per_group = place(sizes)
    width = per_group * rows
    sum_ref[...] = jnp.zeros((size, size), jnp.float32)

    def straight(block):
        return unpack(block, size)[:, :size]

    apart = lax.rem(here - group + n_col, n_col)
    is_late = functools.reduce(jnp.logical_or, [apart == k for k in late], jnp.bool_(False))

    @pl.when(is_late)
    def _():
        total = jnp.zeros((size, size), jnp.float32)
        for d, crossed_ref in enumerate(crossed_refs):
            shift = jnp.where(group < here, d, d + 1)
            column = lax.rem(number + shift, per_group) * rows
            for i in range(rows):
                for j in range(rows):
                    index, valid = found(cols_ref, occ_ref, pair * rows + i, here, column + j)
                    term = straight(packed_ref[i * slots + index]) * straight(crossed_ref[j * rows + i]).T
                    total = total + jnp.where(valid, 2.0 * term, 0.0)
        sum_ref[...] = total

    @pl.when(group == here)
    def _():
        total = jnp.zeros((size, size), jnp.float32)
        for i in range(rows):
            row = pair * rows + i
            for k, strip_ref in zip(early, strip_refs):
                contracted_group = lax.rem(here + k, n_col)
                for t in range(slots):
                    contracted = contracted_group * width + cols_ref[t, contracted_group, row]
                    index, valid = found(cols_ref, occ_ref, contracted, here, number * rows + i)
                    valid = valid & (occ_ref[t, contracted_group, row] == 1)
                    block = strip_block(sizes, rows, slots, mine_ref, other_ref, contracted)(index)
                    term = straight(strip_ref[i * slots + t]) * straight(block).T
                    total = total + jnp.where(valid, term, 0.0)
        sum_ref[...] = total

    total_ref[...] = jnp.full(total_ref.shape, jnp.sum(sum_ref[...]), jnp.float32)


def stack_kernel(ahead, *refs):
    out_ref = refs[-1]
    for n, ref in enumerate(refs[ahead:-1]):
        out_ref[n * ref.shape[0]:(n + 1) * ref.shape[0]] = ref[...]


def product_kernel(sizes, shifts, added, cols_ref, occ_ref, *refs):
    n_row, n_col, n_layer = sizes
    count = len(shifts)
    strip_refs, (mine_ref, other_ref), refs = refs[:count], refs[count:count + 2], refs[count + 2:]
    before_ref, refs = (refs[0], refs[1:]) if added else (None, refs)
    out_ref, a_refs, w_refs = refs[0], refs[1:4], refs[4:]
    rows, _, slots, size, _ = out_ref.shape
    pair, here, _, _, per_group = place(sizes)
    width = per_group * rows

    for w_ref in w_refs:
        for j in range(count * slots):
            w_ref[j * LANES + size:(j + 1) * LANES, :] = jnp.zeros((LANES - size, slots * LANES), jnp.bfloat16)
    for i in range(rows):
        row = pair * rows + i
        targets = [cols_ref[s, here, row] for s in range(slots)]
        for k, shift in enumerate(shifts):
            group = lax.rem(here + shift, n_col)
            for t in range(slots):
                j = k * slots + t
                for a_ref, part in zip(a_refs, parts_of(unpack(strip_refs[k][i * slots + t], size))):
                    a_ref[:, j * LANES:(j + 1) * LANES] = part
                stored = occ_ref[t, group, row] == 1
                contracted = group * width + cols_ref[t, group, row]
                read = strip_block(sizes, rows, slots, mine_ref, other_ref, contracted)
                for s in range(slots):
                    index, valid = found(cols_ref, occ_ref, contracted, here, targets[s])
                    valid = valid & stored & (occ_ref[s, here, row] == 1)
                    block = jnp.where(valid, unpack(read(index), size), 0.0)
                    for w_ref, part in zip(w_refs, parts_of(block)):
                        w_ref[j * LANES:j * LANES + size, s * LANES:(s + 1) * LANES] = part

        def dot(a, w):
            return jnp.dot(a_refs[a][...], w_refs[w][...], preferred_element_type=jnp.float32)

        result = dot(0, 0) + ((dot(0, 1) + dot(1, 0)) + (dot(1, 1) + (dot(0, 2) + dot(2, 0))))
        for s in range(slots):
            block = result[:, s * LANES:s * LANES + size]
            out_ref[i, 0, s] = before_ref[i, 0, s] + block if added else block


def crossing(sizes, late, d):
    n_row, n_col, n_layer = sizes
    per_group = n_row * n_layer // n_col

    def device(group, number, column):
        pair = group * per_group + number
        return (pair // n_layer * n_col + column) * n_layer + pair % n_layer

    pairs = []
    for group in range(n_col):
        for number in range(per_group):
            for column in range(n_col):
                if (column - group) % n_col in late:
                    shift = d if group < column else d + 1
                    pairs.append((device(column, (number + shift) % per_group, group), device(group, number, column)))
    return pairs


def body(blocks, block_cols, occupancy):
    rows, _, slots, size, _ = blocks.shape
    sizes = tuple(lax.axis_size(axis) for axis in AXES)
    n_row, n_col, n_layer = sizes
    per_group = n_row * n_layer // n_col
    tall = tall_of(size)
    cols = jnp.transpose(block_cols, (2, 1, 0))
    occ = jnp.transpose(occupancy, (2, 1, 0))
    late = [k for k in range(n_col) if n_col < 4 * k < 3 * n_col]
    early = [k for k in range(n_col) if k not in late]

    def shape(count):
        return jax.ShapeDtypeStruct((count, tall, LANES), jnp.float32)

    packed = pl.pallas_call(
        pack_kernel,
        out_shape=shape(rows * slots),
        in_specs=[VMEM],
        out_specs=VMEM,
        compiler_params=LIMIT,
        name="pack",
    )(blocks)

    def shifted(k):
        return lax.ppermute(packed, "col", [((c + k) % n_col, c) for c in range(n_col)]) if k else packed

    strip = {k: shifted(k) for k in early}
    mine = [packed]
    for r in range(n_row):
        for y in range(0, n_layer, 2):
            if r or y:
                route = [
                    ((a + r) % n_row * n_layer + (b + y) % n_layer, a * n_layer + b)
                    for a in range(n_row) for b in range(n_layer)
                ]
                mine.append(lax.ppermute(packed, ("row", "layer"), route))
    crossed = pl.pallas_call(
        functools.partial(cross_kernel, sizes, rows),
        out_shape=[shape(rows * rows)] * (per_group // 2),
        in_specs=[SMEM, SMEM, VMEM],
        out_specs=[VMEM] * (per_group // 2),
        compiler_params=LIMIT,
        name="cross",
    )(cols, occ, packed)
    crossed = [lax.ppermute(value, AXES, crossing(sizes, late, d)) for d, value in enumerate(crossed)]

    ahead = [strip[k] for k in early if k] + crossed
    stacked = pl.pallas_call(
        functools.partial(stack_kernel, len(ahead)),
        out_shape=shape(len(mine) * rows * slots),
        in_specs=[pl.BlockSpec(memory_space=pl.ANY)] * len(ahead) + [VMEM] * len(mine),
        out_specs=VMEM,
        compiler_params=LIMIT,
        name="stack",
    )(*ahead, *mine)
    other = lax.ppermute(stacked, "layer", [(i, i ^ 1) for i in range(n_layer)])
    for k in late:
        strip[k] = shifted(k)

    trace = pl.pallas_call(
        functools.partial(trace_kernel, sizes, rows, size, early, late),
        out_shape=jax.ShapeDtypeStruct((n_row * n_col * n_layer, 1, LANES), jnp.float32),
        in_specs=[SMEM, SMEM] + [VMEM] * (len(early) + 2 + len(crossed)),
        out_specs=VMEM,
        scratch_shapes=[pltpu.VMEM((size, size), jnp.float32)],
        compiler_params=LIMIT,
        name="trace_terms",
    )(cols, occ, *[strip[k] for k in early], stacked, other, *crossed)
    trace = lax.all_to_all(trace, AXES, 0, 0, tiled=True)

    product = None
    for shifts in (early, late):
        inner = len(shifts) * slots * LANES
        product = pl.pallas_call(
            functools.partial(product_kernel, sizes, shifts, product is not None),
            out_shape=jax.ShapeDtypeStruct(blocks.shape, jnp.float32),
            in_specs=[SMEM, SMEM] + [VMEM] * (len(shifts) + 2 + (product is not None)),
            out_specs=VMEM,
            scratch_shapes=[pltpu.VMEM((size, inner), jnp.bfloat16)] * 3
            + [pltpu.VMEM((inner, slots * LANES), jnp.bfloat16)] * 3,
            compiler_params=LIMIT,
            name="multiply",
        )(cols, occ, *[strip[k] for k in shifts], stacked, other, *([] if product is None else [product]))
    return product, jnp.sum(trace[:, 0, 0])


def solution(mesh):
    in_specs = (P(("row", "layer"), "col", None, None, None), P(), P())
    out_specs = (P(("row", "layer"), "col", None, None, None), P())
    return jax.shard_map(body, mesh=mesh, in_specs=in_specs, out_specs=out_specs, check_vma=False)
```

```python
import functools

import jax
import jax.numpy as jnp
from jax import lax
from jax.experimental import pallas as pl
from jax.experimental.pallas import tpu as pltpu
from jax.sharding import PartitionSpec as P

LANES = 128
AXES = ("row", "col", "layer")
LIMIT = pltpu.CompilerParams(vmem_limit_bytes=48 * 2 ** 20)
VMEM = pl.BlockSpec(memory_space=pltpu.VMEM)
SMEM = pl.BlockSpec(memory_space=pltpu.SMEM)


def tall_of(size):
    return size * size // LANES


def unpack(block, size):
    tall = block.shape[0]
    spare = LANES - size
    rest = size - tall
    pieces = [block[q * rest:(q + 1) * rest, size:] for q in range(size // spare)]
    pieces.append(jnp.zeros((rest, spare), block.dtype))
    return jnp.concatenate([block, jnp.concatenate(pieces, axis=1)], axis=0)


def parts_of(value):
    parts = []
    for _ in range(3):
        part = value.astype(jnp.bfloat16)
        parts.append(part)
        value = value - part.astype(jnp.float32)
    return parts


def found(cols_ref, occ_ref, row, group, target):
    index = jnp.int32(0)
    valid = jnp.int32(0)
    for u in range(cols_ref.shape[0]):
        hit = jnp.where((cols_ref[u, group, row] == target) & (occ_ref[u, group, row] == 1), 1, 0)
        index = index + hit * u
        valid = valid + hit
    return index, valid > 0


def place(sizes):
    n_row, n_col, n_layer = sizes
    per_group = n_row * n_layer // n_col
    pair = lax.axis_index("row") * n_layer + lax.axis_index("layer")
    return pair, lax.axis_index("col"), lax.div(pair, per_group), lax.rem(pair, per_group), per_group


def pack_kernel(x_ref, out_ref):
    rows, _, slots, size, _ = x_ref.shape
    tall = tall_of(size)
    spare = LANES - size
    rest = size - tall
    for i in range(rows):
        for t in range(slots):
            n = i * slots + t
            out_ref[n, :, :size] = x_ref[i, 0, t, :tall, :]
            for q in range(size // spare):
                out_ref[n, q * rest:(q + 1) * rest, size:] = x_ref[i, 0, t, tall:, q * spare:(q + 1) * spare]


def stack_kernel(ahead, *refs):
    out_ref = refs[-1]
    for n, ref in enumerate(refs[ahead:-1]):
        out_ref[n * ref.shape[0]:(n + 1) * ref.shape[0]] = ref[...]


def strip_block(sizes, rows, slots, mine_ref, other_ref, contracted):
    _, _, n_layer = sizes
    chips = n_layer // 2
    my_row, my_layer = lax.axis_index("row"), lax.axis_index("layer")
    source = lax.div(contracted, rows)
    source_row, source_layer = lax.div(source, n_layer), lax.rem(source, n_layer)
    chip = lax.bitwise_xor(lax.div(source_layer, 2), lax.div(my_layer, 2))
    base = (lax.bitwise_xor(source_row, my_row) * chips + chip) * (rows * slots)
    base = base + lax.rem(contracted, rows) * slots
    same_core = lax.rem(source_layer, 2) == lax.rem(my_layer, 2)
    return lambda index: jnp.where(same_core, mine_ref[base + index], other_ref[base + index])


def product_kernel(sizes, masks, last, cols_ref, occ_ref, *refs):
    n_row, n_col, n_layer = sizes
    count = len(masks)
    strip_refs, (mine_ref, other_ref), refs = refs[:count], refs[count:count + 2], refs[count + 2:]
    before_ref, refs = (refs[0], refs[1:]) if last else (None, refs)
    out_ref, refs = refs[0], refs[1:]
    total_ref, refs = (refs[0], refs[1:]) if last else (None, refs)
    a_ref, w_refs = refs[0], refs[1:]
    rows, _, slots, size, _ = out_ref.shape
    pair, here, _, _, per_group = place(sizes)
    width = per_group * rows
    total = jnp.float32(0)

    for w_ref in w_refs:
        for j in range(count * slots):
            w_ref[j * LANES + size:(j + 1) * LANES, :] = jnp.zeros((LANES - size, slots * LANES), jnp.bfloat16)
    for i in range(rows):
        row = pair * rows + i
        targets = [cols_ref[s, here, row] for s in range(slots)]
        for k, mask in enumerate(masks):
            group = lax.bitwise_xor(here, mask)
            for t in range(slots):
                j = k * slots + t
                for n, part in enumerate(parts_of(unpack(strip_refs[k][i * slots + t], size))):
                    a_ref[n * size:(n + 1) * size, j * LANES:(j + 1) * LANES] = part
                stored = occ_ref[t, group, row] == 1
                contracted = group * width + cols_ref[t, group, row]
                read = strip_block(sizes, rows, slots, mine_ref, other_ref, contracted)
                for s in range(slots):
                    index, valid = found(cols_ref, occ_ref, contracted, here, targets[s])
                    valid = valid & stored & (occ_ref[s, here, row] == 1)
                    block = jnp.where(valid, unpack(read(index), size), 0.0)
                    for w_ref, part in zip(w_refs, parts_of(block)):
                        w_ref[j * LANES:j * LANES + size, s * LANES:(s + 1) * LANES] = part

        high, low, least = [
            jnp.dot(a_ref[:(3 - n) * size], w_refs[n][...], preferred_element_type=jnp.float32) for n in range(3)
        ]
        small = low[size:] + (least + high[2 * size:])
        result = high[:size] + ((low[:size] + high[size:2 * size]) + small)
        across = lax.broadcasted_iota(jnp.int32, (size, size), 0)
        down = lax.broadcasted_iota(jnp.int32, (size, size), 1)
        for s in range(slots):
            block = result[:, s * LANES:s * LANES + size]
            if last:
                block = before_ref[i, 0, s] + block
                on_diagonal = (here * width + targets[s] == row) & (occ_ref[s, here, row] == 1)
                total = total + jnp.sum(jnp.where((across == down) & on_diagonal, block, 0.0))
            out_ref[i, 0, s] = block
    if last:
        total_ref[...] = jnp.full(total_ref.shape, total, jnp.float32)


def exchanged(value, axis, mask):
    return lax.ppermute(value, axis, [(n, n ^ mask) for n in range(lax.axis_size(axis))])


def body(blocks, block_cols, occupancy):
    rows, _, slots, size, _ = blocks.shape
    sizes = tuple(lax.axis_size(axis) for axis in AXES)
    n_row, n_col, n_layer = sizes
    tall = tall_of(size)
    cols = jnp.transpose(block_cols, (2, 1, 0))
    occ = jnp.transpose(occupancy, (2, 1, 0))

    packed = pl.pallas_call(
        pack_kernel,
        out_shape=jax.ShapeDtypeStruct((rows * slots, tall, LANES), jnp.float32),
        in_specs=[VMEM],
        out_specs=VMEM,
        compiler_params=LIMIT,
        name="pack",
    )(blocks)

    strip = {0: packed}
    bit = n_col // 2
    while bit:
        for mask in list(strip):
            strip[mask | bit] = exchanged(strip[mask], "col", bit)
        bit //= 2
    early = sorted(m for m in strip if m & (m - 1) == 0)
    late = sorted(m for m in strip if m not in early)

    mine = {0: packed}
    steps = [("row", 1 << b, (1 << b) * (n_layer // 2)) for b in range((n_row - 1).bit_length())]
    steps += [("layer", 2 << b, 1 << b) for b in range((n_layer // 2 - 1).bit_length())]
    for axis, mask, offset in steps:
        for held in list(mine):
            mine[held | offset] = exchanged(mine[held], axis, mask)
    mine = [mine[n] for n in range(len(mine))]

    ahead = [strip[m] for m in early if m]
    stacked = pl.pallas_call(
        functools.partial(stack_kernel, len(ahead)),
        out_shape=jax.ShapeDtypeStruct((len(mine) * rows * slots, tall, LANES), jnp.float32),
        in_specs=[pl.BlockSpec(memory_space=pl.ANY)] * len(ahead) + [VMEM] * len(mine),
        out_specs=VMEM,
        compiler_params=LIMIT,
        name="stack",
    )(*ahead, *mine)
    other = exchanged(stacked, "layer", 1)

    whole = jax.ShapeDtypeStruct(blocks.shape, jnp.float32)
    terms = jax.ShapeDtypeStruct((n_row * n_col * n_layer, 1, LANES), jnp.float32)

    def multiplied(masks, before):
        inner = len(masks) * slots * LANES
        return pl.pallas_call(
            functools.partial(product_kernel, sizes, masks, bool(before)),
            out_shape=(whole, terms) if before else whole,
            in_specs=[SMEM, SMEM] + [VMEM] * (len(masks) + 2 + len(before)),
            out_specs=(VMEM, VMEM) if before else VMEM,
            scratch_shapes=[pltpu.VMEM((3 * size, inner), jnp.bfloat16)]
            + [pltpu.VMEM((inner, slots * LANES), jnp.bfloat16)] * 3,
            compiler_params=LIMIT,
            name="multiply",
        )(cols, occ, *[strip[m] for m in masks], stacked, other, *before)

    product, trace = multiplied(late, [multiplied(early, [])])
    trace = lax.all_to_all(trace, AXES, 0, 0, tiled=True)
    return product, jnp.sum(trace[:, 0, 0])


def solution(mesh):
    in_specs = (P(("row", "layer"), "col", None, None, None), P(), P())
    out_specs = (P(("row", "layer"), "col", None, None, None), P())
    return jax.shard_map(body, mesh=mesh, in_specs=in_specs, out_specs=out_specs, check_vma=False)
```

```python
import functools

import jax
import jax.numpy as jnp
from jax import lax
from jax.experimental import pallas as pl
from jax.experimental.pallas import tpu as pltpu
from jax.sharding import PartitionSpec as P

LANES = 128
AXES = ("row", "col", "layer")
LIMIT = pltpu.CompilerParams(vmem_limit_bytes=48 * 2 ** 20)
VMEM = pl.BlockSpec(memory_space=pltpu.VMEM)
SMEM = pl.BlockSpec(memory_space=pltpu.SMEM)


def tall_of(size):
    return size * size // LANES


def unpack(block, size):
    tall = block.shape[0]
    spare = LANES - size
    rest = size - tall
    pieces = [block[q * rest:(q + 1) * rest, size:] for q in range(size // spare)]
    pieces.append(jnp.zeros((rest, spare), block.dtype))
    return jnp.concatenate([block, jnp.concatenate(pieces, axis=1)], axis=0)


def parts_of(value):
    parts = []
    for _ in range(3):
        part = value.astype(jnp.bfloat16)
        parts.append(part)
        value = value - part.astype(jnp.float32)
    return parts


def place(sizes):
    n_row, n_col, n_layer = sizes
    per_group = n_row * n_layer // n_col
    pair = lax.axis_index("row") * n_layer + lax.axis_index("layer")
    return pair, lax.axis_index("col"), lax.div(pair, per_group), lax.rem(pair, per_group), per_group


def pack_kernel(x_ref, out_ref):
    rows, _, slots, size, _ = x_ref.shape
    tall = tall_of(size)
    spare = LANES - size
    rest = size - tall
    for i in range(rows):
        for t in range(slots):
            n = i * slots + t
            out_ref[n, :, :size] = x_ref[i, 0, t, :tall, :]
            for q in range(size // spare):
                out_ref[n, q * rest:(q + 1) * rest, size:] = x_ref[i, 0, t, tall:, q * spare:(q + 1) * spare]


def stack_kernel(count, *refs):
    out_ref = refs[-1]
    for n, ref in enumerate(refs[:count]):
        out_ref[n * ref.shape[0]:(n + 1) * ref.shape[0]] = ref[...]


def strip_block(sizes, rows, slots, mine_ref, other_ref, contracted):
    _, _, n_layer = sizes
    chips = n_layer // 2
    my_row, my_layer = lax.axis_index("row"), lax.axis_index("layer")
    source = lax.div(contracted, rows)
    source_row, source_layer = lax.div(source, n_layer), lax.rem(source, n_layer)
    chip = lax.bitwise_xor(lax.div(source_layer, 2), lax.div(my_layer, 2))
    base = (lax.bitwise_xor(source_row, my_row) * chips + chip) * (rows * slots)
    base = base + lax.rem(contracted, rows) * slots
    same_core = lax.rem(source_layer, 2) == lax.rem(my_layer, 2)
    return lambda index: jnp.where(same_core, mine_ref[base + index], other_ref[base + index])


def product_kernel(sizes, groups, added, summed, code_ref, *refs):
    n_row, n_col, n_layer = sizes
    count = len(groups)
    strip_refs, (mine_ref, other_ref), refs = refs[:count], refs[count:count + 2], refs[count + 2:]
    before_ref, refs = (refs[0], refs[1:]) if added else (None, refs)
    out_ref, refs = refs[0], refs[1:]
    total_ref, refs = (refs[0], refs[1:]) if summed else (None, refs)
    a_ref, w_refs = refs[0], refs[1:]
    rows, _, slots, size, _ = out_ref.shape
    pair, here, own_group, _, per_group = place(sizes)
    width = per_group * rows
    upper = own_group >= n_col // 2
    weights = sorted(set(weight for _, _, weight in groups))
    total = jnp.float32(0)

    for w_ref in w_refs:
        for j in range(count * slots):
            w_ref[j * LANES + size:(j + 1) * LANES, :] = jnp.zeros((LANES - size, slots * LANES), jnp.bfloat16)
    for i in range(rows):
        row = pair * rows + i
        targets = [code_ref[s, here, row] for s in range(slots)]
        for k, (value, value_upper, _) in enumerate(groups):
            group = lax.bitwise_xor(here, jnp.where(upper, value_upper, value))
            for t in range(slots):
                j = k * slots + t
                for n, part in enumerate(parts_of(unpack(strip_refs[k][i * slots + t], size))):
                    a_ref[n * size:(n + 1) * size, j * LANES:(j + 1) * LANES] = part
                column = code_ref[t, group, row]
                contracted = group * width + jnp.maximum(column, 0)
                read = strip_block(sizes, rows, slots, mine_ref, other_ref, contracted)
                sources = [jnp.where(column >= 0, code_ref[u, here, contracted], -1) for u in range(slots)]
                for s in range(slots):
                    hits = [source == targets[s] for source in sources]
                    index = functools.reduce(lambda rest, u: jnp.where(hits[u], u, rest), range(1, slots), 0)
                    valid = functools.reduce(jnp.logical_or, hits) & (targets[s] >= 0)
                    block = jnp.where(valid, unpack(read(index), size), 0.0)
                    for w_ref, part in zip(w_refs, parts_of(block)):
                        w_ref[j * LANES:j * LANES + size, s * LANES:(s + 1) * LANES] = part

        across = lax.broadcasted_iota(jnp.int32, (size, size), 0)
        down = lax.broadcasted_iota(jnp.int32, (size, size), 1)
        blocks = [before_ref[i, 0, s] if added else None for s in range(slots)]
        for weight in weights:
            inner = [k for k in range(count) if groups[k][2] == weight]
            first, end = inner[0] * slots * LANES, (inner[-1] + 1) * slots * LANES
            high, low, least = [
                jnp.dot(a_ref[:(3 - n) * size, first:end], w_refs[n][first:end], preferred_element_type=jnp.float32)
                for n in range(3)
            ]
            small = low[size:] + (least + high[2 * size:])
            result = high[:size] + ((low[:size] + high[size:2 * size]) + small)
            for s in range(slots):
                block = result[:, s * LANES:s * LANES + size]
                blocks[s] = block if blocks[s] is None else blocks[s] + block
                if summed:
                    on_diagonal = (here == own_group) & (here * width + targets[s] == row)
                    total = total + jnp.sum(jnp.where((across == down) & on_diagonal, weight * block, 0.0))
        for s in range(slots):
            out_ref[i, 0, s] = blocks[s]
    if summed:
        total_ref[...] = jnp.full(total_ref.shape, total, jnp.float32)


def exchanged(value, axis, mask):
    return lax.ppermute(value, axis, [(n, n ^ mask) for n in range(lax.axis_size(axis))])


def row_strip(packed, sizes):
    n_row, n_col, n_layer = sizes
    if n_col != 4:
        strip = {0: packed}
        bit = n_col // 2
        while bit:
            for mask in list(strip):
                strip[mask | bit] = exchanged(strip[mask], "col", bit)
            bit //= 2
        return [(strip[m], m, m, 1) for m in sorted(strip)], []
    per_group = n_row * n_layer // n_col
    route = []
    for r in range(n_row):
        for c in range(n_col):
            for y in range(n_layer):
                value = 2 if (r * n_layer + y) // per_group < n_col // 2 else 3
                route.append(((r * n_col + c) * n_layer + y, (r * n_col + (c ^ value)) * n_layer + y))
    far = lax.ppermute(packed, AXES, route)
    return [(packed, 0, 0, 1), (None, 1, 1, 1), (far, 2, 3, 2)], [(exchanged(far, "col", 1), 3, 2, 0)]


def body(blocks, block_cols, occupancy):
    rows, _, slots, size, _ = blocks.shape
    sizes = tuple(lax.axis_size(axis) for axis in AXES)
    n_row, n_col, n_layer = sizes
    chips = n_layer // 2
    tall = tall_of(size)
    code = jnp.where(occupancy == 1, block_cols, -1).transpose((2, 1, 0))

    packed = pl.pallas_call(
        pack_kernel,
        out_shape=jax.ShapeDtypeStruct((rows * slots, tall, LANES), jnp.float32),
        in_specs=[VMEM],
        out_specs=VMEM,
        compiler_params=LIMIT,
        name="pack",
    )(blocks)

    early, late = row_strip(packed, sizes)
    mine = [packed]
    for n in range(1, n_row * chips):
        row_bits, chip_bits = n // chips, n % chips
        route = [
            (a * n_layer + b, (a ^ row_bits) * n_layer + (b ^ (2 * chip_bits))) for a in range(n_row) for b in range(n_layer)
        ]
        mine.append(lax.ppermute(packed, ("row", "layer"), route))
    early = [(exchanged(packed, "col", 1) if share is None else share, *rest) for share, *rest in early]

    ahead = [share for share, value, _, _ in reversed(early) if value]
    stacked = pl.pallas_call(
        functools.partial(stack_kernel, len(mine)),
        out_shape=jax.ShapeDtypeStruct((len(mine) * rows * slots, tall, LANES), jnp.float32),
        in_specs=[VMEM] * len(mine) + [pl.BlockSpec(memory_space=pl.ANY)] * len(ahead),
        out_specs=VMEM,
        compiler_params=LIMIT,
        name="stack",
    )(*mine, *ahead)
    other = exchanged(stacked, "layer", 1)

    whole = jax.ShapeDtypeStruct(blocks.shape, jnp.float32)
    terms = jax.ShapeDtypeStruct((n_row * n_col * n_layer, 1, LANES), jnp.float32)

    def multiplied(some, before):
        inner = len(some) * slots * LANES
        summed = not before
        return pl.pallas_call(
            functools.partial(product_kernel, sizes, [tuple(rest) for _, *rest in some], bool(before), summed),
            out_shape=(whole, terms) if summed else whole,
            in_specs=[SMEM] + [VMEM] * (len(some) + 2 + len(before)),
            out_specs=(VMEM, VMEM) if summed else VMEM,
            scratch_shapes=[pltpu.VMEM((3 * size, inner), jnp.bfloat16)]
            + [pltpu.VMEM((inner, slots * LANES), jnp.bfloat16)] * 3,
            compiler_params=LIMIT,
            name="multiply",
        )(code, *[share for share, *_ in some], stacked, other, *before)

    product, trace = multiplied(early, [])
    trace = lax.all_to_all(trace, AXES, 0, 0, tiled=True)
    if late:
        product = multiplied(late, [product])
    return product, jnp.sum(trace[:, 0, 0])


def solution(mesh):
    in_specs = (P(("row", "layer"), "col", None, None, None), P(), P())
    out_specs = (P(("row", "layer"), "col", None, None, None), P())
    return jax.shard_map(body, mesh=mesh, in_specs=in_specs, out_specs=out_specs, check_vma=False)
```

```python
import functools

import jax
import jax.numpy as jnp
from jax import lax
from jax.experimental import pallas as pl
from jax.experimental.pallas import tpu as pltpu
from jax.sharding import PartitionSpec as P

LANES = 128
AXES = ("row", "col", "layer")
LIMIT = pltpu.CompilerParams(vmem_limit_bytes=48 * 2 ** 20)
VMEM = pl.BlockSpec(memory_space=pltpu.VMEM)
SMEM = pl.BlockSpec(memory_space=pltpu.SMEM)


def tall_of(size):
    return size * size // LANES


def unpack(block, size):
    tall = block.shape[0]
    spare = LANES - size
    rest = size - tall
    pieces = [block[q * rest:(q + 1) * rest, size:] for q in range(size // spare)]
    pieces.append(jnp.zeros((rest, spare), block.dtype))
    return jnp.concatenate([block, jnp.concatenate(pieces, axis=1)], axis=0)


def parts_of(value):
    parts = []
    for _ in range(3):
        part = value.astype(jnp.bfloat16)
        parts.append(part)
        value = value - part.astype(jnp.float32)
    return parts


def place(sizes):
    n_row, n_col, n_layer = sizes
    per_group = n_row * n_layer // n_col
    pair = lax.axis_index("row") * n_layer + lax.axis_index("layer")
    return pair, lax.axis_index("col"), lax.div(pair, per_group), lax.rem(pair, per_group), per_group


def pack_kernel(x_ref, out_ref):
    rows, _, slots, size, _ = x_ref.shape
    tall = tall_of(size)
    spare = LANES - size
    rest = size - tall
    for i in range(rows):
        for t in range(slots):
            n = i * slots + t
            out_ref[n, :, :size] = x_ref[i, 0, t, :tall, :]
            for q in range(size // spare):
                out_ref[n, q * rest:(q + 1) * rest, size:] = x_ref[i, 0, t, tall:, q * spare:(q + 1) * spare]


def stack_kernel(count, *refs):
    out_ref = refs[-1]
    for n, ref in enumerate(refs[:count]):
        out_ref[n * ref.shape[0]:(n + 1) * ref.shape[0]] = ref[...]


def strip_block(sizes, rows, slots, mine_ref, other_ref, contracted):
    _, _, n_layer = sizes
    chips = n_layer // 2
    my_row, my_layer = lax.axis_index("row"), lax.axis_index("layer")
    source = lax.div(contracted, rows)
    source_row, source_layer = lax.div(source, n_layer), lax.rem(source, n_layer)
    chip = lax.bitwise_xor(lax.div(source_layer, 2), lax.div(my_layer, 2))
    base = (lax.bitwise_xor(source_row, my_row) * chips + chip) * (rows * slots)
    base = base + lax.rem(contracted, rows) * slots
    same_core = lax.rem(source_layer, 2) == lax.rem(my_layer, 2)
    return lambda index: jnp.where(same_core, mine_ref[base + index], other_ref[base + index])


def group_at(sizes, here, own_group, values):
    return lax.bitwise_xor(here, jnp.where(own_group >= sizes[1] // 2, values[1], values[0]))


def matched(code_ref, here, contracted, stored, target):
    index, valid = jnp.int32(0), jnp.bool_(False)
    for u in range(code_ref.shape[0]):
        hit = code_ref[u, here, contracted] == target
        index = jnp.where(hit, u, index)
        valid = valid | hit
    return index, valid & stored & (target >= 0)


def trace_kernel(sizes, rows, size, groups, code_ref, *refs):
    count = len(groups)
    strip_refs, (mine_ref, other_ref), total_ref = refs[:count], refs[count:count + 2], refs[-1]
    slots = code_ref.shape[0]
    pair, here, own_group, number, per_group = place(sizes)
    width = per_group * rows

    def straight(block):
        return unpack(block, size)[:, :size]

    @pl.when(own_group == here)
    def _():
        total = jnp.zeros((size, size), jnp.float32)
        for i in range(rows):
            row = pair * rows + i
            for strip_ref, (value, value_upper, weight) in zip(strip_refs, groups):
                group = group_at(sizes, here, own_group, (value, value_upper))
                for t in range(slots):
                    column = code_ref[t, group, row]
                    contracted = group * width + jnp.maximum(column, 0)
                    index, valid = matched(code_ref, here, contracted, column >= 0, number * rows + i)
                    block = strip_block(sizes, rows, slots, mine_ref, other_ref, contracted)(index)
                    term = straight(strip_ref[i * slots + t]) * straight(block).T
                    total = total + jnp.where(valid, weight * term, 0.0)
        total_ref[...] = jnp.full(total_ref.shape, jnp.sum(total), jnp.float32)

    @pl.when(own_group != here)
    def _():
        total_ref[...] = jnp.zeros(total_ref.shape, jnp.float32)


def product_kernel(sizes, groups, code_ref, *refs):
    count = len(groups)
    strip_refs, (mine_ref, other_ref), out_ref = refs[:count], refs[count:count + 2], refs[count + 2]
    a_ref, w_refs = refs[count + 3], refs[count + 4:]
    rows, _, slots, size, _ = out_ref.shape
    pair, here, own_group, _, per_group = place(sizes)
    width = per_group * rows

    for w_ref in w_refs:
        for j in range(count * slots):
            w_ref[j * LANES + size:(j + 1) * LANES, :] = jnp.zeros((LANES - size, slots * LANES), jnp.bfloat16)
    for i in range(rows):
        row = pair * rows + i
        targets = [code_ref[s, here, row] for s in range(slots)]
        for k, (value, value_upper, _) in enumerate(groups):
            group = group_at(sizes, here, own_group, (value, value_upper))
            for t in range(slots):
                j = k * slots + t
                for n, part in enumerate(parts_of(unpack(strip_refs[k][i * slots + t], size))):
                    a_ref[n * size:(n + 1) * size, j * LANES:(j + 1) * LANES] = part
                column = code_ref[t, group, row]
                contracted = group * width + jnp.maximum(column, 0)
                read = strip_block(sizes, rows, slots, mine_ref, other_ref, contracted)
                for s in range(slots):
                    index, valid = matched(code_ref, here, contracted, column >= 0, targets[s])
                    block = jnp.where(valid, unpack(read(index), size), 0.0)
                    for w_ref, part in zip(w_refs, parts_of(block)):
                        w_ref[j * LANES:j * LANES + size, s * LANES:(s + 1) * LANES] = part

        high, low, least = [
            jnp.dot(a_ref[:(3 - n) * size], w_refs[n][...], preferred_element_type=jnp.float32) for n in range(3)
        ]
        small = low[size:] + (least + high[2 * size:])
        result = high[:size] + ((low[:size] + high[size:2 * size]) + small)
        for s in range(slots):
            out_ref[i, 0, s] = result[:, s * LANES:s * LANES + size]


def exchanged(value, axis, mask):
    return lax.ppermute(value, axis, [(n, n ^ mask) for n in range(lax.axis_size(axis))])


def row_strip(packed, sizes):
    n_row, n_col, n_layer = sizes
    if n_col != 4:
        strip = {0: packed}
        bit = n_col // 2
        while bit:
            for mask in list(strip):
                strip[mask | bit] = exchanged(strip[mask], "col", bit)
            bit //= 2
        return [(strip[m], m, m, 1) for m in sorted(strip)], []
    per_group = n_row * n_layer // n_col
    route = []
    for r in range(n_row):
        for c in range(n_col):
            for y in range(n_layer):
                value = 2 if (r * n_layer + y) // per_group < n_col // 2 else 3
                route.append(((r * n_col + c) * n_layer + y, (r * n_col + (c ^ value)) * n_layer + y))
    far = lax.ppermute(packed, AXES, route)
    return [(packed, 0, 0, 1), (None, 1, 1, 1), (far, 2, 3, 2)], [(exchanged(far, "col", 1), 3, 2, 0)]


def body(blocks, block_cols, occupancy):
    rows, _, slots, size, _ = blocks.shape
    sizes = tuple(lax.axis_size(axis) for axis in AXES)
    n_row, n_col, n_layer = sizes
    chips = n_layer // 2
    tall = tall_of(size)
    code = jnp.where(occupancy == 1, block_cols, -1).transpose((2, 1, 0))

    packed = pl.pallas_call(
        pack_kernel,
        out_shape=jax.ShapeDtypeStruct((rows * slots, tall, LANES), jnp.float32),
        in_specs=[VMEM],
        out_specs=VMEM,
        compiler_params=LIMIT,
        name="pack",
    )(blocks)

    early, late = row_strip(packed, sizes)
    mine = [packed]
    for n in range(1, n_row * chips):
        row_bits, chip_bits = n // chips, n % chips
        route = [
            (a * n_layer + b, (a ^ row_bits) * n_layer + (b ^ (2 * chip_bits))) for a in range(n_row) for b in range(n_layer)
        ]
        mine.append(lax.ppermute(packed, ("row", "layer"), route))
    early = [(exchanged(packed, "col", 1) if share is None else share, *rest) for share, *rest in early]

    ahead = [share for share, value, _, _ in reversed(early) if value]
    stacked = pl.pallas_call(
        functools.partial(stack_kernel, len(mine)),
        out_shape=jax.ShapeDtypeStruct((len(mine) * rows * slots, tall, LANES), jnp.float32),
        in_specs=[VMEM] * len(mine) + [pl.BlockSpec(memory_space=pl.ANY)] * len(ahead),
        out_specs=VMEM,
        compiler_params=LIMIT,
        name="stack",
    )(*mine, *ahead)
    other = exchanged(stacked, "layer", 1)

    trace = pl.pallas_call(
        functools.partial(trace_kernel, sizes, rows, size, [tuple(rest) for _, *rest in early]),
        out_shape=jax.ShapeDtypeStruct((n_row * n_col * n_layer, 1, LANES), jnp.float32),
        in_specs=[SMEM] + [VMEM] * (len(early) + 2),
        out_specs=VMEM,
        compiler_params=LIMIT,
        name="trace_terms",
    )(code, *[share for share, *_ in early], stacked, other)
    trace = lax.all_to_all(trace, AXES, 0, 0, tiled=True)

    strip = early + late
    inner = len(strip) * slots * LANES
    product = pl.pallas_call(
        functools.partial(product_kernel, sizes, [tuple(rest) for _, *rest in strip]),
        out_shape=jax.ShapeDtypeStruct(blocks.shape, jnp.float32),
        in_specs=[SMEM] + [VMEM] * (len(strip) + 2),
        out_specs=VMEM,
        scratch_shapes=[pltpu.VMEM((3 * size, inner), jnp.bfloat16)]
        + [pltpu.VMEM((inner, slots * LANES), jnp.bfloat16)] * 3,
        compiler_params=LIMIT,
        name="multiply",
    )(code, *[share for share, *_ in strip], stacked, other)
    return product, jnp.sum(trace[:, 0, 0])


def solution(mesh):
    in_specs = (P(("row", "layer"), "col", None, None, None), P(), P())
    out_specs = (P(("row", "layer"), "col", None, None, None), P())
    return jax.shard_map(body, mesh=mesh, in_specs=in_specs, out_specs=out_specs, check_vma=False)
```

```python
import functools

import jax
import jax.numpy as jnp
from jax import lax
from jax.experimental import pallas as pl
from jax.experimental.pallas import tpu as pltpu
from jax.sharding import PartitionSpec as P

LANES = 128
AXES = ("row", "col", "layer")
LIMIT = pltpu.CompilerParams(vmem_limit_bytes=48 * 2 ** 20)
VMEM = pl.BlockSpec(memory_space=pltpu.VMEM)
SMEM = pl.BlockSpec(memory_space=pltpu.SMEM)
UNREAD = pl.BlockSpec(memory_space=pl.ANY)


def tall_of(size):
    return size * size // LANES


def unpack(block, size):
    tall = block.shape[0]
    spare = LANES - size
    rest = size - tall
    pieces = [block[q * rest:(q + 1) * rest, size:] for q in range(size // spare)]
    pieces.append(jnp.zeros((rest, spare), block.dtype))
    return jnp.concatenate([block, jnp.concatenate(pieces, axis=1)], axis=0)


def parts_of(value):
    parts = []
    for _ in range(3):
        part = value.astype(jnp.bfloat16)
        parts.append(part)
        value = value - part.astype(jnp.float32)
    return parts


def place(sizes):
    n_row, n_col, n_layer = sizes
    per_group = n_row * n_layer // n_col
    pair = lax.axis_index("row") * n_layer + lax.axis_index("layer")
    return pair, lax.axis_index("col"), lax.div(pair, per_group), lax.rem(pair, per_group), per_group


def pack_kernel(x_ref, out_ref):
    rows, _, slots, size, _ = x_ref.shape
    tall = tall_of(size)
    spare = LANES - size
    rest = size - tall
    for i in range(rows):
        for t in range(slots):
            n = i * slots + t
            out_ref[n, :, :size] = x_ref[i, 0, t, :tall, :]
            for q in range(size // spare):
                out_ref[n, q * rest:(q + 1) * rest, size:] = x_ref[i, 0, t, tall:, q * spare:(q + 1) * spare]


def stack_kernel(first, count, *refs):
    out_ref = refs[-1]
    for n, ref in enumerate(refs[first:first + count]):
        out_ref[n * ref.shape[0]:(n + 1) * ref.shape[0]] = ref[...]


def strip_block(sizes, rows, slots, mine_ref, other_ref, contracted):
    _, _, n_layer = sizes
    chips = n_layer // 2
    my_row, my_layer = lax.axis_index("row"), lax.axis_index("layer")
    source = lax.div(contracted, rows)
    source_row, source_layer = lax.div(source, n_layer), lax.rem(source, n_layer)
    chip = lax.bitwise_xor(lax.div(source_layer, 2), lax.div(my_layer, 2))
    base = (lax.bitwise_xor(source_row, my_row) * chips + chip) * (rows * slots)
    base = base + lax.rem(contracted, rows) * slots
    same_core = lax.rem(source_layer, 2) == lax.rem(my_layer, 2)
    return lambda index: jnp.where(same_core, mine_ref[base + index], other_ref[base + index])


def group_at(sizes, here, own_group, values):
    return lax.bitwise_xor(here, jnp.where(own_group >= sizes[1] // 2, values[1], values[0]))


def matched(code_ref, here, contracted, stored, target):
    index, valid = jnp.int32(0), jnp.bool_(False)
    for u in range(code_ref.shape[0]):
        hit = code_ref[u, here, contracted] == target
        index = jnp.where(hit, u, index)
        valid = valid | hit
    return index, valid & stored & (target >= 0)


def trace_kernel(sizes, rows, size, groups, code_ref, *refs):
    count = len(groups)
    (mine_ref, other_ref), strip_refs, total_ref = refs[:2], refs[2:2 + count], refs[-1]
    slots = code_ref.shape[0]
    pair, here, own_group, number, per_group = place(sizes)
    width = per_group * rows

    def straight(block):
        return unpack(block, size)[:, :size]

    @pl.when(own_group == here)
    def _():
        total = jnp.zeros((size, size), jnp.float32)
        for i in range(rows):
            row = pair * rows + i
            for strip_ref, (value, value_upper, weight) in zip(strip_refs, groups):
                group = group_at(sizes, here, own_group, (value, value_upper))
                for t in range(slots):
                    column = code_ref[t, group, row]
                    contracted = group * width + jnp.maximum(column, 0)
                    index, valid = matched(code_ref, here, contracted, column >= 0, number * rows + i)
                    block = strip_block(sizes, rows, slots, mine_ref, other_ref, contracted)(index)
                    term = straight(strip_ref[i * slots + t]) * straight(block).T
                    total = total + jnp.where(valid, weight * term, 0.0)
        total_ref[...] = jnp.full(total_ref.shape, jnp.sum(total), jnp.float32)

    @pl.when(own_group != here)
    def _():
        total_ref[...] = jnp.zeros(total_ref.shape, jnp.float32)


def product_kernel(sizes, groups, code_ref, *refs):
    count = len(groups)
    (mine_ref, other_ref), strip_refs = refs[:2], refs[2:2 + count]
    out_ref, a_ref, *w_refs = refs[-5:]
    rows, _, slots, size, _ = out_ref.shape
    pair, here, own_group, _, per_group = place(sizes)
    width = per_group * rows

    for w_ref in w_refs:
        for j in range(count * slots):
            w_ref[j * LANES + size:(j + 1) * LANES, :] = jnp.zeros((LANES - size, slots * LANES), jnp.bfloat16)
    for i in range(rows):
        row = pair * rows + i
        targets = [code_ref[s, here, row] for s in range(slots)]
        for k, (value, value_upper, _) in enumerate(groups):
            group = group_at(sizes, here, own_group, (value, value_upper))
            for t in range(slots):
                j = k * slots + t
                for n, part in enumerate(parts_of(unpack(strip_refs[k][i * slots + t], size))):
                    a_ref[n * size:(n + 1) * size, j * LANES:(j + 1) * LANES] = part
                column = code_ref[t, group, row]
                contracted = group * width + jnp.maximum(column, 0)
                read = strip_block(sizes, rows, slots, mine_ref, other_ref, contracted)
                for s in range(slots):
                    index, valid = matched(code_ref, here, contracted, column >= 0, targets[s])
                    block = jnp.where(valid, unpack(read(index), size), 0.0)
                    for w_ref, part in zip(w_refs, parts_of(block)):
                        w_ref[j * LANES:j * LANES + size, s * LANES:(s + 1) * LANES] = part

        high, low, least = [
            jnp.dot(a_ref[:(3 - n) * size], w_refs[n][...], preferred_element_type=jnp.float32) for n in range(3)
        ]
        small = low[size:] + (least + high[2 * size:])
        result = high[:size] + ((low[:size] + high[size:2 * size]) + small)
        for s in range(slots):
            out_ref[i, 0, s] = result[:, s * LANES:s * LANES + size]


def exchanged(value, axis, mask):
    return lax.ppermute(value, axis, [(n, n ^ mask) for n in range(lax.axis_size(axis))])


def row_strip(packed, sizes):
    n_row, n_col, n_layer = sizes
    if n_col != 4:
        strip = {0: packed}
        bit = n_col // 2
        while bit:
            for mask in list(strip):
                strip[mask | bit] = exchanged(strip[mask], "col", bit)
            bit //= 2
        return [(strip[m], m, m, 1) for m in sorted(strip)], []
    per_group = n_row * n_layer // n_col
    route = []
    for r in range(n_row):
        for c in range(n_col):
            for y in range(n_layer):
                value = 2 if (r * n_layer + y) // per_group < n_col // 2 else 3
                route.append(((r * n_col + c) * n_layer + y, (r * n_col + (c ^ value)) * n_layer + y))
    far = lax.ppermute(packed, AXES, route)
    return [(packed, 0, 0, 1), (None, 1, 1, 1), (far, 2, 3, 2)], [(exchanged(far, "col", 1), 3, 2, 0)]


def body(blocks, block_cols, occupancy):
    rows, _, slots, size, _ = blocks.shape
    sizes = tuple(lax.axis_size(axis) for axis in AXES)
    n_row, n_col, n_layer = sizes
    chips = n_layer // 2
    tall = tall_of(size)
    code = jnp.where(occupancy == 1, block_cols, -1).transpose((2, 1, 0))

    packed = pl.pallas_call(
        pack_kernel,
        out_shape=jax.ShapeDtypeStruct((rows * slots, tall, LANES), jnp.float32),
        in_specs=[VMEM],
        out_specs=VMEM,
        compiler_params=LIMIT,
        name="pack",
    )(blocks)

    early, late = row_strip(packed, sizes)
    mine = [packed]
    for n in range(1, n_row * chips):
        row_bits, chip_bits = n // chips, n % chips
        route = [
            (a * n_layer + b, (a ^ row_bits) * n_layer + (b ^ (2 * chip_bits))) for a in range(n_row) for b in range(n_layer)
        ]
        mine.append(lax.ppermute(packed, ("row", "layer"), route))
    early = [(exchanged(packed, "col", 1) if share is None else share, *rest) for share, *rest in early]

    far = [share for share, value, _, _ in early if value > 1]
    near = [share for share, value, _, _ in early if value == 1]
    stacked = pl.pallas_call(
        functools.partial(stack_kernel, len(far), len(mine)),
        out_shape=jax.ShapeDtypeStruct((len(mine) * rows * slots, tall, LANES), jnp.float32),
        in_specs=[UNREAD] * len(far) + [VMEM] * len(mine) + [UNREAD] * len(near),
        out_specs=VMEM,
        compiler_params=LIMIT,
        name="stack",
    )(*far, *mine, *near)
    other = exchanged(stacked, "layer", 1)

    trace = pl.pallas_call(
        functools.partial(trace_kernel, sizes, rows, size, [tuple(rest) for _, *rest in early]),
        out_shape=jax.ShapeDtypeStruct((n_row * n_col * n_layer, 1, LANES), jnp.float32),
        in_specs=[SMEM] + [VMEM] * (len(early) + 2) + [UNREAD] * (len(mine) - 1),
        out_specs=VMEM,
        compiler_params=LIMIT,
        name="trace_terms",
    )(code, stacked, other, *[share for share, *_ in early], *mine[1:])
    trace = lax.all_to_all(trace, AXES, 0, 0, tiled=True)

    strip = early + late
    inner = len(strip) * slots * LANES
    product = pl.pallas_call(
        functools.partial(product_kernel, sizes, [tuple(rest) for _, *rest in strip]),
        out_shape=jax.ShapeDtypeStruct(blocks.shape, jnp.float32),
        in_specs=[SMEM] + [VMEM] * (len(strip) + 2) + [UNREAD] * (len(mine) - 1),
        out_specs=VMEM,
        scratch_shapes=[pltpu.VMEM((3 * size, inner), jnp.bfloat16)]
        + [pltpu.VMEM((inner, slots * LANES), jnp.bfloat16)] * 3,
        compiler_params=LIMIT,
        name="multiply",
    )(code, stacked, other, *[share for share, *_ in strip], *mine[1:])
    return product, jnp.sum(trace[:, 0, 0])


def solution(mesh):
    in_specs = (P(("row", "layer"), "col", None, None, None), P(), P())
    out_specs = (P(("row", "layer"), "col", None, None, None), P())
    return jax.shard_map(body, mesh=mesh, in_specs=in_specs, out_specs=out_specs, check_vma=False)
```

```python
import functools

import jax
import jax.numpy as jnp
from jax import lax
from jax.experimental import pallas as pl
from jax.experimental.pallas import tpu as pltpu
from jax.sharding import PartitionSpec as P

LANES = 128
AXES = ("row", "col", "layer")
LIMIT = pltpu.CompilerParams(vmem_limit_bytes=48 * 2 ** 20)
VMEM = pl.BlockSpec(memory_space=pltpu.VMEM)
SMEM = pl.BlockSpec(memory_space=pltpu.SMEM)
UNREAD = pl.BlockSpec(memory_space=pl.ANY)


def tall_of(size):
    return size * size // LANES


def unpack(block, size):
    tall = block.shape[0]
    spare = LANES - size
    rest = size - tall
    pieces = [block[q * rest:(q + 1) * rest, size:] for q in range(size // spare)]
    pieces.append(jnp.zeros((rest, spare), block.dtype))
    return jnp.concatenate([block, jnp.concatenate(pieces, axis=1)], axis=0)


def parts_of(value):
    parts = []
    for _ in range(3):
        part = value.astype(jnp.bfloat16)
        parts.append(part)
        value = value - part.astype(jnp.float32)
    return parts


def place(sizes):
    n_row, n_col, n_layer = sizes
    per_group = n_row * n_layer // n_col
    pair = lax.axis_index("row") * n_layer + lax.axis_index("layer")
    return pair, lax.axis_index("col"), lax.div(pair, per_group), lax.rem(pair, per_group), per_group


def pack_kernel(x_ref, out_ref, held_ref, sems):
    rows, _, slots, size, _ = x_ref.shape
    tall = tall_of(size)
    spare = LANES - size
    rest = size - tall
    copies = []
    for n in range(rows * slots):
        copies.append(pltpu.make_async_copy(x_ref.at[n // slots, 0, n % slots], held_ref.at[n], sems.at[n]))
        copies[-1].start()
    for n, copy in enumerate(copies):
        copy.wait()
        out_ref[n, :, :size] = held_ref[n, :tall, :]
        for q in range(size // spare):
            out_ref[n, q * rest:(q + 1) * rest, size:] = held_ref[n, tall:, q * spare:(q + 1) * spare]


def strip_base(sizes, rows, slots, contracted):
    n_layer = sizes[2]
    chips = n_layer // 2
    my_row, my_layer = lax.axis_index("row"), lax.axis_index("layer")
    source = lax.div(contracted, rows)
    source_row, source_layer = lax.div(source, n_layer), lax.rem(source, n_layer)
    chip = lax.bitwise_xor(lax.div(source_layer, 2), lax.div(my_layer, 2))
    base = (lax.bitwise_xor(source_row, my_row) * chips + chip) * (rows * slots)
    base = base + lax.rem(contracted, rows) * slots
    other_core = lax.bitwise_xor(lax.rem(source_layer, 2), lax.rem(my_layer, 2))
    return base + other_core * (sizes[0] * chips * rows * slots)


def group_at(sizes, here, own_group, values):
    return lax.bitwise_xor(here, jnp.where(own_group >= sizes[1] // 2, values[1], values[0]))


def matched(code_ref, here, contracted, stored, target):
    index, valid = jnp.int32(0), jnp.bool_(False)
    for u in range(code_ref.shape[0]):
        hit = code_ref[u, here, contracted] == target
        index = jnp.where(hit, u, index)
        valid = valid | hit
    return index, valid & stored & (target >= 0)


def stack_kernel(sizes, rows, size, groups, parts, code_ref, *refs):
    far, shares, near = parts
    share_refs = refs[far:far + shares // 2] + refs[far + shares // 2 + near:far + shares + near]
    strip_refs = [refs[far]] + list(refs[far + shares // 2:far + shares // 2 + near]) + list(refs[:far])
    out_ref, total_ref = refs[-2:]
    slots = code_ref.shape[0]
    pair, here, own_group, number, per_group = place(sizes)
    width = per_group * rows
    for n, ref in enumerate(share_refs):
        out_ref[n * rows * slots:(n + 1) * rows * slots] = ref[...]

    def straight(block):
        return unpack(block, size)[:, :size]

    @pl.when(own_group == here)
    def _():
        total = jnp.zeros((size, size), jnp.float32)
        for i in range(rows):
            row = pair * rows + i
            for strip_ref, (value, value_upper, weight) in zip(strip_refs, groups):
                group = group_at(sizes, here, own_group, (value, value_upper))
                for t in range(slots):
                    column = code_ref[t, group, row]
                    contracted = group * width + jnp.maximum(column, 0)
                    index, valid = matched(code_ref, here, contracted, column >= 0, number * rows + i)
                    block = out_ref[strip_base(sizes, rows, slots, contracted) + index]
                    term = straight(strip_ref[i * slots + t]) * straight(block).T
                    total = total + jnp.where(valid, weight * term, 0.0)
        total_ref[...] = jnp.full(total_ref.shape, jnp.sum(total), jnp.float32)

    @pl.when(own_group != here)
    def _():
        total_ref[...] = jnp.zeros(total_ref.shape, jnp.float32)


def sum_kernel(terms_ref, out_ref):
    out_ref[...] = jnp.sum(terms_ref[...], axis=0)[:, :1]


def product_kernel(sizes, groups, code_ref, *refs):
    count = len(groups)
    column_ref, strip_refs = refs[0], refs[1:1 + count]
    out_ref, a_ref, *w_refs = refs[-5:]
    rows, _, slots, size, _ = out_ref.shape
    pair, here, own_group, _, per_group = place(sizes)
    width = per_group * rows

    for w_ref in w_refs:
        for j in range(count * slots):
            w_ref[j * LANES + size:(j + 1) * LANES, :] = jnp.zeros((LANES - size, slots * LANES), jnp.bfloat16)
    for i in range(rows):
        row = pair * rows + i
        targets = [code_ref[s, here, row] for s in range(slots)]
        for k, (value, value_upper, _) in enumerate(groups):
            group = group_at(sizes, here, own_group, (value, value_upper))
            for t in range(slots):
                j = k * slots + t
                for n, part in enumerate(parts_of(unpack(strip_refs[k][i * slots + t], size))):
                    a_ref[n * size:(n + 1) * size, j * LANES:(j + 1) * LANES] = part
                column = code_ref[t, group, row]
                contracted = group * width + jnp.maximum(column, 0)
                base = strip_base(sizes, rows, slots, contracted)
                for s in range(slots):
                    index, valid = matched(code_ref, here, contracted, column >= 0, targets[s])
                    block = jnp.where(valid, unpack(column_ref[base + index], size), 0.0)
                    for w_ref, part in zip(w_refs, parts_of(block)):
                        w_ref[j * LANES:j * LANES + size, s * LANES:(s + 1) * LANES] = part

        high, low, least = [
            jnp.dot(a_ref[:(3 - n) * size], w_refs[n][...], preferred_element_type=jnp.float32) for n in range(3)
        ]
        small = low[size:] + (least + high[2 * size:])
        result = high[:size] + ((low[:size] + high[size:2 * size]) + small)
        for s in range(slots):
            out_ref[i, 0, s] = result[:, s * LANES:s * LANES + size]


def exchanged(value, axis, mask):
    return lax.ppermute(value, axis, [(n, n ^ mask) for n in range(lax.axis_size(axis))])


def row_strip(packed, sizes):
    n_row, n_col, n_layer = sizes
    if n_col != 4:
        strip = {0: packed}
        bit = n_col // 2
        while bit:
            for mask in list(strip):
                strip[mask | bit] = exchanged(strip[mask], "col", bit)
            bit //= 2
        return [(strip[m], m, m, 1) for m in sorted(strip)], []
    per_group = n_row * n_layer // n_col
    route = []
    for r in range(n_row):
        for c in range(n_col):
            for y in range(n_layer):
                value = 2 if (r * n_layer + y) // per_group < n_col // 2 else 3
                route.append(((r * n_col + c) * n_layer + y, (r * n_col + (c ^ value)) * n_layer + y))
    far = lax.ppermute(packed, AXES, route)
    return [(packed, 0, 0, 1), (None, 1, 1, 1), (far, 2, 3, 2)], [(exchanged(far, "col", 1), 3, 2, 0)]


def body(blocks, block_cols, occupancy):
    rows, _, slots, size, _ = blocks.shape
    sizes = tuple(lax.axis_size(axis) for axis in AXES)
    n_row, n_col, n_layer = sizes
    chips = n_layer // 2
    tall = tall_of(size)
    code = jnp.where(occupancy == 1, block_cols, -1).transpose((2, 1, 0))

    packed = pl.pallas_call(
        pack_kernel,
        out_shape=jax.ShapeDtypeStruct((rows * slots, tall, LANES), jnp.float32),
        in_specs=[pl.BlockSpec(memory_space=pltpu.HBM)],
        out_specs=VMEM,
        scratch_shapes=[
            pltpu.VMEM((rows * slots, size, size), jnp.float32),
            pltpu.SemaphoreType.DMA((rows * slots,)),
        ],
        compiler_params=LIMIT,
        name="pack",
    )(blocks)

    early, late = row_strip(packed, sizes)
    mine = {0: packed}
    steps = [("row", 1 << b, chips << b) for b in range((n_row - 1).bit_length())]
    steps += [("layer", 2 << b, 1 << b) for b in range((chips - 1).bit_length())]
    for axis, mask, offset in steps:
        for held in list(mine):
            mine[held | offset] = exchanged(mine[held], axis, mask)
    mine = [mine[n] for n in range(len(mine))]
    early = [(exchanged(packed, "col", 1) if share is None else share, *rest) for share, *rest in early]

    others = [exchanged(share, "layer", 1) for share in mine]

    far = [share for share, value, _, _ in early if value > 1]
    near = [share for share, value, _, _ in early if value == 1]
    operands = far + mine + near + others
    stacked, trace = pl.pallas_call(
        functools.partial(
            stack_kernel, sizes, rows, size, [tuple(rest) for _, *rest in early], (len(far), 2 * len(mine), len(near))
        ),
        out_shape=(
            jax.ShapeDtypeStruct((2 * len(mine) * rows * slots, tall, LANES), jnp.float32),
            jax.ShapeDtypeStruct((n_row * n_col * n_layer, 1, LANES), jnp.float32),
        ),
        in_specs=[SMEM] + [VMEM] * len(operands),
        out_specs=(VMEM, VMEM),
        compiler_params=LIMIT,
        name="stack",
    )(code, *operands)
    trace = lax.all_to_all(trace, AXES, 0, 0, tiled=True)

    strip = early + late
    inner = len(strip) * slots * LANES
    product = pl.pallas_call(
        functools.partial(product_kernel, sizes, [tuple(rest) for _, *rest in strip]),
        out_shape=jax.ShapeDtypeStruct(blocks.shape, jnp.float32),
        in_specs=[SMEM] + [VMEM] * (len(strip) + 1),
        out_specs=VMEM,
        scratch_shapes=[pltpu.VMEM((3 * size, inner), jnp.bfloat16)]
        + [pltpu.VMEM((inner, slots * LANES), jnp.bfloat16)] * 3,
        compiler_params=LIMIT,
        name="multiply",
    )(code, stacked, *[share for share, *_ in strip])
    trace = pl.pallas_call(
        sum_kernel,
        out_shape=jax.ShapeDtypeStruct((1, 1), jnp.float32),
        in_specs=[VMEM],
        out_specs=VMEM,
        compiler_params=LIMIT,
        name="sum",
    )(trace)
    return product, trace.reshape(())


def solution(mesh):
    in_specs = (P(("row", "layer"), "col", None, None, None), P(), P())
    out_specs = (P(("row", "layer"), "col", None, None, None), P())
    return jax.shard_map(body, mesh=mesh, in_specs=in_specs, out_specs=out_specs, check_vma=False)
```

```python
import functools

import jax
import jax.numpy as jnp
from jax import lax
from jax.experimental import pallas as pl
from jax.experimental.pallas import tpu as pltpu
from jax.sharding import PartitionSpec as P

LANES = 128
AXES = ("row", "col", "layer")
LIMIT = pltpu.CompilerParams(vmem_limit_bytes=48 * 2 ** 20)
VMEM = pl.BlockSpec(memory_space=pltpu.VMEM)
UNREAD = pl.BlockSpec(memory_space=pl.ANY)
SMEM = pl.BlockSpec(memory_space=pltpu.SMEM)


def tall_of(size):
    return size * size // LANES


def unpack(block, size):
    tall = block.shape[0]
    spare = LANES - size
    rest = size - tall
    pieces = [block[q * rest:(q + 1) * rest, size:] for q in range(size // spare)]
    pieces.append(jnp.zeros((rest, spare), block.dtype))
    return jnp.concatenate([block, jnp.concatenate(pieces, axis=1)], axis=0)


def parts_of(value):
    parts = []
    for _ in range(3):
        part = value.astype(jnp.bfloat16)
        parts.append(part)
        value = value - part.astype(jnp.float32)
    return parts


def place(sizes):
    n_row, n_col, n_layer = sizes
    per_group = n_row * n_layer // n_col
    pair = lax.axis_index("row") * n_layer + lax.axis_index("layer")
    return pair, lax.axis_index("col"), lax.div(pair, per_group), lax.rem(pair, per_group), per_group


def pack_kernel(x_ref, out_ref):
    rows, _, slots, size, _ = x_ref.shape
    tall = tall_of(size)
    spare = LANES - size
    rest = size - tall
    for i in range(rows):
        for t in range(slots):
            n = i * slots + t
            out_ref[n, :, :size] = x_ref[i, 0, t, :tall, :]
            for q in range(size // spare):
                out_ref[n, q * rest:(q + 1) * rest, size:] = x_ref[i, 0, t, tall:, q * spare:(q + 1) * spare]


def four_by_four(sizes):
    return sizes[0] == 2 and sizes[1] == 4 and sizes[2] == 4


def strip_base(sizes, rows, slots, shares, contracted):
    n_row, n_col, n_layer = sizes
    chips = n_layer // 2
    my_row, my_layer = lax.axis_index("row"), lax.axis_index("layer")
    source = lax.div(contracted, rows)
    source_row, source_layer = lax.div(source, n_layer), lax.rem(source, n_layer)
    share = lax.bitwise_xor(source_row, my_row) * chips + lax.bitwise_xor(lax.div(source_layer, 2), lax.div(my_layer, 2))
    if four_by_four(sizes):
        share = jnp.where((share >= 2) & (lax.axis_index("col") >= 2), 5 - share, share)
    other_core = lax.bitwise_xor(lax.rem(source_layer, 2), lax.rem(my_layer, 2))
    return ((share + other_core * shares) * rows + lax.rem(contracted, rows)) * slots


def stack(share_refs, out_ref):
    for n, ref in enumerate(share_refs):
        out_ref[n * ref.shape[0]:(n + 1) * ref.shape[0]] = ref[...]


def group_at(sizes, here, own_group, values):
    return lax.bitwise_xor(here, jnp.where(own_group >= sizes[1] // 2, values[1], values[0]))


def matched(code_ref, here, contracted, stored, target):
    index, valid = jnp.int32(0), jnp.bool_(False)
    for u in range(code_ref.shape[0]):
        hit = code_ref[u, here, contracted] == target
        index = jnp.where(hit, u, index)
        valid = valid | hit
    return index, valid & stored & (target >= 0)


def mark_kernel(_, out_ref):
    out_ref[...] = jnp.zeros(out_ref.shape, jnp.float32)


def trace_kernel(sizes, rows, size, groups, shares, code_ref, *refs):
    strip_refs, share_refs = refs[:len(groups)], refs[len(groups):len(groups) + 2 * shares]
    total_ref, column_ref = refs[-2:]
    slots = code_ref.shape[0]
    pair, here, own_group, number, per_group = place(sizes)
    width = per_group * rows
    def straight(block):
        return unpack(block, size)[:, :size]

    @pl.when(own_group == here)
    def _():
        stack(share_refs, column_ref)
        total = jnp.zeros((size, size), jnp.float32)
        for i in range(rows):
            row = pair * rows + i
            for strip_ref, (value, value_upper, weight) in zip(strip_refs, groups):
                group = group_at(sizes, here, own_group, (value, value_upper))
                for t in range(slots):
                    column = code_ref[t, group, row]
                    contracted = group * width + jnp.maximum(column, 0)
                    index, valid = matched(code_ref, here, contracted, column >= 0, number * rows + i)
                    block = column_ref[strip_base(sizes, rows, slots, shares, contracted) + index]
                    term = straight(strip_ref[i * slots + t]) * straight(block).T
                    total = total + jnp.where(valid, weight * term, 0.0)
        total_ref[...] = jnp.full(total_ref.shape, jnp.sum(total), jnp.float32)

    @pl.when(own_group != here)
    def _():
        total_ref[...] = jnp.zeros(total_ref.shape, jnp.float32)


def sum_kernel(terms_ref, out_ref):
    out_ref[...] = jnp.sum(terms_ref[...], axis=0)[:, :1]


def product_kernel(sizes, groups, strip_at, share_at, code_ref, *refs):
    count = len(groups)
    strip_refs, share_refs = [refs[n] for n in strip_at], [refs[n] for n in share_at]
    shares = len(share_at) // 2
    out_ref, column_ref, a_ref, *w_refs = refs[-6:]
    rows, _, slots, size, _ = out_ref.shape
    pair, here, own_group, _, per_group = place(sizes)
    width = per_group * rows
    stack(share_refs, column_ref)

    for w_ref in w_refs:
        for j in range(count * slots):
            w_ref[j * LANES + size:(j + 1) * LANES, :] = jnp.zeros((LANES - size, slots * LANES), jnp.bfloat16)
    for i in range(rows):
        row = pair * rows + i
        targets = [code_ref[s, here, row] for s in range(slots)]
        for k, (value, value_upper, _) in enumerate(groups):
            group = group_at(sizes, here, own_group, (value, value_upper))
            for t in range(slots):
                j = k * slots + t
                for n, part in enumerate(parts_of(unpack(strip_refs[k][i * slots + t], size))):
                    a_ref[n * size:(n + 1) * size, j * LANES:(j + 1) * LANES] = part
                column = code_ref[t, group, row]
                contracted = group * width + jnp.maximum(column, 0)
                base = strip_base(sizes, rows, slots, shares, contracted)
                for s in range(slots):
                    index, valid = matched(code_ref, here, contracted, column >= 0, targets[s])
                    block = jnp.where(valid, unpack(column_ref[base + index], size), 0.0)
                    for w_ref, part in zip(w_refs, parts_of(block)):
                        w_ref[j * LANES:j * LANES + size, s * LANES:(s + 1) * LANES] = part

        high, low, least = [
            jnp.dot(a_ref[:(3 - n) * size], w_refs[n][...], preferred_element_type=jnp.float32) for n in range(3)
        ]
        small = low[size:] + (least + high[2 * size:])
        result = high[:size] + ((low[:size] + high[size:2 * size]) + small)
        for s in range(slots):
            out_ref[i, 0, s] = result[:, s * LANES:s * LANES + size]


def exchanged(value, axis, mask):
    return lax.ppermute(value, axis, [(n, n ^ mask) for n in range(lax.axis_size(axis))])


def row_strip(packed, sizes):
    n_row, n_col, n_layer = sizes
    if n_col != 4:
        strip = {0: packed}
        bit = n_col // 2
        while bit:
            for mask in list(strip):
                strip[mask | bit] = exchanged(strip[mask], "col", bit)
            bit //= 2
        return [(strip[m], m, m, 1) for m in sorted(strip)], []
    per_group = n_row * n_layer // n_col
    route = []
    for r in range(n_row):
        for c in range(n_col):
            for y in range(n_layer):
                value = 2 if (r * n_layer + y) // per_group < n_col // 2 else 3
                route.append(((r * n_col + c) * n_layer + y, (r * n_col + (c ^ value)) * n_layer + y))
    far = lax.ppermute(packed, AXES, route)
    return [(packed, 0, 0, 1), (None, 1, 1, 1), (far, 2, 3, 2)], [(exchanged(far, "col", 1), 3, 2, 0)]


def body(blocks, block_cols, occupancy):
    rows, _, slots, size, _ = blocks.shape
    sizes = tuple(lax.axis_size(axis) for axis in AXES)
    n_row, n_col, n_layer = sizes
    chips = n_layer // 2
    tall = tall_of(size)
    code = jnp.where(occupancy == 1, block_cols, -1).transpose((2, 1, 0))

    packed = pl.pallas_call(
        pack_kernel,
        out_shape=jax.ShapeDtypeStruct((rows * slots, tall, LANES), jnp.float32),
        in_specs=[VMEM],
        out_specs=VMEM,
        compiler_params=LIMIT,
        name="pack",
    )(blocks)

    early, late = row_strip(packed, sizes)
    def in_plane(steps):
        route = []
        for a in range(n_row):
            for c in range(n_col):
                for b in range(n_layer):
                    row_bits, chip_bits = steps[c >= n_col // 2]
                    target = ((a ^ row_bits) * n_col + c) * n_layer + (b ^ (2 * chip_bits))
                    route.append(((a * n_col + c) * n_layer + b, target))
        return lax.ppermute(packed, AXES, route)

    if four_by_four(sizes):
        mine = [packed, in_plane([(0, 1)] * 2), in_plane([(1, 0), (1, 1)]), in_plane([(1, 1), (1, 0)])]
        needed = 3
    else:
        mine = [packed] + [in_plane([(n // chips, n % chips)] * 2) for n in range(1, n_row * chips)]
        needed = len(mine)
    early = [(exchanged(packed, "col", 1) if share is None else share, *rest) for share, *rest in early]
    others = [exchanged(share, "layer", 1) for share in mine]

    def column(count):
        return jax.ShapeDtypeStruct((2 * count * rows * slots, tall, LANES), jnp.float32)

    far = [share for share, value, _, _ in early if value > 1]
    marks = [
        pl.pallas_call(
            mark_kernel,
            out_shape=jax.ShapeDtypeStruct((8, LANES), jnp.float32),
            in_specs=[UNREAD],
            out_specs=VMEM,
            cost_estimate=pl.CostEstimate(flops=int(5e+09), bytes_accessed=0, transcendentals=0),
            compiler_params=LIMIT,
            name="mark",
        )(share)
        for share in far
    ]
    trace = pl.pallas_call(
        functools.partial(trace_kernel, sizes, rows, size, [tuple(rest) for _, *rest in early], needed),
        out_shape=jax.ShapeDtypeStruct((n_row * n_col * n_layer, 1, LANES), jnp.float32),
        in_specs=[SMEM] + [VMEM] * (len(early) + 2 * needed) + [UNREAD] * len(marks),
        out_specs=VMEM,
        scratch_shapes=[pltpu.VMEM(column(needed).shape, jnp.float32)],
        compiler_params=LIMIT,
        name="trace_terms",
    )(code, *[share for share, *_ in early], *mine[:needed], *others[:needed], *marks)
    trace = lax.all_to_all(trace, AXES, 0, 0, tiled=True)

    strip = early + late
    inner = len(strip) * slots * LANES
    near = [share for share, value, _, _ in early if value == 1]
    operands = far + mine + near + [share for share, *_ in late] + others

    def at(share):
        return next(n for n, operand in enumerate(operands) if operand is share)

    strip_at, share_at = [at(share) for share, *_ in strip], [at(share) for share in mine + others]
    product = pl.pallas_call(
        functools.partial(product_kernel, sizes, [tuple(rest) for _, *rest in strip], strip_at, share_at),
        out_shape=jax.ShapeDtypeStruct(blocks.shape, jnp.float32),
        in_specs=[SMEM] + [VMEM] * len(operands),
        out_specs=VMEM,
        scratch_shapes=[
            pltpu.VMEM(column(len(mine)).shape, jnp.float32),
            pltpu.VMEM((3 * size, inner), jnp.bfloat16),
        ]
        + [pltpu.VMEM((inner, slots * LANES), jnp.bfloat16)] * 3,
        compiler_params=LIMIT,
        name="multiply",
    )(code, *operands)
    trace = pl.pallas_call(
        sum_kernel,
        out_shape=jax.ShapeDtypeStruct((1, 1), jnp.float32),
        in_specs=[VMEM],
        out_specs=VMEM,
        compiler_params=LIMIT,
        name="sum",
    )(trace)
    return product, trace.reshape(())


def solution(mesh):
    in_specs = (P(("row", "layer"), "col", None, None, None), P(), P())
    out_specs = (P(("row", "layer"), "col", None, None, None), P())
    return jax.shard_map(body, mesh=mesh, in_specs=in_specs, out_specs=out_specs, check_vma=False)
```

```python
import functools

import jax
import jax.numpy as jnp
from jax import lax
from jax.experimental import pallas as pl
from jax.experimental.pallas import tpu as pltpu
from jax.sharding import PartitionSpec as P

LANES = 128
AXES = ("row", "col", "layer")
LIMIT = pltpu.CompilerParams(vmem_limit_bytes=48 * 2 ** 20)
VMEM = pl.BlockSpec(memory_space=pltpu.VMEM)
UNREAD = pl.BlockSpec(memory_space=pl.ANY)
SMEM = pl.BlockSpec(memory_space=pltpu.SMEM)


def tall_of(size):
    return size * size // LANES


def unpack(block, size):
    tall = block.shape[0]
    spare = LANES - size
    rest = size - tall
    pieces = [block[q * rest:(q + 1) * rest, size:] for q in range(size // spare)]
    pieces.append(jnp.zeros((rest, spare), block.dtype))
    return jnp.concatenate([block, jnp.concatenate(pieces, axis=1)], axis=0)


def parts_of(value):
    parts = []
    for _ in range(3):
        part = value.astype(jnp.bfloat16)
        parts.append(part)
        value = value - part.astype(jnp.float32)
    return parts


def place(sizes):
    n_row, n_col, n_layer = sizes
    per_group = n_row * n_layer // n_col
    pair = lax.axis_index("row") * n_layer + lax.axis_index("layer")
    return pair, lax.axis_index("col"), lax.div(pair, per_group), lax.rem(pair, per_group), per_group


def pack_kernel(x_ref, out_ref):
    rows, _, slots, size, _ = x_ref.shape
    tall = tall_of(size)
    spare = LANES - size
    rest = size - tall
    for i in range(rows):
        for t in range(slots):
            n = i * slots + t
            out_ref[n, :, :size] = x_ref[i, 0, t, :tall, :]
            for q in range(size // spare):
                out_ref[n, q * rest:(q + 1) * rest, size:] = x_ref[i, 0, t, tall:, q * spare:(q + 1) * spare]


def four_by_four(sizes):
    return sizes[0] == 2 and sizes[1] == 4 and sizes[2] == 4


def strip_base(sizes, rows, slots, shares, contracted):
    n_row, n_col, n_layer = sizes
    chips = n_layer // 2
    my_row, my_layer = lax.axis_index("row"), lax.axis_index("layer")
    source = lax.div(contracted, rows)
    source_row, source_layer = lax.div(source, n_layer), lax.rem(source, n_layer)
    share = lax.bitwise_xor(source_row, my_row) * chips + lax.bitwise_xor(lax.div(source_layer, 2), lax.div(my_layer, 2))
    if four_by_four(sizes):
        share = jnp.where((share >= 2) & (lax.axis_index("col") >= 2), 5 - share, share)
    other_core = lax.bitwise_xor(lax.rem(source_layer, 2), lax.rem(my_layer, 2))
    return ((share + other_core * shares) * rows + lax.rem(contracted, rows)) * slots


def stack(share_refs, out_ref):
    first = 0
    for ref in share_refs:
        for part in [ref] if len(ref.shape) == 3 else [ref.at[n] for n in range(ref.shape[0])]:
            out_ref[first:first + part.shape[0]] = part[...]
            first += part.shape[0]


def group_at(sizes, here, own_group, values):
    return lax.bitwise_xor(here, jnp.where(own_group >= sizes[1] // 2, values[1], values[0]))


def matched(code_ref, here, contracted, stored, target):
    index, valid = jnp.int32(0), jnp.bool_(False)
    for u in range(code_ref.shape[0]):
        hit = code_ref[u, here, contracted] == target
        index = jnp.where(hit, u, index)
        valid = valid | hit
    return index, valid & stored & (target >= 0)


def copy_kernel(x_ref, _, out_ref):
    out_ref[...] = x_ref[...]


def pair_kernel(x_ref, y_ref, out_ref):
    out_ref[0] = x_ref[...]
    out_ref[1] = y_ref[...]


def mark_kernel(_, out_ref):
    out_ref[...] = jnp.zeros(out_ref.shape, jnp.float32)


def trace_kernel(sizes, rows, size, groups, shares, code_ref, *refs):
    strip_refs, share_refs = refs[:len(groups)], refs[len(groups):len(groups) + 2 * shares - 1]
    total_ref, column_ref = refs[-2:]
    slots = code_ref.shape[0]
    pair, here, own_group, number, per_group = place(sizes)
    width = per_group * rows
    def straight(block):
        return unpack(block, size)[:, :size]

    @pl.when(own_group == here)
    def _():
        stack(share_refs, column_ref)
        total = jnp.zeros((size, size), jnp.float32)
        for i in range(rows):
            row = pair * rows + i
            for strip_ref, (value, value_upper, weight) in zip(strip_refs, groups):
                group = group_at(sizes, here, own_group, (value, value_upper))
                for t in range(slots):
                    column = code_ref[t, group, row]
                    contracted = group * width + jnp.maximum(column, 0)
                    index, valid = matched(code_ref, here, contracted, column >= 0, number * rows + i)
                    block = column_ref[strip_base(sizes, rows, slots, shares, contracted) + index]
                    term = straight(strip_ref[i * slots + t]) * straight(block).T
                    total = total + jnp.where(valid, weight * term, 0.0)
        total_ref[...] = jnp.full(total_ref.shape, jnp.sum(total), jnp.float32)

    @pl.when(own_group != here)
    def _():
        total_ref[...] = jnp.zeros(total_ref.shape, jnp.float32)


def sum_kernel(terms_ref, out_ref):
    out_ref[...] = jnp.sum(terms_ref[...], axis=0)[:, :1]


def product_kernel(sizes, groups, strip_at, share_at, code_ref, *refs):
    count = len(groups)
    strip_refs, share_refs = [refs[n] for n in strip_at], [refs[n] for n in share_at]
    shares = (len(share_at) + 1) // 2
    out_ref, column_ref, a_ref, *w_refs = refs[-6:]
    rows, _, slots, size, _ = out_ref.shape
    pair, here, own_group, _, per_group = place(sizes)
    width = per_group * rows
    stack(share_refs, column_ref)

    for w_ref in w_refs:
        for j in range(count * slots):
            w_ref[j * LANES + size:(j + 1) * LANES, :] = jnp.zeros((LANES - size, slots * LANES), jnp.bfloat16)
    for i in range(rows):
        row = pair * rows + i
        targets = [code_ref[s, here, row] for s in range(slots)]
        for k, (value, value_upper, _) in enumerate(groups):
            group = group_at(sizes, here, own_group, (value, value_upper))
            for t in range(slots):
                j = k * slots + t
                for n, part in enumerate(parts_of(unpack(strip_refs[k][i * slots + t], size))):
                    a_ref[n * size:(n + 1) * size, j * LANES:(j + 1) * LANES] = part
                column = code_ref[t, group, row]
                contracted = group * width + jnp.maximum(column, 0)
                base = strip_base(sizes, rows, slots, shares, contracted)
                for s in range(slots):
                    index, valid = matched(code_ref, here, contracted, column >= 0, targets[s])
                    block = jnp.where(valid, unpack(column_ref[base + index], size), 0.0)
                    for w_ref, part in zip(w_refs, parts_of(block)):
                        w_ref[j * LANES:j * LANES + size, s * LANES:(s + 1) * LANES] = part

        high, low, least = [
            jnp.dot(a_ref[:(3 - n) * size], w_refs[n][...], preferred_element_type=jnp.float32) for n in range(3)
        ]
        small = low[size:] + (least + high[2 * size:])
        result = high[:size] + ((low[:size] + high[size:2 * size]) + small)
        for s in range(slots):
            out_ref[i, 0, s] = result[:, s * LANES:s * LANES + size]


def exchanged(value, axis, mask):
    return lax.ppermute(value, axis, [(n, n ^ mask) for n in range(lax.axis_size(axis))])


def row_strip(packed, sizes):
    n_row, n_col, n_layer = sizes
    if n_col != 4:
        strip = {0: packed}
        bit = n_col // 2
        while bit:
            for mask in list(strip):
                strip[mask | bit] = exchanged(strip[mask], "col", bit)
            bit //= 2
        return [(strip[m], m, m, 1) for m in sorted(strip)], []
    per_group = n_row * n_layer // n_col
    route = []
    for r in range(n_row):
        for c in range(n_col):
            for y in range(n_layer):
                value = 2 if (r * n_layer + y) // per_group < n_col // 2 else 3
                route.append(((r * n_col + c) * n_layer + y, (r * n_col + (c ^ value)) * n_layer + y))
    far = lax.ppermute(packed, AXES, route)
    return [(packed, 0, 0, 1), (None, 1, 1, 1), (far, 2, 3, 2)], [(exchanged(far, "col", 1), 3, 2, 0)]


def body(blocks, block_cols, occupancy):
    rows, _, slots, size, _ = blocks.shape
    sizes = tuple(lax.axis_size(axis) for axis in AXES)
    n_row, n_col, n_layer = sizes
    chips = n_layer // 2
    tall = tall_of(size)
    code = jnp.where(occupancy == 1, block_cols, -1).transpose((2, 1, 0))

    packed = pl.pallas_call(
        pack_kernel,
        out_shape=jax.ShapeDtypeStruct((rows * slots, tall, LANES), jnp.float32),
        in_specs=[VMEM],
        out_specs=VMEM,
        compiler_params=LIMIT,
        name="pack",
    )(blocks)

    early, late = row_strip(packed, sizes)
    def in_plane(steps):
        route = []
        for a in range(n_row):
            for c in range(n_col):
                for b in range(n_layer):
                    row_bits, chip_bits = steps[c >= n_col // 2]
                    target = ((a ^ row_bits) * n_col + c) * n_layer + (b ^ (2 * chip_bits))
                    route.append(((a * n_col + c) * n_layer + b, target))
        return lax.ppermute(packed, AXES, route)

    if four_by_four(sizes):
        mine = [packed, in_plane([(0, 1)] * 2), in_plane([(1, 0), (1, 1)]), in_plane([(1, 1), (1, 0)])]
        needed = 3
    else:
        mine = [packed] + [in_plane([(n // chips, n % chips)] * 2) for n in range(1, n_row * chips)]
        needed = len(mine)
    early = [(exchanged(packed, "col", 1) if share is None else share, *rest) for share, *rest in early]
    both = pl.pallas_call(
        pair_kernel,
        out_shape=jax.ShapeDtypeStruct((2,) + packed.shape, jnp.float32),
        in_specs=[VMEM, VMEM],
        out_specs=VMEM,
        compiler_params=LIMIT,
        name="pair",
    )(*mine[:2])
    others = [exchanged(both, "layer", 1)] + [exchanged(share, "layer", 1) for share in mine[2:needed]]

    def column(count):
        return jax.ShapeDtypeStruct((2 * count * rows * slots, tall, LANES), jnp.float32)

    far = [share for share, value, _, _ in early if value > 1]
    marks = [
        pl.pallas_call(
            mark_kernel,
            out_shape=jax.ShapeDtypeStruct((8, LANES), jnp.float32),
            in_specs=[UNREAD],
            out_specs=VMEM,
            cost_estimate=pl.CostEstimate(flops=int(5e+09), bytes_accessed=0, transcendentals=0),
            compiler_params=LIMIT,
            name="mark",
        )(share)
        for share in far
    ]
    trace = pl.pallas_call(
        functools.partial(trace_kernel, sizes, rows, size, [tuple(rest) for _, *rest in early], needed),
        out_shape=jax.ShapeDtypeStruct((n_row * n_col * n_layer, 1, LANES), jnp.float32),
        in_specs=[SMEM] + [VMEM] * (len(early) + 2 * needed - 1) + [UNREAD] * len(marks),
        out_specs=VMEM,
        scratch_shapes=[pltpu.VMEM(column(needed).shape, jnp.float32)],
        compiler_params=LIMIT,
        name="trace_terms",
    )(code, *[share for share, *_ in early], *mine[:needed], *others[:needed - 1], *marks)
    for share in mine[needed:]:
        held = pl.pallas_call(
            copy_kernel,
            out_shape=jax.ShapeDtypeStruct(share.shape, jnp.float32),
            in_specs=[VMEM, UNREAD],
            out_specs=VMEM,
            compiler_params=LIMIT,
            name="copy",
        )(share, trace)
        others.append(exchanged(held, "layer", 1))
    trace = lax.all_to_all(trace, AXES, 0, 0, tiled=True)

    strip = early + late
    inner = len(strip) * slots * LANES
    near = [share for share, value, _, _ in early if value == 1]
    operands = mine[::-1] + near + far + [share for share, *_ in late] + others

    def at(share):
        return next(n for n, operand in enumerate(operands) if operand is share)

    strip_at, share_at = [at(share) for share, *_ in strip], [at(share) for share in mine + others]
    product = pl.pallas_call(
        functools.partial(product_kernel, sizes, [tuple(rest) for _, *rest in strip], strip_at, share_at),
        out_shape=jax.ShapeDtypeStruct(blocks.shape, jnp.float32),
        in_specs=[SMEM] + [VMEM] * len(operands),
        out_specs=VMEM,
        scratch_shapes=[
            pltpu.VMEM(column(len(mine)).shape, jnp.float32),
            pltpu.VMEM((3 * size, inner), jnp.bfloat16),
        ]
        + [pltpu.VMEM((inner, slots * LANES), jnp.bfloat16)] * 3,
        compiler_params=LIMIT,
        name="multiply",
    )(code, *operands)
    trace = pl.pallas_call(
        sum_kernel,
        out_shape=jax.ShapeDtypeStruct((1, 1), jnp.float32),
        in_specs=[VMEM],
        out_specs=VMEM,
        compiler_params=LIMIT,
        name="sum",
    )(trace)
    return product, trace.reshape(())


def solution(mesh):
    in_specs = (P(("row", "layer"), "col", None, None, None), P(), P())
    out_specs = (P(("row", "layer"), "col", None, None, None), P())
    return jax.shard_map(body, mesh=mesh, in_specs=in_specs, out_specs=out_specs, check_vma=False)
```

```python
import functools

import jax
import jax.numpy as jnp
from jax import lax
from jax.experimental import pallas as pl
from jax.experimental.pallas import tpu as pltpu
from jax.sharding import PartitionSpec as P

LANES = 128
AXES = ("row", "col", "layer")
LIMIT = pltpu.CompilerParams(vmem_limit_bytes=48 * 2 ** 20)
VMEM = pl.BlockSpec(memory_space=pltpu.VMEM)
UNREAD = pl.BlockSpec(memory_space=pl.ANY)
SMEM = pl.BlockSpec(memory_space=pltpu.SMEM)


def tall_of(size):
    return size * size // LANES


def unpack(block, size):
    tall = block.shape[0]
    spare = LANES - size
    rest = size - tall
    pieces = [block[q * rest:(q + 1) * rest, size:] for q in range(size // spare)]
    pieces.append(jnp.zeros((rest, spare), block.dtype))
    return jnp.concatenate([block, jnp.concatenate(pieces, axis=1)], axis=0)


def parts_of(value):
    parts = []
    for _ in range(3):
        part = value.astype(jnp.bfloat16)
        parts.append(part)
        value = value - part.astype(jnp.float32)
    return parts


def place(sizes):
    n_row, n_col, n_layer = sizes
    per_group = n_row * n_layer // n_col
    pair = lax.axis_index("row") * n_layer + lax.axis_index("layer")
    return pair, lax.axis_index("col"), lax.div(pair, per_group), lax.rem(pair, per_group), per_group


def pack_kernel(x_ref, out_ref):
    rows, _, slots, size, _ = x_ref.shape
    tall = tall_of(size)
    spare = LANES - size
    rest = size - tall
    for i in range(rows):
        for t in range(slots):
            n = i * slots + t
            out_ref[n, :, :size] = x_ref[i, 0, t, :tall, :]
            for q in range(size // spare):
                out_ref[n, q * rest:(q + 1) * rest, size:] = x_ref[i, 0, t, tall:, q * spare:(q + 1) * spare]


def four_by_four(sizes):
    return sizes[0] == 2 and sizes[1] == 4 and sizes[2] == 4


def strip_base(sizes, rows, slots, shares, contracted):
    n_row, n_col, n_layer = sizes
    chips = n_layer // 2
    my_row, my_layer = lax.axis_index("row"), lax.axis_index("layer")
    source = lax.div(contracted, rows)
    source_row, source_layer = lax.div(source, n_layer), lax.rem(source, n_layer)
    share = lax.bitwise_xor(source_row, my_row) * chips + lax.bitwise_xor(lax.div(source_layer, 2), lax.div(my_layer, 2))
    if four_by_four(sizes):
        share = jnp.where((share >= 2) & (lax.axis_index("col") >= 2), 5 - share, share)
    other_core = lax.bitwise_xor(lax.rem(source_layer, 2), lax.rem(my_layer, 2))
    return ((share + other_core * shares) * rows + lax.rem(contracted, rows)) * slots


def stack(share_refs, out_ref):
    first = 0
    for ref in share_refs:
        for part in [ref] if len(ref.shape) == 3 else [ref.at[n] for n in range(ref.shape[0])]:
            out_ref[first:first + part.shape[0]] = part[...]
            first += part.shape[0]


def group_at(sizes, here, own_group, values):
    return lax.bitwise_xor(here, jnp.where(own_group >= sizes[1] // 2, values[1], values[0]))


def matched(code_ref, here, contracted, stored, target):
    index, valid = jnp.int32(0), jnp.bool_(False)
    for u in range(code_ref.shape[0]):
        hit = code_ref[u, here, contracted] == target
        index = jnp.where(hit, u, index)
        valid = valid | hit
    return index, valid & stored & (target >= 0)


def copy_kernel(x_ref, _, out_ref):
    out_ref[...] = x_ref[...]


def pair_kernel(x_ref, y_ref, out_ref):
    out_ref[0] = x_ref[...]
    out_ref[1] = y_ref[...]


def mark_kernel(_, out_ref):
    out_ref[...] = jnp.zeros(out_ref.shape, jnp.float32)


def trace_kernel(sizes, rows, size, groups, shares, code_ref, *refs):
    strip_refs, share_refs = refs[:len(groups)], refs[len(groups):len(groups) + 2 * shares - 1]
    total_ref, column_ref = refs[-2:]
    slots = code_ref.shape[0]
    pair, here, own_group, number, per_group = place(sizes)
    width = per_group * rows
    def straight(block):
        return unpack(block, size)[:, :size]

    @pl.when(own_group == here)
    def _():
        stack(share_refs, column_ref)
        total = jnp.zeros((size, size), jnp.float32)
        for i in range(rows):
            row = pair * rows + i
            for strip_ref, (value, value_upper, weight) in zip(strip_refs, groups):
                group = group_at(sizes, here, own_group, (value, value_upper))
                for t in range(slots):
                    column = code_ref[t, group, row]
                    contracted = group * width + jnp.maximum(column, 0)
                    index, valid = matched(code_ref, here, contracted, column >= 0, number * rows + i)
                    block = column_ref[strip_base(sizes, rows, slots, shares, contracted) + index]
                    term = straight(strip_ref[i * slots + t]) * straight(block).T
                    total = total + jnp.where(valid, weight * term, 0.0)
        total_ref[...] = jnp.full(total_ref.shape, jnp.sum(total), jnp.float32)

    @pl.when(own_group != here)
    def _():
        total_ref[...] = jnp.zeros(total_ref.shape, jnp.float32)


def sum_kernel(terms_ref, _, out_ref):
    out_ref[...] = jnp.sum(terms_ref[...], axis=0)[:, :1]


def product_kernel(sizes, groups, strip_at, share_at, code_ref, *refs):
    count = len(groups)
    strip_refs, share_refs = [refs[n] for n in strip_at], [refs[n] for n in share_at]
    shares = (len(share_at) + 1) // 2
    out_ref, column_ref, a_ref, *w_refs = refs[-6:]
    rows, _, slots, size, _ = out_ref.shape
    pair, here, own_group, _, per_group = place(sizes)
    width = per_group * rows
    stack(share_refs, column_ref)

    for w_ref in w_refs:
        for j in range(count * slots):
            w_ref[j * LANES + size:(j + 1) * LANES, :] = jnp.zeros((LANES - size, slots * LANES), jnp.bfloat16)
    for i in range(rows):
        row = pair * rows + i
        targets = [code_ref[s, here, row] for s in range(slots)]
        for k, (value, value_upper, _) in enumerate(groups):
            group = group_at(sizes, here, own_group, (value, value_upper))
            for t in range(slots):
                j = k * slots + t
                for n, part in enumerate(parts_of(unpack(strip_refs[k][i * slots + t], size))):
                    a_ref[n * size:(n + 1) * size, j * LANES:(j + 1) * LANES] = part
                column = code_ref[t, group, row]
                contracted = group * width + jnp.maximum(column, 0)
                base = strip_base(sizes, rows, slots, shares, contracted)
                for s in range(slots):
                    index, valid = matched(code_ref, here, contracted, column >= 0, targets[s])
                    block = jnp.where(valid, unpack(column_ref[base + index], size), 0.0)
                    for w_ref, part in zip(w_refs, parts_of(block)):
                        w_ref[j * LANES:j * LANES + size, s * LANES:(s + 1) * LANES] = part

        high, low, least = [
            jnp.dot(a_ref[:(3 - n) * size], w_refs[n][...], preferred_element_type=jnp.float32) for n in range(3)
        ]
        small = low[size:] + (least + high[2 * size:])
        result = high[:size] + ((low[:size] + high[size:2 * size]) + small)
        for s in range(slots):
            out_ref[i, 0, s] = result[:, s * LANES:s * LANES + size]


def exchanged(value, axis, mask):
    return lax.ppermute(value, axis, [(n, n ^ mask) for n in range(lax.axis_size(axis))])


def row_strip(packed, sizes):
    n_row, n_col, n_layer = sizes
    if n_col != 4:
        strip = {0: packed}
        bit = n_col // 2
        while bit:
            for mask in list(strip):
                strip[mask | bit] = exchanged(strip[mask], "col", bit)
            bit //= 2
        return [(strip[m], m, m, 1) for m in sorted(strip)], []
    per_group = n_row * n_layer // n_col
    route = []
    for r in range(n_row):
        for c in range(n_col):
            for y in range(n_layer):
                value = 2 if (r * n_layer + y) // per_group < n_col // 2 else 3
                route.append(((r * n_col + c) * n_layer + y, (r * n_col + (c ^ value)) * n_layer + y))
    far = lax.ppermute(packed, AXES, route)
    return [(packed, 0, 0, 1), (None, 1, 1, 1), (far, 2, 3, 2)], [(exchanged(far, "col", 1), 3, 2, 0)]


def body(blocks, block_cols, occupancy):
    rows, _, slots, size, _ = blocks.shape
    sizes = tuple(lax.axis_size(axis) for axis in AXES)
    n_row, n_col, n_layer = sizes
    chips = n_layer // 2
    tall = tall_of(size)
    code = jnp.where(occupancy == 1, block_cols, -1).transpose((2, 1, 0))

    packed = pl.pallas_call(
        pack_kernel,
        out_shape=jax.ShapeDtypeStruct((rows * slots, tall, LANES), jnp.float32),
        in_specs=[VMEM],
        out_specs=VMEM,
        compiler_params=LIMIT,
        name="pack",
    )(blocks)

    early, late = row_strip(packed, sizes)
    def in_plane(steps):
        route = []
        for a in range(n_row):
            for c in range(n_col):
                for b in range(n_layer):
                    row_bits, chip_bits = steps[c >= n_col // 2]
                    target = ((a ^ row_bits) * n_col + c) * n_layer + (b ^ (2 * chip_bits))
                    route.append(((a * n_col + c) * n_layer + b, target))
        return lax.ppermute(packed, AXES, route)

    if four_by_four(sizes):
        mine = [packed, in_plane([(0, 1)] * 2), in_plane([(1, 0), (1, 1)]), in_plane([(1, 1), (1, 0)])]
        needed = 3
    else:
        mine = [packed] + [in_plane([(n // chips, n % chips)] * 2) for n in range(1, n_row * chips)]
        needed = len(mine)
    early = [(exchanged(packed, "col", 1) if share is None else share, *rest) for share, *rest in early]
    both = pl.pallas_call(
        pair_kernel,
        out_shape=jax.ShapeDtypeStruct((2,) + packed.shape, jnp.float32),
        in_specs=[VMEM, VMEM],
        out_specs=VMEM,
        compiler_params=LIMIT,
        name="pair",
    )(*mine[:2])
    others = [exchanged(both, "layer", 1)] + [exchanged(share, "layer", 1) for share in mine[2:needed]]

    def column(count):
        return jax.ShapeDtypeStruct((2 * count * rows * slots, tall, LANES), jnp.float32)

    far = [share for share, value, _, _ in early if value > 1]
    marks = [
        pl.pallas_call(
            mark_kernel,
            out_shape=jax.ShapeDtypeStruct((8, LANES), jnp.float32),
            in_specs=[UNREAD],
            out_specs=VMEM,
            cost_estimate=pl.CostEstimate(flops=int(5e+09), bytes_accessed=0, transcendentals=0),
            compiler_params=LIMIT,
            name="mark",
        )(share)
        for share in far
    ]
    trace = pl.pallas_call(
        functools.partial(trace_kernel, sizes, rows, size, [tuple(rest) for _, *rest in early], needed),
        out_shape=jax.ShapeDtypeStruct((n_row * n_col * n_layer, 1, LANES), jnp.float32),
        in_specs=[SMEM] + [VMEM] * (len(early) + 2 * needed - 1) + [UNREAD] * len(marks),
        out_specs=VMEM,
        scratch_shapes=[pltpu.VMEM(column(needed).shape, jnp.float32)],
        compiler_params=LIMIT,
        name="trace_terms",
    )(code, *[share for share, *_ in early], *mine[:needed], *others[:needed - 1], *marks)
    for share in mine[needed:]:
        held = pl.pallas_call(
            copy_kernel,
            out_shape=jax.ShapeDtypeStruct(share.shape, jnp.float32),
            in_specs=[VMEM, UNREAD],
            out_specs=VMEM,
            compiler_params=LIMIT,
            name="copy",
        )(share, trace)
        others.append(exchanged(held, "layer", 1))
    trace = lax.all_to_all(trace, AXES, 0, 0, tiled=True)

    strip = early + late
    inner = len(strip) * slots * LANES
    near = [share for share, value, _, _ in early if value == 1]
    operands = mine[::-1] + near + far + [share for share, *_ in late] + others

    def at(share):
        return next(n for n, operand in enumerate(operands) if operand is share)

    strip_at, share_at = [at(share) for share, *_ in strip], [at(share) for share in mine + others]
    product = pl.pallas_call(
        functools.partial(product_kernel, sizes, [tuple(rest) for _, *rest in strip], strip_at, share_at),
        out_shape=jax.ShapeDtypeStruct(blocks.shape, jnp.float32),
        in_specs=[SMEM] + [VMEM] * len(operands),
        out_specs=VMEM,
        scratch_shapes=[
            pltpu.VMEM(column(len(mine)).shape, jnp.float32),
            pltpu.VMEM((3 * size, inner), jnp.bfloat16),
        ]
        + [pltpu.VMEM((inner, slots * LANES), jnp.bfloat16)] * 3,
        compiler_params=LIMIT,
        name="multiply",
    )(code, *operands)
    trace = pl.pallas_call(
        sum_kernel,
        out_shape=jax.ShapeDtypeStruct((1, 1), jnp.float32),
        in_specs=[VMEM, UNREAD],
        out_specs=VMEM,
        compiler_params=LIMIT,
        name="sum",
    )(trace, product)
    return product, trace.reshape(())


def solution(mesh):
    in_specs = (P(("row", "layer"), "col", None, None, None), P(), P())
    out_specs = (P(("row", "layer"), "col", None, None, None), P())
    return jax.shard_map(body, mesh=mesh, in_specs=in_specs, out_specs=out_specs, check_vma=False)
```

```python
import functools

import jax
import jax.numpy as jnp
from jax import lax
from jax.experimental import pallas as pl
from jax.experimental.pallas import tpu as pltpu
from jax.sharding import PartitionSpec as P

LANES = 128
AXES = ("row", "col", "layer")
LIMIT = pltpu.CompilerParams(vmem_limit_bytes=48 * 2 ** 20)
VMEM = pl.BlockSpec(memory_space=pltpu.VMEM)
UNREAD = pl.BlockSpec(memory_space=pl.ANY)
SMEM = pl.BlockSpec(memory_space=pltpu.SMEM)


def tall_of(size):
    return size * size // LANES


def unpack(block, size):
    tall = block.shape[0]
    spare = LANES - size
    rest = size - tall
    pieces = [block[q * rest:(q + 1) * rest, size:] for q in range(size // spare)]
    pieces.append(jnp.zeros((rest, spare), block.dtype))
    return jnp.concatenate([block, jnp.concatenate(pieces, axis=1)], axis=0)


def parts_of(value):
    parts = []
    for _ in range(3):
        part = value.astype(jnp.bfloat16)
        parts.append(part)
        value = value - part.astype(jnp.float32)
    return parts


def place(sizes):
    n_row, n_col, n_layer = sizes
    per_group = n_row * n_layer // n_col
    pair = lax.axis_index("row") * n_layer + lax.axis_index("layer")
    return pair, lax.axis_index("col"), lax.div(pair, per_group), lax.rem(pair, per_group), per_group


def pack_kernel(x_ref, out_ref):
    rows, _, slots, size, _ = x_ref.shape
    tall = tall_of(size)
    spare = LANES - size
    rest = size - tall
    for i in range(rows):
        for t in range(slots):
            n = i * slots + t
            out_ref[n, :, :size] = x_ref[i, 0, t, :tall, :]
            for q in range(size // spare):
                out_ref[n, q * rest:(q + 1) * rest, size:] = x_ref[i, 0, t, tall:, q * spare:(q + 1) * spare]


def four_by_four(sizes):
    return sizes[0] == 2 and sizes[1] == 4 and sizes[2] == 4


def strip_base(sizes, rows, slots, shares, contracted):
    n_row, n_col, n_layer = sizes
    chips = n_layer // 2
    my_row, my_layer = lax.axis_index("row"), lax.axis_index("layer")
    source = lax.div(contracted, rows)
    source_row, source_layer = lax.div(source, n_layer), lax.rem(source, n_layer)
    share = lax.bitwise_xor(source_row, my_row) * chips + lax.bitwise_xor(lax.div(source_layer, 2), lax.div(my_layer, 2))
    if four_by_four(sizes):
        share = jnp.where((share >= 2) & (lax.axis_index("col") >= 2), 5 - share, share)
    other_core = lax.bitwise_xor(lax.rem(source_layer, 2), lax.rem(my_layer, 2))
    return ((share + other_core * shares) * rows + lax.rem(contracted, rows)) * slots


def stack(share_refs, out_ref):
    first = 0
    for ref in share_refs:
        for part in [ref] if len(ref.shape) == 3 else [ref.at[n] for n in range(ref.shape[0])]:
            out_ref[first:first + part.shape[0]] = part[...]
            first += part.shape[0]


def group_at(sizes, here, own_group, values):
    return lax.bitwise_xor(here, jnp.where(own_group >= sizes[1] // 2, values[1], values[0]))


def matched(code_ref, here, contracted, stored, target):
    index, valid = jnp.int32(0), jnp.bool_(False)
    for u in range(code_ref.shape[0]):
        hit = code_ref[u, here, contracted] == target
        index = jnp.where(hit, u, index)
        valid = valid | hit
    return index, valid & stored & (target >= 0)


def copy_kernel(x_ref, _, out_ref):
    out_ref[...] = x_ref[...]


def pair_kernel(x_ref, y_ref, out_ref):
    out_ref[0] = x_ref[...]
    out_ref[1] = y_ref[...]


def mark_kernel(_, out_ref):
    out_ref[...] = jnp.zeros(out_ref.shape, jnp.float32)


def trace_kernel(sizes, rows, size, groups, shares, code_ref, *refs):
    strip_refs, share_refs = refs[:len(groups)], refs[len(groups):len(groups) + 2 * shares - 1]
    total_ref, column_ref = refs[-2:]
    slots = code_ref.shape[0]
    pair, here, own_group, number, per_group = place(sizes)
    width = per_group * rows
    def straight(block):
        return unpack(block, size)[:, :size]

    @pl.when(own_group == here)
    def _():
        stack(share_refs, column_ref)
        total = jnp.zeros((size, size), jnp.float32)
        for i in range(rows):
            row = pair * rows + i
            for strip_ref, (value, value_upper, weight) in zip(strip_refs, groups):
                group = group_at(sizes, here, own_group, (value, value_upper))
                for t in range(slots):
                    column = code_ref[t, group, row]
                    contracted = group * width + jnp.maximum(column, 0)
                    index, valid = matched(code_ref, here, contracted, column >= 0, number * rows + i)
                    block = column_ref[strip_base(sizes, rows, slots, shares, contracted) + index]
                    term = straight(strip_ref[i * slots + t]) * straight(block).T
                    total = total + jnp.where(valid, weight * term, 0.0)
        total_ref[...] = jnp.full(total_ref.shape, jnp.sum(total), jnp.float32)

    @pl.when(own_group != here)
    def _():
        total_ref[...] = jnp.zeros(total_ref.shape, jnp.float32)


def sum_kernel(terms_ref, _, out_ref):
    out_ref[...] = jnp.sum(terms_ref[...], axis=0)[:, :1]


def product_kernel(sizes, groups, strip_at, share_at, code_ref, *refs):
    count = len(groups)
    strip_refs, share_refs = [refs[n] for n in strip_at], [refs[n] for n in share_at]
    shares = (len(share_at) + 1) // 2
    out_ref, end_ref, column_ref, a_ref, *w_refs = refs[-7:]
    end_ref[...] = jnp.zeros(end_ref.shape, jnp.float32)
    rows, _, slots, size, _ = out_ref.shape
    pair, here, own_group, _, per_group = place(sizes)
    width = per_group * rows
    stack(share_refs, column_ref)

    for w_ref in w_refs:
        for j in range(count * slots):
            w_ref[j * LANES + size:(j + 1) * LANES, :] = jnp.zeros((LANES - size, slots * LANES), jnp.bfloat16)
    for i in range(rows):
        row = pair * rows + i
        targets = [code_ref[s, here, row] for s in range(slots)]
        for k, (value, value_upper, _) in enumerate(groups):
            group = group_at(sizes, here, own_group, (value, value_upper))
            for t in range(slots):
                j = k * slots + t
                for n, part in enumerate(parts_of(unpack(strip_refs[k][i * slots + t], size))):
                    a_ref[n * size:(n + 1) * size, j * LANES:(j + 1) * LANES] = part
                column = code_ref[t, group, row]
                contracted = group * width + jnp.maximum(column, 0)
                base = strip_base(sizes, rows, slots, shares, contracted)
                for s in range(slots):
                    index, valid = matched(code_ref, here, contracted, column >= 0, targets[s])
                    block = jnp.where(valid, unpack(column_ref[base + index], size), 0.0)
                    for w_ref, part in zip(w_refs, parts_of(block)):
                        w_ref[j * LANES:j * LANES + size, s * LANES:(s + 1) * LANES] = part

        high, low, least = [
            jnp.dot(a_ref[:(3 - n) * size], w_refs[n][...], preferred_element_type=jnp.float32) for n in range(3)
        ]
        small = low[size:] + (least + high[2 * size:])
        result = high[:size] + ((low[:size] + high[size:2 * size]) + small)
        for s in range(slots):
            out_ref[i, 0, s] = result[:, s * LANES:s * LANES + size]


def exchanged(value, axis, mask):
    return lax.ppermute(value, axis, [(n, n ^ mask) for n in range(lax.axis_size(axis))])


def row_strip(packed, sizes):
    n_row, n_col, n_layer = sizes
    if n_col != 4:
        strip = {0: packed}
        bit = n_col // 2
        while bit:
            for mask in list(strip):
                strip[mask | bit] = exchanged(strip[mask], "col", bit)
            bit //= 2
        return [(strip[m], m, m, 1) for m in sorted(strip)], []
    per_group = n_row * n_layer // n_col
    route = []
    for r in range(n_row):
        for c in range(n_col):
            for y in range(n_layer):
                value = 2 if (r * n_layer + y) // per_group < n_col // 2 else 3
                route.append(((r * n_col + c) * n_layer + y, (r * n_col + (c ^ value)) * n_layer + y))
    far = lax.ppermute(packed, AXES, route)
    return [(packed, 0, 0, 1), (None, 1, 1, 1), (far, 2, 3, 2)], [(exchanged(far, "col", 1), 3, 2, 0)]


def body(blocks, block_cols, occupancy):
    rows, _, slots, size, _ = blocks.shape
    sizes = tuple(lax.axis_size(axis) for axis in AXES)
    n_row, n_col, n_layer = sizes
    chips = n_layer // 2
    tall = tall_of(size)
    code = jnp.where(occupancy == 1, block_cols, -1).transpose((2, 1, 0))

    packed = pl.pallas_call(
        pack_kernel,
        out_shape=jax.ShapeDtypeStruct((rows * slots, tall, LANES), jnp.float32),
        in_specs=[VMEM],
        out_specs=VMEM,
        compiler_params=LIMIT,
        name="pack",
    )(blocks)

    early, late = row_strip(packed, sizes)
    def in_plane(steps):
        route = []
        for a in range(n_row):
            for c in range(n_col):
                for b in range(n_layer):
                    row_bits, chip_bits = steps[c >= n_col // 2]
                    target = ((a ^ row_bits) * n_col + c) * n_layer + (b ^ (2 * chip_bits))
                    route.append(((a * n_col + c) * n_layer + b, target))
        return lax.ppermute(packed, AXES, route)

    if four_by_four(sizes):
        mine = [packed, in_plane([(0, 1)] * 2), in_plane([(1, 0), (1, 1)]), in_plane([(1, 1), (1, 0)])]
        needed = 3
    else:
        mine = [packed] + [in_plane([(n // chips, n % chips)] * 2) for n in range(1, n_row * chips)]
        needed = len(mine)
    early = [(exchanged(packed, "col", 1) if share is None else share, *rest) for share, *rest in early]
    both = pl.pallas_call(
        pair_kernel,
        out_shape=jax.ShapeDtypeStruct((2,) + packed.shape, jnp.float32),
        in_specs=[VMEM, VMEM],
        out_specs=VMEM,
        compiler_params=LIMIT,
        name="pair",
    )(*mine[:2])
    others = [exchanged(both, "layer", 1)] + [exchanged(share, "layer", 1) for share in mine[2:needed]]

    def column(count):
        return jax.ShapeDtypeStruct((2 * count * rows * slots, tall, LANES), jnp.float32)

    far = [share for share, value, _, _ in early if value > 1]
    marks = [
        pl.pallas_call(
            mark_kernel,
            out_shape=jax.ShapeDtypeStruct((8, LANES), jnp.float32),
            in_specs=[UNREAD],
            out_specs=VMEM,
            cost_estimate=pl.CostEstimate(flops=int(5e+09), bytes_accessed=0, transcendentals=0),
            compiler_params=LIMIT,
            name="mark",
        )(share)
        for share in far
    ]
    trace = pl.pallas_call(
        functools.partial(trace_kernel, sizes, rows, size, [tuple(rest) for _, *rest in early], needed),
        out_shape=jax.ShapeDtypeStruct((n_row * n_col * chips, 1, LANES), jnp.float32),
        in_specs=[SMEM] + [VMEM] * (len(early) + 2 * needed - 1) + [UNREAD] * len(marks),
        out_specs=VMEM,
        scratch_shapes=[pltpu.VMEM(column(needed).shape, jnp.float32)],
        compiler_params=LIMIT,
        name="trace_terms",
    )(code, *[share for share, *_ in early], *mine[:needed], *others[:needed - 1], *marks)
    for share in mine[needed:]:
        held = pl.pallas_call(
            copy_kernel,
            out_shape=jax.ShapeDtypeStruct(share.shape, jnp.float32),
            in_specs=[VMEM, UNREAD],
            out_specs=VMEM,
            compiler_params=LIMIT,
            name="copy",
        )(share, trace)
        others.append(exchanged(held, "layer", 1))
    trace = trace + exchanged(trace, "layer", 1)
    like = [list(range(core, n_row * n_col * n_layer, 2)) for core in range(2)]
    trace = lax.all_to_all(trace, AXES, 0, 0, axis_index_groups=like, tiled=True)

    strip = early + late
    inner = len(strip) * slots * LANES
    near = [share for share, value, _, _ in early if value == 1]
    operands = mine[::-1] + near + far + [share for share, *_ in late] + others

    def at(share):
        return next(n for n, operand in enumerate(operands) if operand is share)

    strip_at, share_at = [at(share) for share, *_ in strip], [at(share) for share in mine + others]
    product, end = pl.pallas_call(
        functools.partial(product_kernel, sizes, [tuple(rest) for _, *rest in strip], strip_at, share_at),
        out_shape=(
            jax.ShapeDtypeStruct(blocks.shape, jnp.float32),
            jax.ShapeDtypeStruct((8, LANES), jnp.float32),
        ),
        in_specs=[SMEM] + [VMEM] * len(operands),
        out_specs=(VMEM, VMEM),
        scratch_shapes=[
            pltpu.VMEM(column(len(mine)).shape, jnp.float32),
            pltpu.VMEM((3 * size, inner), jnp.bfloat16),
        ]
        + [pltpu.VMEM((inner, slots * LANES), jnp.bfloat16)] * 3,
        compiler_params=LIMIT,
        name="multiply",
    )(code, *operands)
    trace = pl.pallas_call(
        sum_kernel,
        out_shape=jax.ShapeDtypeStruct((1, 1), jnp.float32),
        in_specs=[VMEM, UNREAD],
        out_specs=VMEM,
        compiler_params=LIMIT,
        name="sum",
    )(trace, end)
    return product, trace.reshape(())


def solution(mesh):
    in_specs = (P(("row", "layer"), "col", None, None, None), P(), P())
    out_specs = (P(("row", "layer"), "col", None, None, None), P())
    return jax.shard_map(body, mesh=mesh, in_specs=in_specs, out_specs=out_specs, check_vma=False)
```

```python
import functools

import jax
import jax.numpy as jnp
from jax import lax
from jax.experimental import pallas as pl
from jax.experimental.pallas import tpu as pltpu
from jax.sharding import PartitionSpec as P

LANES = 128
AXES = ("row", "col", "layer")
LIMIT = pltpu.CompilerParams(vmem_limit_bytes=48 * 2 ** 20)
VMEM = pl.BlockSpec(memory_space=pltpu.VMEM)
UNREAD = pl.BlockSpec(memory_space=pl.ANY)
SMEM = pl.BlockSpec(memory_space=pltpu.SMEM)


def tall_of(size):
    return size * size // LANES


def unpack(block, size):
    tall = block.shape[0]
    spare = LANES - size
    rest = size - tall
    pieces = [block[q * rest:(q + 1) * rest, size:] for q in range(size // spare)]
    pieces.append(jnp.zeros((rest, spare), block.dtype))
    return jnp.concatenate([block, jnp.concatenate(pieces, axis=1)], axis=0)


def parts_of(value):
    parts = []
    for _ in range(3):
        part = value.astype(jnp.bfloat16)
        parts.append(part)
        value = value - part.astype(jnp.float32)
    return parts


def place(sizes):
    n_row, n_col, n_layer = sizes
    per_group = n_row * n_layer // n_col
    pair = lax.axis_index("row") * n_layer + lax.axis_index("layer")
    return pair, lax.axis_index("col"), lax.div(pair, per_group), lax.rem(pair, per_group), per_group


def pack_kernel(x_ref, out_ref):
    rows, _, slots, size, _ = x_ref.shape
    tall = tall_of(size)
    spare = LANES - size
    rest = size - tall
    for i in range(rows):
        for t in range(slots):
            n = i * slots + t
            out_ref[n, :, :size] = x_ref[i, 0, t, :tall, :]
            for q in range(size // spare):
                out_ref[n, q * rest:(q + 1) * rest, size:] = x_ref[i, 0, t, tall:, q * spare:(q + 1) * spare]


def four_by_four(sizes):
    return sizes[0] == 2 and sizes[1] == 4 and sizes[2] == 4


def strip_base(sizes, rows, slots, shares, contracted):
    n_row, n_col, n_layer = sizes
    chips = n_layer // 2
    my_row, my_layer = lax.axis_index("row"), lax.axis_index("layer")
    source = lax.div(contracted, rows)
    source_row, source_layer = lax.div(source, n_layer), lax.rem(source, n_layer)
    share = lax.bitwise_xor(source_row, my_row) * chips + lax.bitwise_xor(lax.div(source_layer, 2), lax.div(my_layer, 2))
    if four_by_four(sizes):
        share = jnp.where((share >= 2) & (lax.axis_index("col") >= 2), 5 - share, share)
    other_core = lax.bitwise_xor(lax.rem(source_layer, 2), lax.rem(my_layer, 2))
    return ((share + other_core * shares) * rows + lax.rem(contracted, rows)) * slots


def stack(share_refs, out_ref):
    first = 0
    for ref in share_refs:
        for part in [ref] if len(ref.shape) == 3 else [ref.at[n] for n in range(ref.shape[0])]:
            out_ref[first:first + part.shape[0]] = part[...]
            first += part.shape[0]


def group_at(sizes, here, own_group, values):
    return lax.bitwise_xor(here, jnp.where(own_group >= sizes[1] // 2, values[1], values[0]))


def matched(code_ref, here, contracted, stored, target):
    index, valid = jnp.int32(0), jnp.bool_(False)
    for u in range(code_ref.shape[0]):
        hit = code_ref[u, here, contracted] == target
        index = jnp.where(hit, u, index)
        valid = valid | hit
    return index, valid & stored & (target >= 0)


def copy_kernel(x_ref, _, out_ref):
    out_ref[...] = x_ref[...]


def pair_kernel(x_ref, y_ref, out_ref):
    out_ref[0] = x_ref[...]
    out_ref[1] = y_ref[...]


def mark_kernel(_, out_ref):
    out_ref[...] = jnp.zeros(out_ref.shape, jnp.float32)


def trace_kernel(sizes, rows, size, groups, shares, code_ref, *refs):
    strip_refs, share_refs = refs[:len(groups)], refs[len(groups):len(groups) + 2 * shares - 1]
    total_ref, column_ref = refs[-2:]
    slots = code_ref.shape[0]
    pair, here, own_group, number, per_group = place(sizes)
    width = per_group * rows
    def straight(block):
        return unpack(block, size)[:, :size]

    @pl.when(own_group == here)
    def _():
        stack(share_refs, column_ref)
        total = jnp.zeros((size, size), jnp.float32)
        for i in range(rows):
            row = pair * rows + i
            for strip_ref, (value, value_upper, weight) in zip(strip_refs, groups):
                group = group_at(sizes, here, own_group, (value, value_upper))
                for t in range(slots):
                    column = code_ref[t, group, row]
                    contracted = group * width + jnp.maximum(column, 0)
                    index, valid = matched(code_ref, here, contracted, column >= 0, number * rows + i)
                    block = column_ref[strip_base(sizes, rows, slots, shares, contracted) + index]
                    term = straight(strip_ref[i * slots + t]) * straight(block).T
                    total = total + jnp.where(valid, weight * term, 0.0)
        total_ref[...] = jnp.full(total_ref.shape, jnp.sum(total), jnp.float32)

    @pl.when(own_group != here)
    def _():
        total_ref[...] = jnp.zeros(total_ref.shape, jnp.float32)


def sum_kernel(terms_ref, _, out_ref):
    out_ref[...] = jnp.sum(terms_ref[...], axis=0)[:, :1]


def product_kernel(sizes, groups, strip_at, share_at, code_ref, *refs):
    count = len(groups)
    strip_refs, share_refs = [refs[n] for n in strip_at], [refs[n] for n in share_at]
    shares = (len(share_at) + 1) // 2
    out_ref, end_ref, column_ref, a_ref, *w_refs = refs[-7:]
    end_ref[...] = jnp.zeros(end_ref.shape, jnp.float32)
    rows, _, slots, size, _ = out_ref.shape
    pair, here, own_group, _, per_group = place(sizes)
    width = per_group * rows
    stack(share_refs, column_ref)

    for w_ref in w_refs:
        for j in range(count * slots):
            w_ref[j * LANES + size:(j + 1) * LANES, :] = jnp.zeros((LANES - size, slots * LANES), jnp.bfloat16)
    for i in range(rows):
        row = pair * rows + i
        targets = [code_ref[s, here, row] for s in range(slots)]
        for k, (value, value_upper, _) in enumerate(groups):
            group = group_at(sizes, here, own_group, (value, value_upper))
            for t in range(slots):
                j = k * slots + t
                for n, part in enumerate(parts_of(unpack(strip_refs[k][i * slots + t], size))):
                    a_ref[n * size:(n + 1) * size, j * LANES:(j + 1) * LANES] = part
                column = code_ref[t, group, row]
                contracted = group * width + jnp.maximum(column, 0)
                base = strip_base(sizes, rows, slots, shares, contracted)
                for s in range(slots):
                    index, valid = matched(code_ref, here, contracted, column >= 0, targets[s])
                    block = jnp.where(valid, unpack(column_ref[base + index], size), 0.0)
                    for w_ref, part in zip(w_refs, parts_of(block)):
                        w_ref[j * LANES:j * LANES + size, s * LANES:(s + 1) * LANES] = part

        high, low, least = [
            jnp.dot(a_ref[:(3 - n) * size], w_refs[n][...], preferred_element_type=jnp.float32) for n in range(3)
        ]
        small = low[size:] + (least + high[2 * size:])
        result = high[:size] + ((low[:size] + high[size:2 * size]) + small)
        for s in range(slots):
            out_ref[i, 0, s] = result[:, s * LANES:s * LANES + size]


def exchanged(value, axis, mask):
    return lax.ppermute(value, axis, [(n, n ^ mask) for n in range(lax.axis_size(axis))])


def row_strip(packed, sizes):
    n_row, n_col, n_layer = sizes
    if n_col != 4:
        strip = {0: packed}
        bit = n_col // 2
        while bit:
            for mask in list(strip):
                strip[mask | bit] = exchanged(strip[mask], "col", bit)
            bit //= 2
        return [(strip[m], m, m, 1) for m in sorted(strip)], []
    per_group = n_row * n_layer // n_col
    route = []
    for r in range(n_row):
        for c in range(n_col):
            for y in range(n_layer):
                value = 2 if (r * n_layer + y) // per_group < n_col // 2 else 3
                route.append(((r * n_col + c) * n_layer + y, (r * n_col + (c ^ value)) * n_layer + y))
    far = lax.ppermute(packed, AXES, route)
    return [(packed, 0, 0, 1), (None, 1, 1, 1), (far, 2, 3, 2)], [(exchanged(far, "col", 1), 3, 2, 0)]


def body(blocks, block_cols, occupancy):
    rows, _, slots, size, _ = blocks.shape
    sizes = tuple(lax.axis_size(axis) for axis in AXES)
    n_row, n_col, n_layer = sizes
    chips = n_layer // 2
    tall = tall_of(size)
    code = jnp.where(occupancy == 1, block_cols, -1).transpose((2, 1, 0))

    packed = pl.pallas_call(
        pack_kernel,
        out_shape=jax.ShapeDtypeStruct((rows * slots, tall, LANES), jnp.float32),
        in_specs=[VMEM],
        out_specs=VMEM,
        compiler_params=LIMIT,
        name="pack",
    )(blocks)

    early, late = row_strip(packed, sizes)
    def copied(share, after):
        return pl.pallas_call(
            copy_kernel,
            out_shape=jax.ShapeDtypeStruct(share.shape, jnp.float32),
            in_specs=[VMEM, UNREAD],
            out_specs=VMEM,
            compiler_params=LIMIT,
            name="copy",
        )(share, after)

    def in_plane(steps, value=packed):
        route = []
        for a in range(n_row):
            for c in range(n_col):
                for b in range(n_layer):
                    row_bits, chip_bits = steps[c >= n_col // 2]
                    target = ((a ^ row_bits) * n_col + c) * n_layer + (b ^ (2 * chip_bits))
                    route.append(((a * n_col + c) * n_layer + b, target))
        return lax.ppermute(value, AXES, route)

    if four_by_four(sizes):
        mine = [packed, in_plane([(0, 1)] * 2), in_plane([(1, 0), (1, 1)])]
        mine.append(in_plane([(1, 1), (1, 0)], copied(packed, mine[1])))
        needed = 3
    else:
        mine = [packed] + [in_plane([(n // chips, n % chips)] * 2) for n in range(1, n_row * chips)]
        needed = len(mine)
    early = [(exchanged(packed, "col", 1) if share is None else share, *rest) for share, *rest in early]
    both = pl.pallas_call(
        pair_kernel,
        out_shape=jax.ShapeDtypeStruct((2,) + packed.shape, jnp.float32),
        in_specs=[VMEM, VMEM],
        out_specs=VMEM,
        compiler_params=LIMIT,
        name="pair",
    )(*mine[:2])
    others = [exchanged(both, "layer", 1)] + [exchanged(share, "layer", 1) for share in mine[2:needed]]

    def column(count):
        return jax.ShapeDtypeStruct((2 * count * rows * slots, tall, LANES), jnp.float32)

    far = [share for share, value, _, _ in early if value > 1]
    marks = [
        pl.pallas_call(
            mark_kernel,
            out_shape=jax.ShapeDtypeStruct((8, LANES), jnp.float32),
            in_specs=[UNREAD],
            out_specs=VMEM,
            cost_estimate=pl.CostEstimate(flops=int(5e+09), bytes_accessed=0, transcendentals=0),
            compiler_params=LIMIT,
            name="mark",
        )(share)
        for share in far
    ]
    trace = pl.pallas_call(
        functools.partial(trace_kernel, sizes, rows, size, [tuple(rest) for _, *rest in early], needed),
        out_shape=jax.ShapeDtypeStruct((n_row * n_col * n_layer, 1, LANES), jnp.float32),
        in_specs=[SMEM] + [VMEM] * (len(early) + 2 * needed - 1) + [UNREAD] * len(marks),
        out_specs=VMEM,
        scratch_shapes=[pltpu.VMEM(column(needed).shape, jnp.float32)],
        compiler_params=LIMIT,
        name="trace_terms",
    )(code, *[share for share, *_ in early], *mine[:needed], *others[:needed - 1], *marks)
    for share in mine[needed:]:
        others.append(exchanged(copied(share, trace), "layer", 1))
    trace = lax.all_to_all(trace, AXES, 0, 0, tiled=True)

    strip = early + late
    inner = len(strip) * slots * LANES
    near = [share for share, value, _, _ in early if value == 1]
    operands = mine[::-1] + near + far + [share for share, *_ in late] + others

    def at(share):
        return next(n for n, operand in enumerate(operands) if operand is share)

    strip_at, share_at = [at(share) for share, *_ in strip], [at(share) for share in mine + others]
    product, end = pl.pallas_call(
        functools.partial(product_kernel, sizes, [tuple(rest) for _, *rest in strip], strip_at, share_at),
        out_shape=(
            jax.ShapeDtypeStruct(blocks.shape, jnp.float32),
            jax.ShapeDtypeStruct((8, LANES), jnp.float32),
        ),
        in_specs=[SMEM] + [VMEM] * len(operands),
        out_specs=(VMEM, VMEM),
        scratch_shapes=[
            pltpu.VMEM(column(len(mine)).shape, jnp.float32),
            pltpu.VMEM((3 * size, inner), jnp.bfloat16),
        ]
        + [pltpu.VMEM((inner, slots * LANES), jnp.bfloat16)] * 3,
        compiler_params=LIMIT,
        name="multiply",
    )(code, *operands)
    trace = pl.pallas_call(
        sum_kernel,
        out_shape=jax.ShapeDtypeStruct((1, 1), jnp.float32),
        in_specs=[VMEM, UNREAD],
        out_specs=VMEM,
        compiler_params=LIMIT,
        name="sum",
    )(trace, end)
    return product, trace.reshape(())


def solution(mesh):
    in_specs = (P(("row", "layer"), "col", None, None, None), P(), P())
    out_specs = (P(("row", "layer"), "col", None, None, None), P())
    return jax.shard_map(body, mesh=mesh, in_specs=in_specs, out_specs=out_specs, check_vma=False)
```

```python
import functools

import jax
import jax.numpy as jnp
from jax import lax
from jax.experimental import pallas as pl
from jax.experimental.pallas import tpu as pltpu
from jax.sharding import PartitionSpec as P

LANES = 128
AXES = ("row", "col", "layer")
LIMIT = pltpu.CompilerParams(vmem_limit_bytes=48 * 2 ** 20)
VMEM = pl.BlockSpec(memory_space=pltpu.VMEM)
UNREAD = pl.BlockSpec(memory_space=pl.ANY)
SMEM = pl.BlockSpec(memory_space=pltpu.SMEM)


def tall_of(size):
    return size * size // LANES


def unpack(block, size):
    tall = block.shape[0]
    spare = LANES - size
    rest = size - tall
    pieces = [block[q * rest:(q + 1) * rest, size:] for q in range(size // spare)]
    pieces.append(jnp.zeros((rest, spare), block.dtype))
    return jnp.concatenate([block, jnp.concatenate(pieces, axis=1)], axis=0)


def parts_of(value):
    parts = []
    for _ in range(3):
        part = value.astype(jnp.bfloat16)
        parts.append(part)
        value = value - part.astype(jnp.float32)
    return parts


def place(sizes):
    n_row, n_col, n_layer = sizes
    per_group = n_row * n_layer // n_col
    pair = lax.axis_index("row") * n_layer + lax.axis_index("layer")
    return pair, lax.axis_index("col"), lax.div(pair, per_group), lax.rem(pair, per_group), per_group


def pack_kernel(x_ref, out_ref):
    rows, _, slots, size, _ = x_ref.shape
    tall = tall_of(size)
    spare = LANES - size
    rest = size - tall
    for i in range(rows):
        for t in range(slots):
            n = i * slots + t
            out_ref[n, :, :size] = x_ref[i, 0, t, :tall, :]
            for q in range(size // spare):
                out_ref[n, q * rest:(q + 1) * rest, size:] = x_ref[i, 0, t, tall:, q * spare:(q + 1) * spare]


def four_by_four(sizes):
    return sizes[0] == 2 and sizes[1] == 4 and sizes[2] == 4


def strip_base(sizes, rows, slots, shares, contracted):
    n_row, n_col, n_layer = sizes
    chips = n_layer // 2
    my_row, my_layer = lax.axis_index("row"), lax.axis_index("layer")
    source = lax.div(contracted, rows)
    source_row, source_layer = lax.div(source, n_layer), lax.rem(source, n_layer)
    share = lax.bitwise_xor(source_row, my_row) * chips + lax.bitwise_xor(lax.div(source_layer, 2), lax.div(my_layer, 2))
    if four_by_four(sizes):
        share = jnp.where((share >= 2) & (lax.axis_index("col") >= 2), 5 - share, share)
    other_core = lax.bitwise_xor(lax.rem(source_layer, 2), lax.rem(my_layer, 2))
    return ((share + other_core * shares) * rows + lax.rem(contracted, rows)) * slots


def stack(share_refs, out_ref):
    first = 0
    for ref in share_refs:
        for part in [ref] if len(ref.shape) == 3 else [ref.at[n] for n in range(ref.shape[0])]:
            out_ref[first:first + part.shape[0]] = part[...]
            first += part.shape[0]


def group_at(sizes, here, own_group, values):
    return lax.bitwise_xor(here, jnp.where(own_group >= sizes[1] // 2, values[1], values[0]))


def matched(code_ref, here, contracted, stored, target):
    index, valid = jnp.int32(0), jnp.bool_(False)
    for u in range(code_ref.shape[0]):
        hit = code_ref[u, here, contracted] == target
        index = jnp.where(hit, u, index)
        valid = valid | hit
    return index, valid & stored & (target >= 0)


def pair_kernel(x_ref, y_ref, out_ref):
    out_ref[0] = x_ref[...]
    out_ref[1] = y_ref[...]


def mark_kernel(_, out_ref):
    out_ref[...] = jnp.zeros(out_ref.shape, jnp.float32)


def trace_kernel(sizes, rows, size, groups, shares, code_ref, *refs):
    strip_refs, share_refs = refs[:len(groups)], refs[len(groups):len(groups) + 2 * shares - 1]
    total_ref, column_ref = refs[-2:]
    slots = code_ref.shape[0]
    pair, here, own_group, number, per_group = place(sizes)
    width = per_group * rows
    def straight(block):
        return unpack(block, size)[:, :size]

    @pl.when(own_group == here)
    def _():
        stack(share_refs, column_ref)
        total = jnp.zeros((size, size), jnp.float32)
        for i in range(rows):
            row = pair * rows + i
            for strip_ref, (value, value_upper, weight) in zip(strip_refs, groups):
                group = group_at(sizes, here, own_group, (value, value_upper))
                for t in range(slots):
                    column = code_ref[t, group, row]
                    contracted = group * width + jnp.maximum(column, 0)
                    index, valid = matched(code_ref, here, contracted, column >= 0, number * rows + i)
                    block = column_ref[strip_base(sizes, rows, slots, shares, contracted) + index]
                    term = straight(strip_ref[i * slots + t]) * straight(block).T
                    total = total + jnp.where(valid, weight * term, 0.0)
        total_ref[...] = jnp.full(total_ref.shape, jnp.sum(total), jnp.float32)

    @pl.when(own_group != here)
    def _():
        total_ref[...] = jnp.zeros(total_ref.shape, jnp.float32)


def sum_kernel(terms_ref, _, out_ref):
    out_ref[...] = jnp.sum(terms_ref[...], axis=0)[:, :1]


def product_kernel(sizes, groups, strip_at, share_at, code_ref, *refs):
    count = len(groups)
    strip_refs, share_refs = [refs[n] for n in strip_at], [refs[n] for n in share_at]
    shares = (len(share_at) + 1) // 2
    out_ref, end_ref, column_ref, a_ref, *w_refs = refs[-7:]
    end_ref[...] = jnp.zeros(end_ref.shape, jnp.float32)
    rows, _, slots, size, _ = out_ref.shape
    pair, here, own_group, _, per_group = place(sizes)
    width = per_group * rows
    stack(share_refs, column_ref)

    for w_ref in w_refs:
        for j in range(count * slots):
            w_ref[j * LANES + size:(j + 1) * LANES, :] = jnp.zeros((LANES - size, slots * LANES), jnp.bfloat16)
    for i in range(rows):
        row = pair * rows + i
        targets = [code_ref[s, here, row] for s in range(slots)]
        for k, (value, value_upper, _) in enumerate(groups):
            group = group_at(sizes, here, own_group, (value, value_upper))
            for t in range(slots):
                j = k * slots + t
                for n, part in enumerate(parts_of(unpack(strip_refs[k][i * slots + t], size))):
                    a_ref[n * size:(n + 1) * size, j * LANES:(j + 1) * LANES] = part
                column = code_ref[t, group, row]
                contracted = group * width + jnp.maximum(column, 0)
                base = strip_base(sizes, rows, slots, shares, contracted)
                for s in range(slots):
                    index, valid = matched(code_ref, here, contracted, column >= 0, targets[s])
                    block = jnp.where(valid, unpack(column_ref[base + index], size), 0.0)
                    for w_ref, part in zip(w_refs, parts_of(block)):
                        w_ref[j * LANES:j * LANES + size, s * LANES:(s + 1) * LANES] = part

        high, low, least = [
            jnp.dot(a_ref[:(3 - n) * size], w_refs[n][...], preferred_element_type=jnp.float32) for n in range(3)
        ]
        small = low[size:] + (least + high[2 * size:])
        result = high[:size] + ((low[:size] + high[size:2 * size]) + small)
        for s in range(slots):
            out_ref[i, 0, s] = result[:, s * LANES:s * LANES + size]


def exchanged(value, axis, mask):
    return lax.ppermute(value, axis, [(n, n ^ mask) for n in range(lax.axis_size(axis))])


def row_strip(packed, sizes):
    n_row, n_col, n_layer = sizes
    if n_col != 4:
        strip = {0: packed}
        bit = n_col // 2
        while bit:
            for mask in list(strip):
                strip[mask | bit] = exchanged(strip[mask], "col", bit)
            bit //= 2
        return [(strip[m], m, m, 1) for m in sorted(strip)], []
    per_group = n_row * n_layer // n_col
    route = []
    for r in range(n_row):
        for c in range(n_col):
            for y in range(n_layer):
                value = 2 if (r * n_layer + y) // per_group < n_col // 2 else 3
                route.append(((r * n_col + c) * n_layer + y, (r * n_col + (c ^ value)) * n_layer + y))
    far = lax.ppermute(packed, AXES, route)
    return [(packed, 0, 0, 1), (None, 1, 1, 1), (far, 2, 3, 2)], [(exchanged(far, "col", 1), 3, 2, 0)]


def body(blocks, block_cols, occupancy):
    rows, _, slots, size, _ = blocks.shape
    sizes = tuple(lax.axis_size(axis) for axis in AXES)
    n_row, n_col, n_layer = sizes
    chips = n_layer // 2
    tall = tall_of(size)
    code = jnp.where(occupancy == 1, block_cols, -1).transpose((2, 1, 0))

    packed = pl.pallas_call(
        pack_kernel,
        out_shape=jax.ShapeDtypeStruct((rows * slots, tall, LANES), jnp.float32),
        in_specs=[VMEM],
        out_specs=VMEM,
        compiler_params=LIMIT,
        name="pack",
    )(blocks)

    early, late = row_strip(packed, sizes)
    def in_plane(steps):
        route = []
        for a in range(n_row):
            for c in range(n_col):
                for b in range(n_layer):
                    row_bits, chip_bits = steps[c >= n_col // 2]
                    target = ((a ^ row_bits) * n_col + c) * n_layer + (b ^ (2 * chip_bits))
                    route.append(((a * n_col + c) * n_layer + b, target))
        return lax.ppermute(packed, AXES, route)

    if four_by_four(sizes):
        mine = [packed, in_plane([(0, 1)] * 2), in_plane([(1, 0), (1, 1)]), in_plane([(1, 1), (1, 0)])]
        needed = 3
    else:
        mine = [packed] + [in_plane([(n // chips, n % chips)] * 2) for n in range(1, n_row * chips)]
        needed = len(mine)
    early = [(exchanged(packed, "col", 1) if share is None else share, *rest) for share, *rest in early]
    both = pl.pallas_call(
        pair_kernel,
        out_shape=jax.ShapeDtypeStruct((2,) + packed.shape, jnp.float32),
        in_specs=[VMEM, VMEM],
        out_specs=VMEM,
        compiler_params=LIMIT,
        name="pair",
    )(*mine[:2])
    others = [exchanged(both, "layer", 1)] + [exchanged(share, "layer", 1) for share in mine[2:]]

    def column(count):
        return jax.ShapeDtypeStruct((2 * count * rows * slots, tall, LANES), jnp.float32)

    far = [share for share, value, _, _ in early if value > 1]
    marks = [
        pl.pallas_call(
            mark_kernel,
            out_shape=jax.ShapeDtypeStruct((8, LANES), jnp.float32),
            in_specs=[UNREAD],
            out_specs=VMEM,
            cost_estimate=pl.CostEstimate(flops=int(5e+09), bytes_accessed=0, transcendentals=0),
            compiler_params=LIMIT,
            name="mark",
        )(share)
        for share in far
    ]
    trace = pl.pallas_call(
        functools.partial(trace_kernel, sizes, rows, size, [tuple(rest) for _, *rest in early], needed),
        out_shape=jax.ShapeDtypeStruct((n_row * n_col * n_layer, 1, LANES), jnp.float32),
        in_specs=[SMEM] + [VMEM] * (len(early) + 2 * needed - 1) + [UNREAD] * len(marks),
        out_specs=VMEM,
        scratch_shapes=[pltpu.VMEM(column(needed).shape, jnp.float32)],
        compiler_params=LIMIT,
        name="trace_terms",
    )(code, *[share for share, *_ in early], *mine[:needed], *others[:needed - 1], *marks)
    trace = lax.all_to_all(trace, AXES, 0, 0, tiled=True)

    strip = early + late
    inner = len(strip) * slots * LANES
    near = [share for share, value, _, _ in early if value == 1]
    operands = far + near + mine + [share for share, *_ in late] + others

    def at(share):
        return next(n for n, operand in enumerate(operands) if operand is share)

    strip_at, share_at = [at(share) for share, *_ in strip], [at(share) for share in mine + others]
    product, end = pl.pallas_call(
        functools.partial(product_kernel, sizes, [tuple(rest) for _, *rest in strip], strip_at, share_at),
        out_shape=(
            jax.ShapeDtypeStruct(blocks.shape, jnp.float32),
            jax.ShapeDtypeStruct((8, LANES), jnp.float32),
        ),
        in_specs=[SMEM] + [VMEM] * len(operands),
        out_specs=(VMEM, VMEM),
        scratch_shapes=[
            pltpu.VMEM(column(len(mine)).shape, jnp.float32),
            pltpu.VMEM((3 * size, inner), jnp.bfloat16),
        ]
        + [pltpu.VMEM((inner, slots * LANES), jnp.bfloat16)] * 3,
        compiler_params=LIMIT,
        name="multiply",
    )(code, *operands)
    trace = pl.pallas_call(
        sum_kernel,
        out_shape=jax.ShapeDtypeStruct((1, 1), jnp.float32),
        in_specs=[VMEM, UNREAD],
        out_specs=VMEM,
        compiler_params=LIMIT,
        name="sum",
    )(trace, end)
    return product, trace.reshape(())


def solution(mesh):
    in_specs = (P(("row", "layer"), "col", None, None, None), P(), P())
    out_specs = (P(("row", "layer"), "col", None, None, None), P())
    return jax.shard_map(body, mesh=mesh, in_specs=in_specs, out_specs=out_specs, check_vma=False)
```

```python
import functools

import jax
import jax.numpy as jnp
from jax import lax
from jax.experimental import pallas as pl
from jax.experimental.pallas import tpu as pltpu
from jax.sharding import PartitionSpec as P

LANES = 128
AXES = ("row", "col", "layer")
LIMIT = pltpu.CompilerParams(vmem_limit_bytes=48 * 2 ** 20)
VMEM = pl.BlockSpec(memory_space=pltpu.VMEM)
UNREAD = pl.BlockSpec(memory_space=pl.ANY)
SMEM = pl.BlockSpec(memory_space=pltpu.SMEM)


def tall_of(size):
    return size * size // LANES


def unpack(block, size):
    tall = block.shape[0]
    spare = LANES - size
    rest = size - tall
    pieces = [block[q * rest:(q + 1) * rest, size:] for q in range(size // spare)]
    pieces.append(jnp.zeros((rest, spare), block.dtype))
    return jnp.concatenate([block, jnp.concatenate(pieces, axis=1)], axis=0)


def parts_of(value):
    parts = []
    for _ in range(3):
        part = value.astype(jnp.bfloat16)
        parts.append(part)
        value = value - part.astype(jnp.float32)
    return parts


def place(sizes):
    n_row, n_col, n_layer = sizes
    per_group = n_row * n_layer // n_col
    pair = lax.axis_index("row") * n_layer + lax.axis_index("layer")
    return pair, lax.axis_index("col"), lax.div(pair, per_group), lax.rem(pair, per_group), per_group


def pack_kernel(x_ref, out_ref):
    rows, _, slots, size, _ = x_ref.shape
    tall = tall_of(size)
    spare = LANES - size
    rest = size - tall
    for i in range(rows):
        for t in range(slots):
            n = i * slots + t
            out_ref[n, :, :size] = x_ref[i, 0, t, :tall, :]
            for q in range(size // spare):
                out_ref[n, q * rest:(q + 1) * rest, size:] = x_ref[i, 0, t, tall:, q * spare:(q + 1) * spare]


def four_by_four(sizes):
    return sizes[0] == 2 and sizes[1] == 4 and sizes[2] == 4


def strip_base(sizes, rows, slots, shares, contracted):
    n_row, n_col, n_layer = sizes
    chips = n_layer // 2
    my_row, my_layer = lax.axis_index("row"), lax.axis_index("layer")
    source = lax.div(contracted, rows)
    source_row, source_layer = lax.div(source, n_layer), lax.rem(source, n_layer)
    share = lax.bitwise_xor(source_row, my_row) * chips + lax.bitwise_xor(lax.div(source_layer, 2), lax.div(my_layer, 2))
    if four_by_four(sizes):
        share = jnp.where((share >= 2) & (lax.axis_index("col") >= 2), 5 - share, share)
    other_core = lax.bitwise_xor(lax.rem(source_layer, 2), lax.rem(my_layer, 2))
    return ((share + other_core * shares) * rows + lax.rem(contracted, rows)) * slots


def stack(share_refs, out_ref):
    first = 0
    for ref in share_refs:
        for part in [ref] if len(ref.shape) == 3 else [ref.at[n] for n in range(ref.shape[0])]:
            out_ref[first:first + part.shape[0]] = part[...]
            first += part.shape[0]


def group_at(sizes, here, own_group, values):
    return lax.bitwise_xor(here, jnp.where(own_group >= sizes[1] // 2, values[1], values[0]))


def matched(code_ref, here, contracted, stored, target):
    index, valid = jnp.int32(0), jnp.bool_(False)
    for u in range(code_ref.shape[0]):
        hit = code_ref[u, here, contracted] == target
        index = jnp.where(hit, u, index)
        valid = valid | hit
    return index, valid & stored & (target >= 0)


def copy_kernel(x_ref, _, out_ref):
    out_ref[...] = x_ref[...]


def pair_kernel(x_ref, y_ref, out_ref):
    out_ref[0] = x_ref[...]
    out_ref[1] = y_ref[...]


def mark_kernel(_, out_ref):
    out_ref[...] = jnp.zeros(out_ref.shape, jnp.float32)


def trace_kernel(sizes, rows, size, groups, shares, code_ref, *refs):
    strip_refs, share_refs = refs[:len(groups)], refs[len(groups):len(groups) + 2 * shares - 1]
    total_ref, column_ref, sum_ref = refs[-3:]
    slots = code_ref.shape[0]
    pair, here, own_group, number, per_group = place(sizes)
    width = per_group * rows
    def straight(block):
        return unpack(block, size)[:, :size]

    @pl.when(own_group == here)
    def _():
        stack(share_refs, column_ref)
        sum_ref[...] = jnp.zeros(sum_ref.shape, jnp.float32)
        for i in range(rows):
            row = pair * rows + i
            for strip_ref, (value, value_upper, weight) in zip(strip_refs, groups):
                group = group_at(sizes, here, own_group, (value, value_upper))
                for t in range(slots):
                    column = code_ref[t, group, row]
                    contracted = group * width + jnp.maximum(column, 0)
                    index, valid = matched(code_ref, here, contracted, column >= 0, number * rows + i)
                    left = strip_ref.at[i * slots + t]
                    right = column_ref.at[strip_base(sizes, rows, slots, shares, contracted) + index]

                    @pl.when(valid)
                    def _(left=left, right=right, weight=weight):
                        sum_ref[...] += weight * (straight(left[...]) * straight(right[...]).T)

        total_ref[...] = jnp.full(total_ref.shape, jnp.sum(sum_ref[...]), jnp.float32)

    @pl.when(own_group != here)
    def _():
        total_ref[...] = jnp.zeros(total_ref.shape, jnp.float32)


def sum_kernel(terms_ref, _, out_ref):
    out_ref[...] = jnp.sum(terms_ref[...], axis=0)[:, :1]


def product_kernel(sizes, groups, strip_at, share_at, code_ref, *refs):
    count = len(groups)
    strip_refs, share_refs = [refs[n] for n in strip_at], [refs[n] for n in share_at]
    shares = (len(share_at) + 1) // 2
    out_ref, end_ref, column_ref, a_ref, *w_refs = refs[-7:]
    end_ref[...] = jnp.zeros(end_ref.shape, jnp.float32)
    rows, _, slots, size, _ = out_ref.shape
    pair, here, own_group, _, per_group = place(sizes)
    width = per_group * rows
    stack(share_refs, column_ref)

    for w_ref in w_refs:
        for j in range(count * slots):
            w_ref[j * LANES + size:(j + 1) * LANES, :] = jnp.zeros((LANES - size, slots * LANES), jnp.bfloat16)
    for i in range(rows):
        row = pair * rows + i
        targets = [code_ref[s, here, row] for s in range(slots)]
        for k, (value, value_upper, _) in enumerate(groups):
            group = group_at(sizes, here, own_group, (value, value_upper))
            for t in range(slots):
                j = k * slots + t
                for n, part in enumerate(parts_of(unpack(strip_refs[k][i * slots + t], size))):
                    a_ref[n * size:(n + 1) * size, j * LANES:(j + 1) * LANES] = part
                column = code_ref[t, group, row]
                contracted = group * width + jnp.maximum(column, 0)
                base = strip_base(sizes, rows, slots, shares, contracted)
                for s in range(slots):
                    index, valid = matched(code_ref, here, contracted, column >= 0, targets[s])
                    block = jnp.where(valid, unpack(column_ref[base + index], size), 0.0)
                    for w_ref, part in zip(w_refs, parts_of(block)):
                        w_ref[j * LANES:j * LANES + size, s * LANES:(s + 1) * LANES] = part

        high, low, least = [
            jnp.dot(a_ref[:(3 - n) * size], w_refs[n][...], preferred_element_type=jnp.float32) for n in range(3)
        ]
        small = low[size:] + (least + high[2 * size:])
        result = high[:size] + ((low[:size] + high[size:2 * size]) + small)
        for s in range(slots):
            out_ref[i, 0, s] = result[:, s * LANES:s * LANES + size]


def exchanged(value, axis, mask):
    return lax.ppermute(value, axis, [(n, n ^ mask) for n in range(lax.axis_size(axis))])


def row_strip(packed, sizes):
    n_row, n_col, n_layer = sizes
    if n_col != 4:
        strip = {0: packed}
        bit = n_col // 2
        while bit:
            for mask in list(strip):
                strip[mask | bit] = exchanged(strip[mask], "col", bit)
            bit //= 2
        return [(strip[m], m, m, 1) for m in sorted(strip)], []
    per_group = n_row * n_layer // n_col
    route = []
    for r in range(n_row):
        for c in range(n_col):
            for y in range(n_layer):
                value = 2 if (r * n_layer + y) // per_group < n_col // 2 else 3
                route.append(((r * n_col + c) * n_layer + y, (r * n_col + (c ^ value)) * n_layer + y))
    far = lax.ppermute(packed, AXES, route)
    return [(packed, 0, 0, 1), (None, 1, 1, 1), (far, 2, 3, 2)], [(exchanged(far, "col", 1), 3, 2, 0)]


def body(blocks, block_cols, occupancy):
    rows, _, slots, size, _ = blocks.shape
    sizes = tuple(lax.axis_size(axis) for axis in AXES)
    n_row, n_col, n_layer = sizes
    chips = n_layer // 2
    tall = tall_of(size)
    code = jnp.where(occupancy == 1, block_cols, -1).transpose((2, 1, 0))

    packed = pl.pallas_call(
        pack_kernel,
        out_shape=jax.ShapeDtypeStruct((rows * slots, tall, LANES), jnp.float32),
        in_specs=[VMEM],
        out_specs=VMEM,
        compiler_params=LIMIT,
        name="pack",
    )(blocks)

    early, late = row_strip(packed, sizes)
    def copied(share, after):
        return pl.pallas_call(
            copy_kernel,
            out_shape=jax.ShapeDtypeStruct(share.shape, jnp.float32),
            in_specs=[VMEM, UNREAD],
            out_specs=VMEM,
            compiler_params=LIMIT,
            name="copy",
        )(share, after)

    def in_plane(steps):
        route = []
        for a in range(n_row):
            for c in range(n_col):
                for b in range(n_layer):
                    row_bits, chip_bits = steps[c >= n_col // 2]
                    target = ((a ^ row_bits) * n_col + c) * n_layer + (b ^ (2 * chip_bits))
                    route.append(((a * n_col + c) * n_layer + b, target))
        return lax.ppermute(packed, AXES, route)

    if four_by_four(sizes):
        mine = [packed, in_plane([(0, 1)] * 2), in_plane([(1, 0), (1, 1)]), in_plane([(1, 1), (1, 0)])]
        needed = 3
    else:
        mine = [packed] + [in_plane([(n // chips, n % chips)] * 2) for n in range(1, n_row * chips)]
        needed = len(mine)
    early = [(exchanged(packed, "col", 1) if share is None else share, *rest) for share, *rest in early]
    both = pl.pallas_call(
        pair_kernel,
        out_shape=jax.ShapeDtypeStruct((2,) + packed.shape, jnp.float32),
        in_specs=[VMEM, VMEM],
        out_specs=VMEM,
        compiler_params=LIMIT,
        name="pair",
    )(*mine[:2])
    others = [exchanged(both, "layer", 1)] + [exchanged(share, "layer", 1) for share in mine[2:needed]]

    def column(count):
        return jax.ShapeDtypeStruct((2 * count * rows * slots, tall, LANES), jnp.float32)

    far = [share for share, value, _, _ in early if value > 1]
    marks = [
        pl.pallas_call(
            mark_kernel,
            out_shape=jax.ShapeDtypeStruct((8, LANES), jnp.float32),
            in_specs=[UNREAD],
            out_specs=VMEM,
            cost_estimate=pl.CostEstimate(flops=int(5e+09), bytes_accessed=0, transcendentals=0),
            compiler_params=LIMIT,
            name="mark",
        )(share)
        for share in far
    ]
    trace = pl.pallas_call(
        functools.partial(trace_kernel, sizes, rows, size, [tuple(rest) for _, *rest in early], needed),
        out_shape=jax.ShapeDtypeStruct((n_row * n_col * n_layer, 1, LANES), jnp.float32),
        in_specs=[SMEM] + [VMEM] * (len(early) + 2 * needed - 1) + [UNREAD] * len(marks),
        out_specs=VMEM,
        scratch_shapes=[pltpu.VMEM(column(needed).shape, jnp.float32), pltpu.VMEM((size, size), jnp.float32)],
        compiler_params=LIMIT,
        name="trace_terms",
    )(code, *[share for share, *_ in early], *mine[:needed], *others[:needed - 1], *marks)
    for share in mine[needed:]:
        others.append(exchanged(copied(share, trace), "layer", 1))
    trace = lax.all_to_all(trace, AXES, 0, 0, tiled=True)

    strip = early + late
    inner = len(strip) * slots * LANES
    near = [share for share, value, _, _ in early if value == 1]
    operands = mine[::-1] + near + far + [share for share, *_ in late] + others

    def at(share):
        return next(n for n, operand in enumerate(operands) if operand is share)

    strip_at, share_at = [at(share) for share, *_ in strip], [at(share) for share in mine + others]
    product, end = pl.pallas_call(
        functools.partial(product_kernel, sizes, [tuple(rest) for _, *rest in strip], strip_at, share_at),
        out_shape=(
            jax.ShapeDtypeStruct(blocks.shape, jnp.float32),
            jax.ShapeDtypeStruct((8, LANES), jnp.float32),
        ),
        in_specs=[SMEM] + [VMEM] * len(operands),
        out_specs=(VMEM, VMEM),
        scratch_shapes=[
            pltpu.VMEM(column(len(mine)).shape, jnp.float32),
            pltpu.VMEM((3 * size, inner), jnp.bfloat16),
        ]
        + [pltpu.VMEM((inner, slots * LANES), jnp.bfloat16)] * 3,
        compiler_params=LIMIT,
        name="multiply",
    )(code, *operands)
    trace = pl.pallas_call(
        sum_kernel,
        out_shape=jax.ShapeDtypeStruct((1, 1), jnp.float32),
        in_specs=[VMEM, UNREAD],
        out_specs=VMEM,
        compiler_params=LIMIT,
        name="sum",
    )(trace, end)
    return product, trace.reshape(())


def solution(mesh):
    in_specs = (P(("row", "layer"), "col", None, None, None), P(), P())
    out_specs = (P(("row", "layer"), "col", None, None, None), P())
    return jax.shard_map(body, mesh=mesh, in_specs=in_specs, out_specs=out_specs, check_vma=False)
```

```python
import functools

import jax
import jax.numpy as jnp
from jax import lax
from jax.experimental import pallas as pl
from jax.experimental.pallas import tpu as pltpu
from jax.sharding import PartitionSpec as P

LANES = 128
AXES = ("row", "col", "layer")
LIMIT = pltpu.CompilerParams(vmem_limit_bytes=48 * 2 ** 20)
VMEM = pl.BlockSpec(memory_space=pltpu.VMEM)
UNREAD = pl.BlockSpec(memory_space=pl.ANY)
SMEM = pl.BlockSpec(memory_space=pltpu.SMEM)


def tall_of(size):
    return size * size // LANES


def unpack(block, size):
    tall = block.shape[0]
    spare = LANES - size
    rest = size - tall
    pieces = [block[q * rest:(q + 1) * rest, size:] for q in range(size // spare)]
    pieces.append(jnp.zeros((rest, spare), block.dtype))
    return jnp.concatenate([block, jnp.concatenate(pieces, axis=1)], axis=0)


def parts_of(value):
    parts = []
    for _ in range(3):
        part = value.astype(jnp.bfloat16)
        parts.append(part)
        value = value - part.astype(jnp.float32)
    return parts


def place(sizes):
    n_row, n_col, n_layer = sizes
    per_group = n_row * n_layer // n_col
    pair = lax.axis_index("row") * n_layer + lax.axis_index("layer")
    return pair, lax.axis_index("col"), lax.div(pair, per_group), lax.rem(pair, per_group), per_group


def pack_kernel(x_ref, out_ref):
    rows, _, slots, size, _ = x_ref.shape
    tall = tall_of(size)
    spare = LANES - size
    rest = size - tall
    for i in range(rows):
        for t in range(slots):
            n = i * slots + t
            out_ref[n, :, :size] = x_ref[i, 0, t, :tall, :]
            for q in range(size // spare):
                out_ref[n, q * rest:(q + 1) * rest, size:] = x_ref[i, 0, t, tall:, q * spare:(q + 1) * spare]


def four_by_four(sizes):
    return sizes[0] == 2 and sizes[1] == 4 and sizes[2] == 4


def strip_base(sizes, rows, slots, shares, contracted):
    n_row, n_col, n_layer = sizes
    chips = n_layer // 2
    my_row, my_layer = lax.axis_index("row"), lax.axis_index("layer")
    source = lax.div(contracted, rows)
    source_row, source_layer = lax.div(source, n_layer), lax.rem(source, n_layer)
    share = lax.bitwise_xor(source_row, my_row) * chips + lax.bitwise_xor(lax.div(source_layer, 2), lax.div(my_layer, 2))
    if four_by_four(sizes):
        share = jnp.where((share >= 2) & (lax.axis_index("col") >= 2), 5 - share, share)
    other_core = lax.bitwise_xor(lax.rem(source_layer, 2), lax.rem(my_layer, 2))
    return ((share + other_core * shares) * rows + lax.rem(contracted, rows)) * slots


def stack(share_refs, out_ref):
    first = 0
    for ref in share_refs:
        for part in [ref] if len(ref.shape) == 3 else [ref.at[n] for n in range(ref.shape[0])]:
            out_ref[first:first + part.shape[0]] = part[...]
            first += part.shape[0]


def group_at(sizes, here, own_group, values):
    return lax.bitwise_xor(here, jnp.where(own_group >= sizes[1] // 2, values[1], values[0]))


def matched(code_ref, here, contracted, stored, target):
    index, valid = jnp.int32(0), jnp.bool_(False)
    for u in range(code_ref.shape[0]):
        hit = code_ref[u, here, contracted] == target
        index = jnp.where(hit, u, index)
        valid = valid | hit
    return index, valid & stored & (target >= 0)


def copy_kernel(x_ref, _, out_ref):
    out_ref[...] = x_ref[...]


def pair_kernel(x_ref, y_ref, out_ref):
    out_ref[0] = x_ref[...]
    out_ref[1] = y_ref[...]


def mark_kernel(_, out_ref):
    out_ref[...] = jnp.zeros(out_ref.shape, jnp.float32)


def trace_kernel(sizes, rows, size, groups, shares, code_ref, *refs):
    strip_refs, share_refs = refs[:len(groups)], refs[len(groups):len(groups) + 2 * shares - 1]
    total_ref, column_ref = refs[-2:]
    slots = code_ref.shape[0]
    pair, here, own_group, number, per_group = place(sizes)
    width = per_group * rows
    def straight(block):
        return unpack(block, size)[:, :size]

    @pl.when(own_group == here)
    def _():
        stack(share_refs, column_ref)
        total = jnp.zeros((size, size), jnp.float32)
        for i in range(rows):
            row = pair * rows + i
            for strip_ref, (value, value_upper, weight) in zip(strip_refs, groups):
                group = group_at(sizes, here, own_group, (value, value_upper))
                for t in range(slots):
                    column = code_ref[t, group, row]
                    contracted = group * width + jnp.maximum(column, 0)
                    index, valid = matched(code_ref, here, contracted, column >= 0, number * rows + i)
                    block = column_ref[strip_base(sizes, rows, slots, shares, contracted) + index]
                    factor = jnp.where(valid, jnp.float32(weight), jnp.float32(0))
                    total = total + factor * (straight(strip_ref[i * slots + t]) * straight(block).T)
        total_ref[...] = jnp.full(total_ref.shape, jnp.sum(total), jnp.float32)

    @pl.when(own_group != here)
    def _():
        total_ref[...] = jnp.zeros(total_ref.shape, jnp.float32)


def sum_kernel(terms_ref, _, out_ref):
    out_ref[...] = jnp.sum(terms_ref[...], axis=0)[:, :1]


def product_kernel(sizes, groups, strip_at, share_at, code_ref, *refs):
    count = len(groups)
    strip_refs, share_refs = [refs[n] for n in strip_at], [refs[n] for n in share_at]
    shares = (len(share_at) + 1) // 2
    out_ref, end_ref, column_ref, a_ref, *w_refs = refs[-7:]
    end_ref[...] = jnp.zeros(end_ref.shape, jnp.float32)
    rows, _, slots, size, _ = out_ref.shape
    pair, here, own_group, _, per_group = place(sizes)
    width = per_group * rows
    stack(share_refs, column_ref)

    for w_ref in w_refs:
        for j in range(count * slots):
            w_ref[j * LANES + size:(j + 1) * LANES, :] = jnp.zeros((LANES - size, slots * LANES), jnp.bfloat16)
    for i in range(rows):
        row = pair * rows + i
        targets = [code_ref[s, here, row] for s in range(slots)]
        for k, (value, value_upper, _) in enumerate(groups):
            group = group_at(sizes, here, own_group, (value, value_upper))
            for t in range(slots):
                j = k * slots + t
                for n, part in enumerate(parts_of(unpack(strip_refs[k][i * slots + t], size))):
                    a_ref[n * size:(n + 1) * size, j * LANES:(j + 1) * LANES] = part
                column = code_ref[t, group, row]
                contracted = group * width + jnp.maximum(column, 0)
                base = strip_base(sizes, rows, slots, shares, contracted)
                for s in range(slots):
                    index, valid = matched(code_ref, here, contracted, column >= 0, targets[s])
                    block = jnp.where(valid, unpack(column_ref[base + index], size), 0.0)
                    for w_ref, part in zip(w_refs, parts_of(block)):
                        w_ref[j * LANES:j * LANES + size, s * LANES:(s + 1) * LANES] = part

        high, low, least = [
            jnp.dot(a_ref[:(3 - n) * size], w_refs[n][...], preferred_element_type=jnp.float32) for n in range(3)
        ]
        small = low[size:] + (least + high[2 * size:])
        result = high[:size] + ((low[:size] + high[size:2 * size]) + small)
        for s in range(slots):
            out_ref[i, 0, s] = result[:, s * LANES:s * LANES + size]


def exchanged(value, axis, mask):
    return lax.ppermute(value, axis, [(n, n ^ mask) for n in range(lax.axis_size(axis))])


def row_strip(packed, sizes):
    n_row, n_col, n_layer = sizes
    if n_col != 4:
        strip = {0: packed}
        bit = n_col // 2
        while bit:
            for mask in list(strip):
                strip[mask | bit] = exchanged(strip[mask], "col", bit)
            bit //= 2
        return [(strip[m], m, m, 1) for m in sorted(strip)], []
    per_group = n_row * n_layer // n_col
    route = []
    for r in range(n_row):
        for c in range(n_col):
            for y in range(n_layer):
                value = 2 if (r * n_layer + y) // per_group < n_col // 2 else 3
                route.append(((r * n_col + c) * n_layer + y, (r * n_col + (c ^ value)) * n_layer + y))
    far = lax.ppermute(packed, AXES, route)
    return [(packed, 0, 0, 1), (None, 1, 1, 1), (far, 2, 3, 2)], [(exchanged(far, "col", 1), 3, 2, 0)]


def body(blocks, block_cols, occupancy):
    rows, _, slots, size, _ = blocks.shape
    sizes = tuple(lax.axis_size(axis) for axis in AXES)
    n_row, n_col, n_layer = sizes
    chips = n_layer // 2
    tall = tall_of(size)
    code = jnp.where(occupancy == 1, block_cols, -1).transpose((2, 1, 0))

    packed = pl.pallas_call(
        pack_kernel,
        out_shape=jax.ShapeDtypeStruct((rows * slots, tall, LANES), jnp.float32),
        in_specs=[VMEM],
        out_specs=VMEM,
        compiler_params=LIMIT,
        name="pack",
    )(blocks)

    early, late = row_strip(packed, sizes)
    def copied(share, after):
        return pl.pallas_call(
            copy_kernel,
            out_shape=jax.ShapeDtypeStruct(share.shape, jnp.float32),
            in_specs=[VMEM, UNREAD],
            out_specs=VMEM,
            compiler_params=LIMIT,
            name="copy",
        )(share, after)

    def in_plane(steps):
        route = []
        for a in range(n_row):
            for c in range(n_col):
                for b in range(n_layer):
                    row_bits, chip_bits = steps[c >= n_col // 2]
                    target = ((a ^ row_bits) * n_col + c) * n_layer + (b ^ (2 * chip_bits))
                    route.append(((a * n_col + c) * n_layer + b, target))
        return lax.ppermute(packed, AXES, route)

    if four_by_four(sizes):
        mine = [packed, in_plane([(0, 1)] * 2), in_plane([(1, 0), (1, 1)]), in_plane([(1, 1), (1, 0)])]
        needed = 3
    else:
        mine = [packed] + [in_plane([(n // chips, n % chips)] * 2) for n in range(1, n_row * chips)]
        needed = len(mine)
    early = [(exchanged(packed, "col", 1) if share is None else share, *rest) for share, *rest in early]
    both = pl.pallas_call(
        pair_kernel,
        out_shape=jax.ShapeDtypeStruct((2,) + packed.shape, jnp.float32),
        in_specs=[VMEM, VMEM],
        out_specs=VMEM,
        compiler_params=LIMIT,
        name="pair",
    )(*mine[:2])
    others = [exchanged(both, "layer", 1)] + [exchanged(share, "layer", 1) for share in mine[2:needed]]

    def column(count):
        return jax.ShapeDtypeStruct((2 * count * rows * slots, tall, LANES), jnp.float32)

    far = [share for share, value, _, _ in early if value > 1]
    marks = [
        pl.pallas_call(
            mark_kernel,
            out_shape=jax.ShapeDtypeStruct((8, LANES), jnp.float32),
            in_specs=[UNREAD],
            out_specs=VMEM,
            cost_estimate=pl.CostEstimate(flops=int(5e+09), bytes_accessed=0, transcendentals=0),
            compiler_params=LIMIT,
            name="mark",
        )(share)
        for share in far
    ]
    trace = pl.pallas_call(
        functools.partial(trace_kernel, sizes, rows, size, [tuple(rest) for _, *rest in early], needed),
        out_shape=jax.ShapeDtypeStruct((n_row * n_col * n_layer, 1, LANES), jnp.float32),
        in_specs=[SMEM] + [VMEM] * (len(early) + 2 * needed - 1) + [UNREAD] * len(marks),
        out_specs=VMEM,
        scratch_shapes=[pltpu.VMEM(column(needed).shape, jnp.float32)],
        compiler_params=LIMIT,
        name="trace_terms",
    )(code, *[share for share, *_ in early], *mine[:needed], *others[:needed - 1], *marks)
    for share in mine[needed:]:
        others.append(exchanged(copied(share, trace), "layer", 1))
    trace = lax.all_to_all(trace, AXES, 0, 0, tiled=True)

    strip = early + late
    inner = len(strip) * slots * LANES
    near = [share for share, value, _, _ in early if value == 1]
    operands = mine[::-1] + near + far + [share for share, *_ in late] + others

    def at(share):
        return next(n for n, operand in enumerate(operands) if operand is share)

    strip_at, share_at = [at(share) for share, *_ in strip], [at(share) for share in mine + others]
    product, end = pl.pallas_call(
        functools.partial(product_kernel, sizes, [tuple(rest) for _, *rest in strip], strip_at, share_at),
        out_shape=(
            jax.ShapeDtypeStruct(blocks.shape, jnp.float32),
            jax.ShapeDtypeStruct((8, LANES), jnp.float32),
        ),
        in_specs=[SMEM] + [VMEM] * len(operands),
        out_specs=(VMEM, VMEM),
        scratch_shapes=[
            pltpu.VMEM(column(len(mine)).shape, jnp.float32),
            pltpu.VMEM((3 * size, inner), jnp.bfloat16),
        ]
        + [pltpu.VMEM((inner, slots * LANES), jnp.bfloat16)] * 3,
        compiler_params=LIMIT,
        name="multiply",
    )(code, *operands)
    trace = pl.pallas_call(
        sum_kernel,
        out_shape=jax.ShapeDtypeStruct((1, 1), jnp.float32),
        in_specs=[VMEM, UNREAD],
        out_specs=VMEM,
        compiler_params=LIMIT,
        name="sum",
    )(trace, end)
    return product, trace.reshape(())


def solution(mesh):
    in_specs = (P(("row", "layer"), "col", None, None, None), P(), P())
    out_specs = (P(("row", "layer"), "col", None, None, None), P())
    return jax.shard_map(body, mesh=mesh, in_specs=in_specs, out_specs=out_specs, check_vma=False)
```

```python
import functools

import jax
import jax.numpy as jnp
from jax import lax
from jax.experimental import pallas as pl
from jax.experimental.pallas import tpu as pltpu
from jax.sharding import PartitionSpec as P

LANES = 128
AXES = ("row", "col", "layer")
LIMIT = pltpu.CompilerParams(vmem_limit_bytes=48 * 2 ** 20)
VMEM = pl.BlockSpec(memory_space=pltpu.VMEM)
UNREAD = pl.BlockSpec(memory_space=pl.ANY)
SMEM = pl.BlockSpec(memory_space=pltpu.SMEM)


def tall_of(size):
    return size * size // LANES


def unpack(block, size):
    tall = block.shape[0]
    spare = LANES - size
    rest = size - tall
    pieces = [block[q * rest:(q + 1) * rest, size:] for q in range(size // spare)]
    pieces.append(jnp.zeros((rest, spare), block.dtype))
    return jnp.concatenate([block, jnp.concatenate(pieces, axis=1)], axis=0)


def parts_of(value):
    parts = []
    for _ in range(3):
        part = value.astype(jnp.bfloat16)
        parts.append(part)
        value = value - part.astype(jnp.float32)
    return parts


def place(sizes):
    n_row, n_col, n_layer = sizes
    per_group = n_row * n_layer // n_col
    pair = lax.axis_index("row") * n_layer + lax.axis_index("layer")
    return pair, lax.axis_index("col"), lax.div(pair, per_group), lax.rem(pair, per_group), per_group


def pack_kernel(x_ref, out_ref):
    rows, _, slots, size, _ = x_ref.shape
    tall = tall_of(size)
    spare = LANES - size
    rest = size - tall
    for i in range(rows):
        for t in range(slots):
            n = i * slots + t
            out_ref[n, :, :size] = x_ref[i, 0, t, :tall, :]
            for q in range(size // spare):
                out_ref[n, q * rest:(q + 1) * rest, size:] = x_ref[i, 0, t, tall:, q * spare:(q + 1) * spare]


def four_by_four(sizes):
    return sizes[0] == 2 and sizes[1] == 4 and sizes[2] == 4


def strip_base(sizes, rows, slots, shares, contracted):
    n_row, n_col, n_layer = sizes
    chips = n_layer // 2
    my_row, my_layer = lax.axis_index("row"), lax.axis_index("layer")
    source = lax.div(contracted, rows)
    source_row, source_layer = lax.div(source, n_layer), lax.rem(source, n_layer)
    share = lax.bitwise_xor(source_row, my_row) * chips + lax.bitwise_xor(lax.div(source_layer, 2), lax.div(my_layer, 2))
    if four_by_four(sizes):
        share = jnp.where((share >= 2) & (lax.axis_index("col") >= 2), 5 - share, share)
    other_core = lax.bitwise_xor(lax.rem(source_layer, 2), lax.rem(my_layer, 2))
    return ((share + other_core * shares) * rows + lax.rem(contracted, rows)) * slots


def stack(share_refs, out_ref):
    for n, ref in enumerate(share_refs):
        out_ref[n * ref.shape[0]:(n + 1) * ref.shape[0]] = ref[...]


def group_at(sizes, here, own_group, values):
    return lax.bitwise_xor(here, jnp.where(own_group >= sizes[1] // 2, values[1], values[0]))


def matched(code_ref, here, contracted, stored, target):
    index, valid = jnp.int32(0), jnp.bool_(False)
    for u in range(code_ref.shape[0]):
        hit = code_ref[u, here, contracted] == target
        index = jnp.where(hit, u, index)
        valid = valid | hit
    return index, valid & stored & (target >= 0)


def mark_kernel(_, out_ref):
    out_ref[...] = jnp.zeros(out_ref.shape, jnp.float32)


def trace_kernel(sizes, rows, size, groups, shares, code_ref, *refs):
    strip_refs, share_refs = refs[:len(groups)], refs[len(groups):len(groups) + 2 * shares]
    total_ref, column_ref = refs[-2:]
    slots = code_ref.shape[0]
    pair, here, own_group, number, per_group = place(sizes)
    width = per_group * rows
    def straight(block):
        return unpack(block, size)[:, :size]

    @pl.when(own_group == here)
    def _():
        stack(share_refs, column_ref)
        total = jnp.zeros((size, size), jnp.float32)
        for i in range(rows):
            row = pair * rows + i
            for strip_ref, (value, value_upper, weight) in zip(strip_refs, groups):
                group = group_at(sizes, here, own_group, (value, value_upper))
                for t in range(slots):
                    column = code_ref[t, group, row]
                    contracted = group * width + jnp.maximum(column, 0)
                    index, valid = matched(code_ref, here, contracted, column >= 0, number * rows + i)
                    block = column_ref[strip_base(sizes, rows, slots, shares, contracted) + index]
                    factor = jnp.where(valid, jnp.float32(weight), jnp.float32(0))
                    total = total + factor * (straight(strip_ref[i * slots + t]) * straight(block).T)
        total_ref[...] = jnp.full(total_ref.shape, jnp.sum(total), jnp.float32)

    @pl.when(own_group != here)
    def _():
        total_ref[...] = jnp.zeros(total_ref.shape, jnp.float32)


def sum_kernel(terms_ref, out_ref):
    out_ref[...] = jnp.sum(terms_ref[...], axis=0)[:, :1]


def product_kernel(sizes, groups, strip_at, share_at, code_ref, *refs):
    count = len(groups)
    strip_refs, share_refs = [refs[n] for n in strip_at], [refs[n] for n in share_at]
    shares = len(share_at) // 2
    out_ref, column_ref, a_ref, *w_refs = refs[-6:]
    rows, _, slots, size, _ = out_ref.shape
    pair, here, own_group, _, per_group = place(sizes)
    width = per_group * rows
    stack(share_refs, column_ref)

    for w_ref in w_refs:
        for j in range(count * slots):
            w_ref[j * LANES + size:(j + 1) * LANES, :] = jnp.zeros((LANES - size, slots * LANES), jnp.bfloat16)
    for i in range(rows):
        row = pair * rows + i
        targets = [code_ref[s, here, row] for s in range(slots)]
        for k, (value, value_upper, _) in enumerate(groups):
            group = group_at(sizes, here, own_group, (value, value_upper))
            for t in range(slots):
                j = k * slots + t
                for n, part in enumerate(parts_of(unpack(strip_refs[k][i * slots + t], size))):
                    a_ref[n * size:(n + 1) * size, j * LANES:(j + 1) * LANES] = part
                column = code_ref[t, group, row]
                contracted = group * width + jnp.maximum(column, 0)
                base = strip_base(sizes, rows, slots, shares, contracted)
                for s in range(slots):
                    index, valid = matched(code_ref, here, contracted, column >= 0, targets[s])
                    block = jnp.where(valid, unpack(column_ref[base + index], size), 0.0)
                    for w_ref, part in zip(w_refs, parts_of(block)):
                        w_ref[j * LANES:j * LANES + size, s * LANES:(s + 1) * LANES] = part

        high, low, least = [
            jnp.dot(a_ref[:(3 - n) * size], w_refs[n][...], preferred_element_type=jnp.float32) for n in range(3)
        ]
        small = low[size:] + (least + high[2 * size:])
        result = high[:size] + ((low[:size] + high[size:2 * size]) + small)
        for s in range(slots):
            out_ref[i, 0, s] = result[:, s * LANES:s * LANES + size]


def exchanged(value, axis, mask):
    return lax.ppermute(value, axis, [(n, n ^ mask) for n in range(lax.axis_size(axis))])


def row_strip(packed, sizes):
    n_row, n_col, n_layer = sizes
    if n_col != 4:
        strip = {0: packed}
        bit = n_col // 2
        while bit:
            for mask in list(strip):
                strip[mask | bit] = exchanged(strip[mask], "col", bit)
            bit //= 2
        return [(strip[m], m, m, 1) for m in sorted(strip)], []
    per_group = n_row * n_layer // n_col
    route = []
    for r in range(n_row):
        for c in range(n_col):
            for y in range(n_layer):
                value = 2 if (r * n_layer + y) // per_group < n_col // 2 else 3
                route.append(((r * n_col + c) * n_layer + y, (r * n_col + (c ^ value)) * n_layer + y))
    far = lax.ppermute(packed, AXES, route)
    return [(packed, 0, 0, 1), (None, 1, 1, 1), (far, 2, 3, 2)], [(exchanged(far, "col", 1), 3, 2, 0)]


def body(blocks, block_cols, occupancy):
    rows, _, slots, size, _ = blocks.shape
    sizes = tuple(lax.axis_size(axis) for axis in AXES)
    n_row, n_col, n_layer = sizes
    chips = n_layer // 2
    tall = tall_of(size)
    code = jnp.where(occupancy == 1, block_cols, -1).transpose((2, 1, 0))

    packed = pl.pallas_call(
        pack_kernel,
        out_shape=jax.ShapeDtypeStruct((rows * slots, tall, LANES), jnp.float32),
        in_specs=[VMEM],
        out_specs=VMEM,
        compiler_params=LIMIT,
        name="pack",
    )(blocks)

    early, late = row_strip(packed, sizes)
    def in_plane(steps):
        route = []
        for a in range(n_row):
            for c in range(n_col):
                for b in range(n_layer):
                    row_bits, chip_bits = steps[c >= n_col // 2]
                    target = ((a ^ row_bits) * n_col + c) * n_layer + (b ^ (2 * chip_bits))
                    route.append(((a * n_col + c) * n_layer + b, target))
        return lax.ppermute(packed, AXES, route)

    if four_by_four(sizes):
        mine = [packed, in_plane([(0, 1)] * 2), in_plane([(1, 0), (1, 1)]), in_plane([(1, 1), (1, 0)])]
        needed = 3
    else:
        mine = [packed] + [in_plane([(n // chips, n % chips)] * 2) for n in range(1, n_row * chips)]
        needed = len(mine)
    early = [(exchanged(packed, "col", 1) if share is None else share, *rest) for share, *rest in early]
    others = [exchanged(share, "layer", 1) for share in mine]

    def column(count):
        return jax.ShapeDtypeStruct((2 * count * rows * slots, tall, LANES), jnp.float32)

    far = [share for share, value, _, _ in early if value > 1]
    marks = [
        pl.pallas_call(
            mark_kernel,
            out_shape=jax.ShapeDtypeStruct((8, LANES), jnp.float32),
            in_specs=[UNREAD],
            out_specs=VMEM,
            cost_estimate=pl.CostEstimate(flops=int(5e+09), bytes_accessed=0, transcendentals=0),
            compiler_params=LIMIT,
            name="mark",
        )(share)
        for share in far
    ]
    trace = pl.pallas_call(
        functools.partial(trace_kernel, sizes, rows, size, [tuple(rest) for _, *rest in early], needed),
        out_shape=jax.ShapeDtypeStruct((n_row * n_col * n_layer, 1, LANES), jnp.float32),
        in_specs=[SMEM] + [VMEM] * (len(early) + 2 * needed) + [UNREAD] * len(marks),
        out_specs=VMEM,
        scratch_shapes=[pltpu.VMEM(column(needed).shape, jnp.float32)],
        compiler_params=LIMIT,
        name="trace_terms",
    )(code, *[share for share, *_ in early], *mine[:needed], *others[:needed], *marks)
    trace = lax.all_to_all(trace, AXES, 0, 0, tiled=True)

    strip = early + late
    inner = len(strip) * slots * LANES
    near = [share for share, value, _, _ in early if value == 1]
    operands = far + mine + near + [share for share, *_ in late] + others

    def at(share):
        return next(n for n, operand in enumerate(operands) if operand is share)

    strip_at, share_at = [at(share) for share, *_ in strip], [at(share) for share in mine + others]
    product = pl.pallas_call(
        functools.partial(product_kernel, sizes, [tuple(rest) for _, *rest in strip], strip_at, share_at),
        out_shape=jax.ShapeDtypeStruct(blocks.shape, jnp.float32),
        in_specs=[SMEM] + [VMEM] * len(operands),
        out_specs=VMEM,
        scratch_shapes=[
            pltpu.VMEM(column(len(mine)).shape, jnp.float32),
            pltpu.VMEM((3 * size, inner), jnp.bfloat16),
        ]
        + [pltpu.VMEM((inner, slots * LANES), jnp.bfloat16)] * 3,
        compiler_params=LIMIT,
        name="multiply",
    )(code, *operands)
    trace = pl.pallas_call(
        sum_kernel,
        out_shape=jax.ShapeDtypeStruct((1, 1), jnp.float32),
        in_specs=[VMEM],
        out_specs=VMEM,
        compiler_params=LIMIT,
        name="sum",
    )(trace)
    return product, trace.reshape(())


def solution(mesh):
    in_specs = (P(("row", "layer"), "col", None, None, None), P(), P())
    out_specs = (P(("row", "layer"), "col", None, None, None), P())
    return jax.shard_map(body, mesh=mesh, in_specs=in_specs, out_specs=out_specs, check_vma=False)
```
